32 devices in a mesh: dp: 2 (over x), blk: 16 (over z, y, core).
Axes of the slice: x: 2, y: 2, z: 4, core: 2. Of those that a mesh axis runs over, the one named last changes fastest.
Arguments:
- tokens: bfloat16 [16384, 768], P(('dp', 'blk')), may hold values from -6 to 6
- w_qkv: bfloat16 [768, 2304], replicated, may hold values from -0.21875 to 0.21875
- b_query: bfloat16 [768], replicated, may hold values from -1.796875 to 1.796875
- b_value: bfloat16 [768], replicated, may hold values from -1.796875 to 1.796875
- w_out: bfloat16 [768, 768], replicated, may hold values from -2.5 to 2.5
- b_out: bfloat16 [768], replicated, may hold values from -1.796875 to 1.796875
- gain_one: bfloat16 [768], replicated, may hold values from 0.5 to 1.5
- shift_one: bfloat16 [768], replicated, may hold values from -1.796875 to 1.796875
- w_up: bfloat16 [768, 3072], replicated, may hold values from -0.21875 to 0.21875
- b_up: bfloat16 [3072], replicated, may hold values from -1.796875 to 1.796875
- w_down: bfloat16 [3072, 768], replicated, may hold values from -0.109375 to 0.109375
- b_down: bfloat16 [768], replicated, may hold values from -1.796875 to 1.796875
- gain_two: bfloat16 [768], replicated, may hold values from 0.5 to 1.5
- shift_two: bfloat16 [768], replicated, may hold values from -1.796875 to 1.796875
- cluster_perm: int32 [2, 12, 8192], P('dp', None, 'blk'), may hold values from 0 to 8191, as said below
- cluster_pairs: int32 [2, 12, 64, 2], P('dp'), may hold values from 0 to 63, as said below
- cotangent: bfloat16 [16384, 768], P(('dp', 'blk')), may hold values from -6 to 6
Outputs:
- layer_out: bfloat16 [16384, 768], P(('dp', 'blk'))
- grad_tokens: bfloat16 [16384, 768], P(('dp', 'blk'))
- grad_w_qkv: float32 [768, 2304], replicated
- grad_b_query: float32 [768], replicated
- grad_b_value: float32 [768], replicated
- grad_w_out: float32 [768, 768], replicated
- grad_b_out: float32 [768], replicated
- grad_gain_one: float32 [768], replicated
- grad_shift_one: float32 [768], replicated
- grad_w_up: float32 [768, 3072], replicated
- grad_b_up: float32 [3072], replicated
- grad_w_down: float32 [3072, 768], replicated
- grad_b_down: float32 [768], replicated
- grad_gain_two: float32 [768], replicated
- grad_shift_two: float32 [768], replicated
The draws below stay inside these ranges and needn't reach their ends.
Inputs may be any that keep to these rules, and one draw needn't show every extreme that they name: `cluster_perm`: for each item and head, a permutation of the item's 8192 positions that maps every aligned block of 512 positions onto itself; cluster c of the head is the 128 positions listed at places c * 128 to (c + 1) * 128 - 1. `cluster_pairs`: entry [i, h, c, p] names key-value cluster number p of query cluster c of head h in item i. The clusters of a device are, in each head, the 4 clusters of the positions it holds. Of the 96 entries of one device's query clusters (all heads and all p), at most 7 name clusters of one and the same device, and exactly 7 name clusters of some device.
All inputs are finite; a program needn't handle non-finite values.
Results may differ from the reference program's by a relative error of at most 0.015.
Values may be sent and summed in bfloat16 or wider, within the bound.
No kernel may reach another device: no remote copies, remote signals or barrier semaphores. Data moves between devices by JAX's collectives and lax.ppermute only.
A program may use at most 192 MiB of HBM per device.

```python
from functools import partial
import jax
import jax.numpy as jnp
from jax import lax

D = 768
HEADS = 12
HEAD_DIM = 64
FF = 3072
CLUS = 128
PAIRS = 2
TOK_DEV = 512
SEQ = 8192
TOKENS = 16384
NCL = 64
QC_DEV = 4
REQ = 96
CAP = 7
N_DP = 2
N_BLK = 16


def draw_cluster_perm(key, part):
    key = jax.random.fold_in(key, 11)
    noise = jax.random.randint(key, (N_DP, HEADS, N_BLK, TOK_DEV), 0, 1 << 19)
    ranked = noise * TOK_DEV + jnp.arange(TOK_DEV, dtype=jnp.int32)
    order = jnp.argsort(ranked, axis=-1, stable=True).astype(jnp.int32)
    base = (jnp.arange(N_BLK, dtype=jnp.int32) * TOK_DEV)[None, None, :, None]
    return (order + base).reshape(N_DP, HEADS, SEQ)


def draw_cluster_pairs(key, part):
    key = jax.random.fold_in(key, 23)
    key_first = jax.random.fold_in(key, 1)
    key_pick = jax.random.fold_in(key, 2)
    key_shuffle = jax.random.fold_in(key, 3)
    key_local = jax.random.fold_in(key, 4)
    groups = N_DP * N_BLK
    others = (N_BLK - 1) * CAP
    first = jax.random.randint(key_first, (groups, 1), 0, N_BLK)
    noise = jax.random.randint(key_pick, (groups, others), 0, 1 << 16)
    picked = jnp.argsort(noise * others + jnp.arange(others, dtype=jnp.int32), axis=-1, stable=True)[:, :REQ - CAP].astype(jnp.int32)
    relative = picked // CAP
    sources = relative + (relative >= first).astype(jnp.int32)
    sources = jnp.concatenate([jnp.broadcast_to(first, (groups, CAP)), sources], axis=1)
    shuffle_noise = jax.random.randint(key_shuffle, (groups, REQ), 0, 1 << 16)
    shuffle = jnp.argsort(shuffle_noise * REQ + jnp.arange(REQ, dtype=jnp.int32), axis=-1, stable=True).astype(jnp.int32)
    sources = jnp.take_along_axis(sources, shuffle, axis=1)
    local = jax.random.randint(key_local, (groups, REQ), 0, QC_DEV)
    clusters = sources * QC_DEV + local
    clusters = clusters.reshape(N_DP, N_BLK, HEADS, QC_DEV, PAIRS).transpose(0, 2, 1, 3, 4)
    return clusters.reshape(N_DP, HEADS, NCL, PAIRS).astype(jnp.int32)


def block_scale(stream_key, shape, split, smallest, high):
    gain = 1.0
    for axis_at, shards_of in split:
        heights = jax.random.uniform(jax.random.fold_in(jax.random.fold_in(stream_key, 6), axis_at), (shards_of,), jnp.float32, smallest / len(split), high / len(split))
        gain = gain * jnp.repeat(jnp.exp(heights), shape[axis_at] // shards_of).reshape((-1,) + (1,) * (len(shape) - 1 - axis_at))
    return gain


def scatter_about(stream_key, extent, deviation, most, shards=(), kind=jnp.bfloat16):
    array = jax.random.normal(stream_key, extent, jnp.float32) * deviation
    if len(shards) > 0:
        array = block_scale(stream_key, extent, shards, -0.22, 0.18) * array
    return jnp.clip(array, min=-most, max=most).astype(kind)


def setup_inputs(seed: int = 0) -> dict:
    keys = jax.random.split(jax.random.key(seed), 18)
    tokens = scatter_about(keys[0], (TOKENS, D), 1.0, 6.0, ((0, 32),))
    w_qkv = scatter_about(keys[1], (D, 3 * D), D ** -0.5, 0.21875)
    b_query = scatter_about(keys[2], (D,), 0.3, 1.796875)
    b_value = scatter_about(keys[3], (D,), 0.3, 1.796875)
    w_out = scatter_about(keys[4], (D, D), (D * 2 // (PAIRS * CLUS)) ** -0.5, 2.5)
    b_out = scatter_about(keys[5], (D,), 0.3, 1.796875)
    gain_one = jnp.clip(1.0 + 0.1 * jax.random.normal(keys[6], (D,), jnp.float32), 0.5, 1.5).astype(jnp.bfloat16)
    shift_one = scatter_about(keys[7], (D,), 0.3, 1.796875)
    w_up = scatter_about(keys[8], (D, FF), D ** -0.5, 0.21875)
    b_up = scatter_about(keys[9], (FF,), 0.3, 1.796875)
    w_down = scatter_about(keys[10], (FF, D), FF ** -0.5, 0.109375)
    b_down = scatter_about(keys[11], (D,), 0.3, 1.796875)
    gain_two = jnp.clip(1.0 + 0.1 * jax.random.normal(keys[12], (D,), jnp.float32), 0.5, 1.5).astype(jnp.bfloat16)
    shift_two = scatter_about(keys[13], (D,), 0.3, 1.796875)
    cluster_perm = draw_cluster_perm(jax.random.fold_in(keys[17], 71), 0)
    cluster_pairs = draw_cluster_pairs(jax.random.fold_in(keys[17], 71), 0)
    cotangent = scatter_about(keys[16], (TOKENS, D), 1.0, 6.0, ((0, 32),))
    return dict(tokens=tokens, w_qkv=w_qkv, b_query=b_query, b_value=b_value, w_out=w_out, b_out=b_out, gain_one=gain_one, shift_one=shift_one, w_up=w_up, b_up=b_up, w_down=w_down, b_down=b_down, gain_two=gain_two, shift_two=shift_two, cluster_perm=cluster_perm, cluster_pairs=cluster_pairs, cotangent=cotangent)


@jax.custom_vjp
def low(v):
    return lax.optimization_barrier(v.astype(jnp.bfloat16)).astype(jnp.float32)

@jax.custom_vjp
def low_back(v):
    return v

def low_keep(v):
    return (low(v), None)

def low_pass(kept, grad):
    return (grad,)

def back_keep(v):
    return (v, None)

def back_low(kept, grad):
    return (low(grad),)
low.defvjp(low_keep, low_pass)
low_back.defvjp(back_keep, back_low)

def dot_high(left, right):
    return jnp.dot(left, right, precision=lax.Precision.HIGHEST, preferred_element_type=jnp.float32)

def layer_norm(values, scaling, offset):
    average = lax.optimization_barrier(jnp.mean(values, -1, keepdims=True))
    centred = values - average
    variance = lax.optimization_barrier(jnp.mean(centred * centred, -1, keepdims=True))
    return centred * lax.rsqrt(variance + 1e-06) * scaling + offset

def attend_head(packed):
    query_rows, key_rows, value_rows, order_rows, partner = packed
    sorted_q = query_rows[order_rows].reshape(NCL, CLUS, HEAD_DIM)
    sorted_k = key_rows[order_rows].reshape(NCL, CLUS, HEAD_DIM)
    sorted_v = value_rows[order_rows].reshape(NCL, CLUS, HEAD_DIM)
    pair_k = sorted_k[partner].reshape(NCL, PAIRS * CLUS, HEAD_DIM)
    pair_v = sorted_v[partner].reshape(NCL, PAIRS * CLUS, HEAD_DIM)
    scores = jnp.einsum('cqd,ckd->cqk', sorted_q, pair_k, precision=lax.Precision.HIGHEST) * HEAD_DIM ** (-0.5)
    scores = low_back(scores)
    row_top = lax.optimization_barrier(jnp.max(scores, -1, keepdims=True))
    exponent = jnp.exp(scores - row_top)
    attention = low(exponent / lax.optimization_barrier(jnp.sum(exponent, -1, keepdims=True)))
    mixture = jnp.einsum('cqk,ckd->cqd', attention, pair_v, precision=lax.Precision.HIGHEST)
    return jnp.zeros((SEQ, HEAD_DIM), jnp.float32).at[order_rows].set(mixture.reshape(SEQ, HEAD_DIM))

def heads_first(tensor):
    return tensor.reshape(SEQ, HEADS, HEAD_DIM).transpose(1, 0, 2)

def layer(inputs, w_qkv, b_query, b_value, w_out, b_out, gain_one, shift_one, w_up, b_up, w_down, b_down, gain_two, shift_two, order, partner):
    projected = dot_high(inputs, w_qkv)
    queries = low(low_back(projected[:, :D] + b_query))
    keys_all = low(low_back(projected[:, D:2 * D]))
    values = low(low_back(projected[:, 2 * D:] + b_value))
    per_head = lax.map(jax.checkpoint(attend_head), (heads_first(queries), heads_first(keys_all), heads_first(values), order, partner))
    attn = low(low_back(per_head.transpose(1, 0, 2).reshape(SEQ, D)))
    branch = low_back(dot_high(attn, w_out) + b_out)
    normed = layer_norm(inputs + branch, gain_one, shift_one)
    inner_pre = low_back(dot_high(low(normed), w_up) + b_up)
    active = low(jax.nn.gelu(inner_pre, approximate=False))
    second = low_back(dot_high(active, w_down) + b_down)
    return layer_norm(normed + second, gain_two, shift_two)

def reference(tokens, w_qkv, b_query, b_value, w_out, b_out, gain_one, shift_one, w_up, b_up, w_down, b_down, gain_two, shift_two, cluster_perm, cluster_pairs, cotangent):
    params = tuple((item.astype(jnp.float32) for item in (w_qkv, b_query, b_value, w_out, b_out, gain_one, shift_one, w_up, b_up, w_down, b_down, gain_two, shift_two)))
    outputs = []
    input_grads = []
    summed = None
    for sequence in range(N_DP):
        item_rows = tokens[sequence * SEQ:(sequence + 1) * SEQ].astype(jnp.float32)
        bound_layer = partial(layer, order=cluster_perm[sequence], partner=cluster_pairs[sequence])
        result, pullback = jax.vjp(bound_layer, item_rows, *params)
        grads = pullback(cotangent[sequence * SEQ:(sequence + 1) * SEQ].astype(jnp.float32))
        outputs.append(result.astype(jnp.bfloat16))
        input_grads.append(grads[0].astype(jnp.bfloat16))
        if summed is None:
            summed = list(grads[1:])
        else:
            summed = [left + right for left, right in zip(summed, grads[1:])]
    layer_out = jnp.concatenate(outputs, 0)
    grad_tokens = jnp.concatenate(input_grads, 0)
    return (layer_out, grad_tokens, summed[0], summed[1], summed[2], summed[3], summed[4], summed[5], summed[6], summed[7], summed[8], summed[9], summed[10], summed[11], summed[12])
```

```python
from functools import partial

import jax
import jax.numpy as jnp
from jax import lax
from jax.sharding import PartitionSpec as P

D = 768
HEADS = 12
HEAD_DIM = 64
CLUS = 128
PAIRS = 2


def layer_norm(values, scaling, offset):
    average = jnp.mean(values, -1, keepdims=True)
    centred = values - average
    variance = jnp.mean(centred * centred, -1, keepdims=True)
    return centred * lax.rsqrt(variance + 1e-06) * scaling + offset


def column_sums(matrix):
    return jnp.sum(matrix.astype(jnp.float32), axis=0)


def swap(value, axis, distance):
    size = lax.axis_size(axis)
    return lax.ppermute(value, axis, [(i, i ^ distance) for i in range(size)])


def bit_of(axis, distance):
    return (lax.axis_index(axis) & distance) != 0


def routes(count_blk):
    dp = ("dp", 1)
    chip = [("blk", 2), ("blk", 4), ("blk", 8)]
    rest = []
    distance = 16
    while distance < count_blk:
        rest.append(("blk", distance))
        distance *= 2
    first = [dp, chip[0], chip[1], chip[2]]
    second = [chip[0], dp, chip[1], chip[2]]
    return first, second, rest


def add_low(left, right):
    return (left.astype(jnp.float32) + right.astype(jnp.float32)).astype(jnp.bfloat16)


def scatter_sum(value, route, rest):
    for axis, distance in route:
        half = value.shape[0] // 2
        low, high = value[:half], value[half:]
        bit = bit_of(axis, distance)
        given = swap(jnp.where(bit, low, high), axis, distance)
        value = add_low(jnp.where(bit, high, low), given)
    for axis, distance in rest:
        value = add_low(value, swap(value, axis, distance))
    return value


def gather_rows(value, route):
    for axis, distance in reversed(route):
        given = swap(value, axis, distance)
        bit = bit_of(axis, distance)
        value = jnp.where(
            bit, jnp.concatenate([given, value]), jnp.concatenate([value, given])
        )
    return value


def sum_everywhere(halves, count_blk):
    first, second, rest = routes(count_blk)
    core = lax.axis_index("blk") & 1
    mine = lax.dynamic_index_in_dim(halves, core, 0, keepdims=False)
    other = lax.dynamic_index_in_dim(halves, 1 - core, 0, keepdims=False)
    mine = add_low(mine, swap(other, "blk", 1))
    totals = [
        gather_rows(scatter_sum(mine[at], route, rest), route)
        for at, route in enumerate((first, second))
    ]
    own = jnp.stack(totals)
    given = swap(own, "blk", 1)
    return jnp.where(core == 1, jnp.stack([given, own]), jnp.stack([own, given]))


def per_device(
    tokens,
    w_qkv,
    b_query,
    b_value,
    w_out,
    b_out,
    gain_one,
    shift_one,
    w_up,
    b_up,
    w_down,
    b_down,
    gain_two,
    shift_two,
    cluster_perm,
    cluster_pairs,
    cotangent,
):
    count_blk = lax.axis_size("blk")
    my_index = lax.axis_index("blk")
    rows_dev = tokens.shape[0]
    per_dev = rows_dev // CLUS
    requests = per_dev * HEADS * PAIRS
    capacity = max(2, (requests + count_blk - 1) // count_blk + 1)
    score_scale = HEAD_DIM ** (-0.5)
    pair_width = 2 * HEAD_DIM
    local_order = cluster_perm[0] - my_index * rows_dev
    places = jnp.arange(rows_dev, dtype=jnp.int32)
    onehot = (local_order[:, :, None] == places[None, None, :]).astype(jnp.bfloat16)

    def sort_heads(tensor):
        shaped = tensor.reshape(rows_dev, HEADS, -1)
        return jnp.einsum(
            "hji,ihd->hjd", onehot, shaped, preferred_element_type=jnp.float32
        ).astype(jnp.bfloat16)

    def unsort_heads(tensor):
        return (
            jnp.einsum("hji,hjd->ihd", onehot, tensor, preferred_element_type=jnp.float32)
            .astype(jnp.bfloat16)
            .reshape(rows_dev, -1)
        )

    projected = jnp.dot(tokens, w_qkv, preferred_element_type=jnp.float32)
    queries = (projected[:, :D] + b_query.astype(jnp.float32)).astype(jnp.bfloat16)
    keys_all = projected[:, D : 2 * D].astype(jnp.bfloat16)
    values = (projected[:, 2 * D :] + b_value.astype(jnp.float32)).astype(jnp.bfloat16)
    q_sorted = sort_heads(queries).reshape(HEADS, per_dev, CLUS, HEAD_DIM)
    joined = jnp.concatenate(
        [keys_all.reshape(rows_dev, HEADS, HEAD_DIM), values.reshape(rows_dev, HEADS, HEAD_DIM)],
        axis=2,
    )
    kv_blocks = sort_heads(joined.reshape(rows_dev, HEADS * pair_width)).reshape(
        HEADS * per_dev, CLUS, pair_width
    )
    wanted = (
        cluster_pairs[0]
        .reshape(HEADS, count_blk, per_dev, PAIRS)
        .transpose(1, 0, 2, 3)
        .reshape(count_blk, requests)
    )
    positions = jnp.arange(requests, dtype=jnp.int32)
    before = positions[:, None] < positions[None, :]
    source = wanted // per_dev
    named = source == my_index
    rank = jnp.sum(named[:, :, None] & before[None], axis=1)
    head_of = positions // (per_dev * PAIRS)
    block_id = head_of[None, :] * per_dev + wanted % per_dev
    matches = named[:, :, None] & (
        rank[:, :, None] == jnp.arange(capacity, dtype=jnp.int32)[None, None, :]
    )
    filled = jnp.any(matches, axis=1)
    chosen = jnp.sum(jnp.where(matches, block_id[:, :, None], 0), axis=1)
    my_source = lax.dynamic_index_in_dim(wanted, my_index, 0, keepdims=False) // per_dev
    my_rank = jnp.sum((my_source[:, None] == my_source[None, :]) & before, axis=0)
    fetch_index = my_source * capacity + my_rank
    segment = jnp.where(filled, chosen, HEADS * per_dev).reshape(-1)
    outgoing = kv_blocks[chosen]
    arrived = lax.all_to_all(outgoing, "blk", split_axis=0, concat_axis=0, tiled=True)
    pairs_kv = arrived.reshape(count_blk * capacity, CLUS, pair_width)[fetch_index].reshape(
        HEADS, per_dev, PAIRS * CLUS, pair_width
    )
    pair_keys = pairs_kv[..., :HEAD_DIM]
    pair_values = pairs_kv[..., HEAD_DIM:]
    scores = (
        jnp.einsum("hcqd,hckd->hcqk", q_sorted, pair_keys, preferred_element_type=jnp.float32)
        * score_scale
    )
    row_top = jnp.max(scores, -1, keepdims=True)
    exponent = jnp.exp(scores - row_top)
    row_total = jnp.sum(exponent, -1, keepdims=True)
    attention = exponent / row_total
    attention_low = attention.astype(jnp.bfloat16)
    mixture = jnp.einsum(
        "hcqk,hckd->hcqd",
        attention_low,
        pair_values,
        preferred_element_type=jnp.float32,
    )
    attn = unsort_heads(mixture.astype(jnp.bfloat16).reshape(HEADS, rows_dev, HEAD_DIM))
    branch = jnp.dot(attn, w_out, preferred_element_type=jnp.float32) + b_out.astype(jnp.float32)
    resid = tokens.astype(jnp.float32) + branch
    normed, norm_one_back = jax.vjp(
        layer_norm, resid, gain_one.astype(jnp.float32), shift_one.astype(jnp.float32)
    )
    normed_low = normed.astype(jnp.bfloat16)
    inner_pre = jnp.dot(normed_low, w_up, preferred_element_type=jnp.float32) + b_up.astype(
        jnp.float32
    )
    active_full, gelu_back = jax.vjp(partial(jax.nn.gelu, approximate=False), inner_pre)
    active = active_full.astype(jnp.bfloat16)
    second = jnp.dot(active, w_down, preferred_element_type=jnp.float32) + b_down.astype(
        jnp.float32
    )
    result_full, norm_two_back = jax.vjp(
        layer_norm, normed + second, gain_two.astype(jnp.float32), shift_two.astype(jnp.float32)
    )
    layer_out = result_full.astype(jnp.bfloat16)
    grad_sum_two, grad_gain_two, grad_shift_two = norm_two_back(cotangent.astype(jnp.float32))
    grad_second = grad_sum_two.astype(jnp.bfloat16)
    grad_b_down = column_sums(grad_second)
    (grad_inner_full,) = gelu_back(
        jnp.dot(grad_second, w_down.T, preferred_element_type=jnp.float32)
    )
    grad_inner = grad_inner_full.astype(jnp.bfloat16)
    grad_b_up = column_sums(grad_inner)
    grad_normed = grad_sum_two + jnp.dot(grad_inner, w_up.T, preferred_element_type=jnp.float32)
    grad_resid, grad_gain_one, grad_shift_one = norm_one_back(grad_normed)
    grad_branch = grad_resid.astype(jnp.bfloat16)
    grad_b_out = column_sums(grad_branch)
    grad_attn = jnp.dot(grad_branch, w_out.T, preferred_element_type=jnp.float32).astype(
        jnp.bfloat16
    )
    grad_mixture = sort_heads(grad_attn).reshape(HEADS, per_dev, CLUS, HEAD_DIM)
    grad_probs = jnp.einsum(
        "hcqd,hckd->hcqk", grad_mixture, pair_values, preferred_element_type=jnp.float32
    )
    grad_values = jnp.einsum(
        "hcqk,hcqd->hckd",
        attention_low,
        grad_mixture,
        preferred_element_type=jnp.float32,
    )
    grad_scores = (
        attention * (grad_probs - jnp.sum(grad_probs * attention, -1, keepdims=True))
    ).astype(jnp.bfloat16)
    grad_query = (
        jnp.einsum("hcqk,hckd->hcqd", grad_scores, pair_keys, preferred_element_type=jnp.float32)
        * score_scale
    ).astype(jnp.bfloat16)
    grad_keys = (
        jnp.einsum("hcqk,hcqd->hckd", grad_scores, q_sorted, preferred_element_type=jnp.float32)
        * score_scale
    )
    grad_pair = jnp.concatenate([grad_keys, grad_values], axis=3).reshape(
        requests, CLUS, pair_width
    ).astype(jnp.bfloat16)
    returned = (
        jnp.zeros((count_blk * capacity, CLUS, pair_width), jnp.bfloat16)
        .at[fetch_index]
        .set(grad_pair)
    )
    returned_grads = lax.all_to_all(
        returned.reshape(count_blk, capacity, CLUS, pair_width),
        "blk",
        split_axis=0,
        concat_axis=0,
        tiled=True,
    ).astype(jnp.float32)
    grad_w_down = jnp.dot(active.T, grad_second, preferred_element_type=jnp.float32)
    grad_w_up = jnp.dot(normed_low.T, grad_inner, preferred_element_type=jnp.float32)
    grad_w_out = jnp.dot(attn.T, grad_branch, preferred_element_type=jnp.float32)
    grad_q = unsort_heads(grad_query.reshape(HEADS, rows_dev, HEAD_DIM))
    grad_w_q = jnp.dot(tokens.T, grad_q, preferred_element_type=jnp.float32)

    sum_down = sum_everywhere(
        grad_w_down.astype(jnp.bfloat16).reshape(2, 2, D, D), count_blk
    ).reshape(4 * D, D)
    sum_up = (
        sum_everywhere(
            jnp.stack(jnp.split(grad_w_up.astype(jnp.bfloat16), 4, axis=1)).reshape(2, 2, D, D),
            count_blk,
        )
        .reshape(4, D, D)
        .transpose(1, 0, 2)
        .reshape(D, 4 * D)
    )

    def two_matrices(first, second):
        both = jnp.stack([first, second]).astype(jnp.bfloat16)
        halves = both.reshape(2, D, 2, D // 2).transpose(2, 0, 1, 3)
        total = sum_everywhere(halves, count_blk)
        return total.transpose(1, 2, 0, 3).reshape(2, D, D)

    sum_q, sum_out = two_matrices(grad_w_q, grad_w_out)

    summed = jax.ops.segment_sum(
        returned_grads.reshape(count_blk * capacity, CLUS, pair_width),
        segment,
        num_segments=HEADS * per_dev + 1,
    )[: HEADS * per_dev].astype(jnp.bfloat16)
    grad_kv_rows = unsort_heads(summed.reshape(HEADS, rows_dev, pair_width)).reshape(
        rows_dev, HEADS, pair_width
    )
    grad_k = grad_kv_rows[:, :, :HEAD_DIM].reshape(rows_dev, D)
    grad_v = grad_kv_rows[:, :, HEAD_DIM:].reshape(rows_dev, D)
    grad_w_k = jnp.dot(tokens.T, grad_k, preferred_element_type=jnp.float32)
    grad_w_v = jnp.dot(tokens.T, grad_v, preferred_element_type=jnp.float32)
    sum_k, sum_v = two_matrices(grad_w_k, grad_w_v)
    grad_b_query = column_sums(grad_q)
    grad_b_value = jnp.sum(grad_values, axis=(1, 2)).reshape(D)
    vectors = (
        grad_b_query,
        grad_b_value,
        grad_b_out,
        grad_gain_one,
        grad_shift_one,
        grad_b_up,
        grad_b_down,
        grad_gain_two,
        grad_shift_two,
    )
    totals = lax.psum(jnp.concatenate(vectors), ("dp", "blk"))
    pieces = []
    offset = 0
    for vector in vectors:
        pieces.append(totals[offset : offset + vector.shape[0]])
        offset += vector.shape[0]
    sum_qkv = jnp.concatenate([sum_q, sum_k, sum_v], axis=1)
    grad_proj = jnp.concatenate([grad_q, grad_k, grad_v], axis=1)
    grad_tokens = (
        grad_resid + jnp.dot(grad_proj, w_qkv.T, preferred_element_type=jnp.float32)
    ).astype(jnp.bfloat16)
    return (
        layer_out,
        grad_tokens,
        sum_qkv.astype(jnp.float32),
        pieces[0],
        pieces[1],
        sum_out.astype(jnp.float32),
        pieces[2],
        pieces[3],
        pieces[4],
        sum_up.astype(jnp.float32),
        pieces[5],
        sum_down.astype(jnp.float32),
        pieces[6],
        pieces[7],
        pieces[8],
    )


def solution(mesh):
    whole = P()
    rows = P(("dp", "blk"), None)
    return jax.shard_map(
        per_device,
        mesh=mesh,
        in_specs=(
            (rows,)
            + (whole,) * 13
            + (P("dp", None, "blk"), P("dp", None, None, None), rows)
        ),
        out_specs=(rows, rows) + (whole,) * 13,
        check_vma=False,
    )
```

```python
from functools import partial

import jax
import jax.numpy as jnp
from jax import lax
from jax.experimental import pallas as pl
from jax.experimental.pallas import tpu as pltpu
from jax.sharding import PartitionSpec as P

D = 768
HEADS = 12
HEAD_DIM = 64
CLUS = 128
PAIRS = 2
LANES = 128

F32 = jnp.float32
LOW = jnp.bfloat16


def nn(left, right):
    return jnp.dot(left, right, preferred_element_type=F32)


def nt(left, right):
    return lax.dot_general(left, right, (((1,), (1,)), ((), ())), preferred_element_type=F32)


def tn(left, right):
    return lax.dot_general(left, right, (((0,), (0,)), ((), ())), preferred_element_type=F32)


def left_half(shape):
    return lax.broadcasted_iota(jnp.int32, shape, 1) < HEAD_DIM


def pick(hot):
    return jnp.where(hot, 1.0, 0.0).astype(LOW)


def params(megabytes=60):
    return pltpu.CompilerParams(vmem_limit_bytes=megabytes << 20)


def kv_kernel(chosen, tok, w_key, w_value, b_value, order, out, blocks, sem):
    rows = tok.shape[0]
    per_dev = rows // CLUS
    place = lax.broadcasted_iota(jnp.int32, (rows, rows), 1)
    left = left_half((rows, 2 * HEAD_DIM))
    inputs = tok[...]
    for quad in range(HEADS // 4):
        four = slice(quad * 4 * HEAD_DIM, (quad + 1) * 4 * HEAD_DIM)
        keys = nn(inputs, w_key[:, four])
        values = nn(inputs, w_value[:, four]) + b_value[:, four].astype(F32)
        for pair in range(2):
            two = slice(pair * 2 * HEAD_DIM, (pair + 1) * 2 * HEAD_DIM)
            key_two = keys[:, two]
            value_two = pltpu.roll(values[:, two], HEAD_DIM, 1)
            for odd in range(2):
                head = quad * 4 + pair * 2 + odd
                joined = jnp.where(left, value_two, key_two) if odd else jnp.where(left, key_two, value_two)
                hot = pick(order[:, head : head + 1] == place)
                ranked = nn(hot, joined.astype(LOW)).astype(LOW)
                blocks[head * per_dev : (head + 1) * per_dev] = ranked.reshape(per_dev, CLUS, 2 * HEAD_DIM)
    devices, capacity = chosen.shape

    @pl.loop(0, devices)
    def _(device):
        for slot in range(capacity):
            pltpu.make_async_copy(
                blocks.at[chosen[device, slot]], out.at[device * capacity + slot], sem
            ).start()

    pltpu.make_async_copy(out, out, sem).wait()


def q_kernel(tok, w_query, b_query, order, out):
    rows = tok.shape[0]
    place = lax.broadcasted_iota(jnp.int32, (rows, rows), 1)
    left = left_half((rows, 2 * HEAD_DIM))
    inputs = tok[...]
    for quad in range(HEADS // 4):
        four = slice(quad * 4 * HEAD_DIM, (quad + 1) * 4 * HEAD_DIM)
        queries = nn(inputs, w_query[:, four]) + b_query[:, four].astype(F32)
        queries = (queries.astype(LOW).astype(F32) * HEAD_DIM ** (-0.5)).astype(LOW)
        for pair in range(2):
            two = queries[:, pair * 2 * HEAD_DIM : (pair + 1) * 2 * HEAD_DIM]
            for odd in range(2):
                head = quad * 4 + pair * 2 + odd
                hot = pick(order[:, head : head + 1] == place)
                ranked = nn(hot, two)
                kept = jnp.where(left, 0.0, ranked) if odd else jnp.where(left, ranked, 0.0)
                out[head] = kept.astype(LOW)


ROW_TILE = 128
WIDE = 768


def mid_kernel(
    fetch, queries, arrived, order, inverse, tok, cot, vecs, b_up, w_out_hbm, w_up_hbm, w_down_hbm,
    back, dq_out, attn_out, z_out, active_out, du_out, df_out, db_out, dh1_out, layer_out, sums,
    kv, probs, attn, mixed, w_out, w_up, w_down, hidden, z_full, n_one, r_one, z_low, active, slope,
    dh2, df, db, d_out, dh1, final, dq, kv_sem, w_sem, out_sem, back_sem,
):
    rows = tok.shape[0]
    per_dev = rows // CLUS
    pair_width = 2 * HEAD_DIM
    requests = fetch.shape[0]
    each = 2 * per_dev * PAIRS
    width = w_up.shape[1]
    tiles = rows // ROW_TILE
    left = left_half((CLUS, pair_width))
    left_rows = left_half((rows, pair_width))
    down = lax.broadcasted_iota(jnp.int32, (rows, rows), 0)

    @pl.loop(0, HEADS // 2)
    def _(group):
        for step in range(each):
            entry = group * each + step
            pltpu.make_async_copy(arrived.at[fetch[entry]], kv.at[entry], kv_sem.at[group]).start()

    loads = [
        pltpu.make_async_copy(source, target, w_sem.at[at])
        for at, (source, target) in enumerate(
            ((w_out_hbm, w_out), (w_up_hbm, w_up), (w_down_hbm, w_down))
        )
    ]
    for load in loads:
        load.start()
    stores = []

    def store(source, target):
        copy = pltpu.make_async_copy(source, target, out_sem.at[len(stores)])
        copy.start()
        stores.append(copy)

    @pl.loop(0, HEADS // 2)
    def _(group):
        span = kv.at[pl.ds(group * each, each)]
        pltpu.make_async_copy(span, span, kv_sem.at[group]).wait()
        for odd in range(2):
            head = 2 * group + odd
            for cluster in range(per_dev):
                unit = head * per_dev + cluster
                query = queries[head, cluster * CLUS : (cluster + 1) * CLUS, :]
                pair = kv[pl.ds(unit * PAIRS, PAIRS)].reshape(PAIRS * CLUS, pair_width)
                scores = nt(query, pair)
                exponent = jnp.exp(scores - jnp.max(scores, -1, keepdims=True))
                low = (exponent / jnp.sum(exponent, -1, keepdims=True)).astype(LOW)
                probs[unit] = low
                mixed[odd, cluster * CLUS : (cluster + 1) * CLUS, :] = nn(low, pair).astype(LOW)
        even = nn(pick(down == order[2 * group]), mixed[0])
        other = nn(pick(down == order[2 * group + 1]), mixed[1])
        both = pltpu.roll(jnp.where(left_rows, other, even), HEAD_DIM, 1)
        attn[:, pl.ds(pl.multiple_of(group * pair_width, pair_width), pair_width)] = both.astype(LOW)

    store(attn, attn_out)
    loads[0].wait()
    hidden[...] = nn(attn[...], w_out[...])

    @pl.loop(0, tiles)
    def _(tile):
        at = pl.ds(pl.multiple_of(tile * ROW_TILE, ROW_TILE), ROW_TILE)
        value = hidden[at, :] + (vecs[0:1, :] + tok[at, :].astype(F32))
        centred = value - jnp.mean(value, -1, keepdims=True)
        scale = lax.rsqrt(jnp.mean(centred * centred, -1, keepdims=True) + 1e-06)
        unit = centred * scale
        z = unit * vecs[1:2, :] + vecs[2:3, :]
        n_one[at, :] = unit
        r_one[at, :] = scale
        z_low[at, :] = z.astype(LOW)
        z_full[at, :] = z
        hidden[at, :] = z + vecs[3:4, :]

    store(z_low, z_out)
    loads[1].wait()
    loads[2].wait()

    @pl.loop(0, width // WIDE)
    def _(step):
        at = pl.ds(pl.multiple_of(step * WIDE, WIDE), WIDE)
        inner = nn(z_low[...], w_up[:, at]) + b_up[:, at]
        normal = 0.5 * (1.0 + lax.erf(inner * 0.7071067811865476))
        density = jnp.exp(inner * inner * -0.5) * 0.3989422804014327
        active[:, at] = (inner * normal).astype(LOW)
        slope[:, at] = (normal + inner * density).astype(LOW)
        hidden[...] += nn(active[:, at], w_down[at, :])

    store(active, active_out)
    sums[...] = jnp.zeros_like(sums)

    @pl.loop(0, tiles)
    def _(tile):
        at = pl.ds(pl.multiple_of(tile * ROW_TILE, ROW_TILE), ROW_TILE)
        value = hidden[at, :]
        centred = value - jnp.mean(value, -1, keepdims=True)
        scale = lax.rsqrt(jnp.mean(centred * centred, -1, keepdims=True) + 1e-06)
        unit = centred * scale
        final[at, :] = (unit * vecs[4:5, :] + vecs[5:6, :]).astype(LOW)
        grad = cot[at, :].astype(F32)
        lifted = grad * vecs[4:5, :]
        back_grad = scale * (
            lifted - jnp.mean(lifted, -1, keepdims=True) - unit * jnp.mean(lifted * unit, -1, keepdims=True)
        )
        dh2[at, :] = back_grad
        low = back_grad.astype(LOW)
        df[at, :] = low
        sums[0:1, :] += jnp.sum(grad * unit, axis=0, keepdims=True)
        sums[1:2, :] += jnp.sum(grad, axis=0, keepdims=True)
        sums[2:3, :] += jnp.sum(low.astype(F32), axis=0, keepdims=True)

    store(final, layer_out)
    store(df, df_out)
    ones = jnp.ones((8, rows), LOW)

    @pl.loop(0, width // WIDE)
    def _(step):
        at = pl.ds(pl.multiple_of(step * WIDE, WIDE), WIDE)
        grad = (nt(df[...], w_down[at, :]) * slope[:, at].astype(F32)).astype(LOW)
        slope[:, at] = grad
        sums[pl.ds(8 + step, 1), :] = nn(ones, grad)[0:1]
        dh2[...] += nt(grad, w_up[:, at])

    store(slope, du_out)

    @pl.loop(0, tiles)
    def _(tile):
        at = pl.ds(pl.multiple_of(tile * ROW_TILE, ROW_TILE), ROW_TILE)
        grad = dh2[at, :]
        unit = n_one[at, :]
        lifted = grad * vecs[1:2, :]
        back_grad = r_one[at, :] * (
            lifted - jnp.mean(lifted, -1, keepdims=True) - unit * jnp.mean(lifted * unit, -1, keepdims=True)
        )
        dh1[at, :] = back_grad
        low = back_grad.astype(LOW)
        db[at, :] = low
        sums[3:4, :] += jnp.sum(grad * unit, axis=0, keepdims=True)
        sums[4:5, :] += jnp.sum(grad, axis=0, keepdims=True)
        sums[5:6, :] += jnp.sum(low.astype(F32), axis=0, keepdims=True)

    store(dh1, dh1_out)
    store(db, db_out)
    d_out[...] = nt(db[...], w_out[...]).astype(LOW)

    @pl.loop(0, HEADS // 2)
    def _(group):
        lanes = pl.ds(pl.multiple_of(group * pair_width, pair_width), pair_width)
        tile = d_out[:, lanes]
        bias = []
        q_total = jnp.zeros((1, pair_width), F32)
        for odd in range(2):
            head = 2 * group + odd
            turned = pltpu.roll(nn(pick(down == inverse[head]), tile), HEAD_DIM, 1)
            grads = (jnp.where(left_rows, turned, 0.0) if odd else jnp.where(left_rows, 0.0, turned)).astype(LOW)
            total = jnp.zeros((1, pair_width), F32)
            for cluster in range(per_dev):
                unit = head * per_dev + cluster
                query = queries[head, cluster * CLUS : (cluster + 1) * CLUS, :]
                grad = grads[cluster * CLUS : (cluster + 1) * CLUS]
                pair = kv[pl.ds(unit * PAIRS, PAIRS)].reshape(PAIRS * CLUS, pair_width)
                low = probs[unit]
                wide = low.astype(F32)
                d_probs = nt(grad, pair)
                d_scores = (wide * (d_probs - jnp.sum(d_probs * wide, -1, keepdims=True))).astype(LOW)
                d_query = nn(d_scores, pair) * HEAD_DIM ** (-0.5)
                d_query = (jnp.where(left, 0.0, d_query) if odd else jnp.where(left, d_query, 0.0)).astype(LOW)
                dq[head, cluster * CLUS : (cluster + 1) * CLUS, :] = d_query
                q_total += jnp.sum(d_query.astype(F32), axis=0, keepdims=True)
                d_pair = tn(d_scores, query) + tn(low, grad)
                total += jnp.sum(d_pair, axis=0, keepdims=True)
                kv[pl.ds(unit * PAIRS, PAIRS)] = d_pair.astype(LOW).reshape(PAIRS, CLUS, pair_width)
                for part in range(PAIRS):
                    entry = unit * PAIRS + part
                    pltpu.make_async_copy(kv.at[entry], back.at[fetch[entry]], back_sem).start()
            bias.append(total)
        both = jnp.where(left_half((1, pair_width)), bias[1], bias[0])
        sums[7:8, lanes] = q_total
        sums[6:7, lanes] = pltpu.roll(jnp.broadcast_to(both, (8, pair_width)), HEAD_DIM, 1)[0:1]

    store(dq, dq_out)
    span = back.at[pl.ds(0, requests)]
    pltpu.make_async_copy(kv, span, back_sem).wait()
    for copy in stores:
        copy.wait()


CHUNKS = 16


def chunk_rows(at, size):
    return pl.ds(pl.multiple_of(at * size, size), size)


def place_chunks(source, target, info, sem, start=1):
    size = source.shape[0] // CHUNKS
    for chunk in range(CHUNKS):
        pltpu.make_async_copy(
            source.at[chunk * size : (chunk + 1) * size],
            target.at[chunk_rows(info[start + chunk], size)],
            sem,
        ).start()


def wait_chunks(source, target, sem):
    pltpu.make_async_copy(source, target, sem).wait()


def core_of(info, side):
    return info[0] if side else 1 - info[0]


def up_kernel(info, z_low, grad, give, keep, turned, buf, sem):
    half = keep.shape[1]
    turned[...] = z_low[...].T
    for side, out in ((0, give), (1, keep)):
        base = core_of(info, side) * half

        @pl.loop(0, half // WIDE)
        def _(step):
            at = pl.ds(pl.multiple_of(base + step * WIDE, WIDE), WIDE)
            to = pl.ds(pl.multiple_of(step * WIDE, WIDE), WIDE)
            buf[side, :, to] = nn(turned[...], grad[:, at]).astype(LOW)

        place_chunks(buf.at[side], out, info, sem.at[side])
    for side, out in ((0, give), (1, keep)):
        wait_chunks(buf.at[side], out, sem.at[side])


def down_kernel(info, active, grad, give, keep, buf, sem):
    size = keep.shape[0]
    for side, out in ((0, give), (1, keep)):
        for part in range(keep.shape[1] // size):
            block = core_of(info, side) * (keep.shape[1] // size) + part
            at = pl.ds(pl.multiple_of(block * size, size), size)
            buf[side, :, part * size : (part + 1) * size] = nn(active[:, at].T, grad[...]).astype(LOW)
        place_chunks(buf.at[side], out, info, sem.at[side])
    for side, out in ((0, give), (1, keep)):
        wait_chunks(buf.at[side], out, sem.at[side])


def out_q_kernel(info, attn, db, tok, dq, order, sums, give, keep, grad_q, attn_t, tok_t, buf, sem):
    rows = tok.shape[0]
    half = D // 2
    down = lax.broadcasted_iota(jnp.int32, (rows, rows), 0)
    for pair in range(HEADS // 2):
        total = nn(pick(down == order[2 * pair]), dq[2 * pair])
        total += nn(pick(down == order[2 * pair + 1]), dq[2 * pair + 1])
        lanes = slice(pair * 2 * HEAD_DIM, (pair + 1) * 2 * HEAD_DIM)
        grad_q[:, lanes] = total.astype(LOW)
    attn_t[...] = attn[...].T
    tok_t[...] = tok[...].T
    size = D // CHUNKS
    filler = jnp.zeros((size - D // LANES, LANES), F32)
    for vector in range(CHUNKS):
        rows_of = [sums[vector : vector + 1, row * LANES : (row + 1) * LANES] for row in range(D // LANES)]
        value = jnp.concatenate(rows_of + [filler]).astype(LOW)
        for side in range(2):
            buf[side, vector * size : (vector + 1) * size, D:] = value
    for side, out in ((0, give), (1, keep)):
        at = pl.ds(pl.multiple_of(core_of(info, side) * half, half), half)
        buf[side, :, :half] = nn(attn_t[...], db[:, at]).astype(LOW)
        buf[side, :, half:D] = nn(tok_t[...], grad_q[:, at]).astype(LOW)
        place_chunks(buf.at[side], out, info, sem.at[side], 65)
    for side, out in ((0, give), (1, keep)):
        wait_chunks(buf.at[side], out, sem.at[side])


def key_value_kernel(
    info, segment, returned, order, tok, key_give, key_keep, value_give, value_keep, grad_kv, total, tok_t, buf, sem
):
    rows = tok.shape[0]
    half = D // 2
    per_dev = rows // CLUS
    pair_width = 2 * HEAD_DIM
    down = lax.broadcasted_iota(jnp.int32, (rows, rows), 0)
    left = left_half((rows, pair_width))
    total[...] = jnp.zeros_like(total)

    @pl.loop(0, segment.shape[0])
    def _(slot):
        block = segment[slot]
        total[block] += returned[slot].astype(F32)

    for pair in range(HEADS // 2):
        placed = []
        for head in (2 * pair, 2 * pair + 1):
            summed = total[head * per_dev : (head + 1) * per_dev].reshape(rows, pair_width)
            placed.append(nn(pick(down == order[head]), summed.astype(LOW)))
        even, odd = placed
        grad_kv[:, pair * pair_width : (pair + 1) * pair_width] = jnp.where(left, even, odd).astype(LOW)
        values = pltpu.roll(jnp.where(left, odd, even), HEAD_DIM, 1)
        grad_kv[:, D + pair * pair_width : D + (pair + 1) * pair_width] = values.astype(LOW)
    tok_t[...] = tok[...].T
    outs = ((key_give, key_keep), (value_give, value_keep))
    for side in range(2):
        base = core_of(info, side) * half
        for part in range(2):
            at = pl.ds(pl.multiple_of(part * D + base, half), half)
            buf[part, side] = nn(tok_t[...], grad_kv[:, at]).astype(LOW)
            place_chunks(buf.at[part, side], outs[part][side], info, sem.at[part, side], 65 if part else 1)
    for side in range(2):
        for part in range(2):
            wait_chunks(buf.at[part, side], outs[part][side], sem.at[part, side])


def spread_start(info, start, pieces, targets, buf, sem):
    size = buf.shape[2]
    copies = []
    for at, piece in enumerate(pieces):
        core = core_of(info, 1 - at)
        for chunk in range(CHUNKS // 2):
            buf[at, chunk] = piece[chunk * size : (chunk + 1) * size].astype(F32)
            for lanes, target in targets(core, info[start + chunk], size, at == 0):
                copies.append(pltpu.make_async_copy(buf.at[at, chunk, : target.shape[0], lanes], target, sem))
                copies[-1].start()
    return copies


def spread(info, start, pieces, targets, buf, sem):
    for copy in spread_start(info, start, pieces, targets, buf, sem):
        copy.wait()


def up_targets(out, half):
    def targets(core, chunk, size, mine):
        rows = chunk_rows(chunk, size)
        yield pl.ds(0, half), out.at[rows, pl.ds(pl.multiple_of(core * half, half), half)]

    return targets


def down_targets(out, half):
    parts = half // D

    def targets(core, chunk, size, mine):
        rows = chunk_rows(chunk, size)
        for part in range(parts):
            yield pl.ds(part * D, D), out.at[core * parts + part, rows]

    return targets


def attention_targets(w_out, w_qkv, vectors, wide):
    half = D // 2

    def targets(core, chunk, size, mine):
        rows = chunk_rows(chunk, size)
        at = pl.ds(pl.multiple_of(core * half, half), half)
        yield pl.ds(0, half), w_out.at[rows, at]
        for part, lane in enumerate((half, D + LANES, D + LANES + half)):
            to = pl.ds(pl.multiple_of(part * D + core * half, half), half)
            yield pl.ds(lane, half), w_qkv.at[rows, to]
        if mine:
            yield pl.ds(D, LANES), vectors.at[chunk]

    return targets


def spread_kernel(start, route, count, info, mine, other, *refs):
    buf, sem = refs[-2:]
    spread(info, start, (mine, other), route(*refs[:count], mine.shape[1]), buf, sem)


def spread_last_kernel(info, *refs):
    pieces, outs, staged, bufs = refs[:6], refs[11:16], refs[16:22], refs[22:25]
    load_sem, sem = refs[25:]
    w_up, w_down, w_out, w_qkv, vectors = outs
    half = w_up.shape[1] // 2
    loads = []
    for at, (source, target) in enumerate(zip(pieces, staged)):
        loads.append(pltpu.make_async_copy(source, target, load_sem.at[at]))
        loads[-1].start()
    routes = (up_targets(w_up, half), down_targets(w_down, half), attention_targets(w_out, w_qkv, vectors, half))
    copies = []
    for at, (start, targets) in enumerate(zip((25, 41, 57), routes)):
        for load in loads[2 * at : 2 * at + 2]:
            load.wait()
        copies += spread_start(info, start, staged[2 * at : 2 * at + 2], targets, bufs[at], sem.at[at])
    for copy in copies:
        copy.wait()


X, Y, Z0, Z1 = ("dp", 1), ("blk", 2), ("blk", 4), ("blk", 8)
CORE = ("blk", 1)


def swap(value, bit):
    axis, distance = bit
    size = lax.axis_size(axis)
    return lax.ppermute(value, axis, [(i, i ^ distance) for i in range(size)])


def further_bits(count_blk):
    bits = []
    distance = 16
    while distance < count_blk:
        bits.append(("blk", distance))
        distance *= 2
    return bits


def chip_bits():
    return [(lax.axis_index(axis) // distance) % 2 for axis, distance in (X, Y, Z0, Z1)]


def chunk_places():
    x, y, z0, z1 = chip_bits()
    chip = x * 8 + y * 4 + z0 * 2 + z1
    core = lax.axis_index("blk") % 2
    every = jnp.arange(CHUNKS, dtype=jnp.int32)
    value = {X: 8, Y: 4, Z0: 2, Z1: 1}

    def from_order(order):
        at = sum(((every // 2**step) % 2) * value[bit] for step, bit in enumerate(order))
        return at ^ chip

    placed = every ^ chip
    x_y_swapped = placed % 4 + (placed // 8) * 4 + (placed // 4 % 2) * 8
    return jnp.concatenate(
        [core[None], placed]
        + [from_order(order) for order in (ORDER_X, ORDER_Y, ORDER_Z)]
        + [x_y_swapped]
    )


ORDER_X = (Z1, Z0, Y, X)
ORDER_Y = (Z1, X, Z0, Y)
ORDER_Z = (Z1, Y, X, Z0)


def sum_rows(terms, low, high):
    total = terms[0][low:high].astype(F32)
    for term in terms[1:]:
        total = total + term[low:high].astype(F32)
    return total


def scatter_start(terms, bits):
    rows = terms[-1].shape[0]
    for bit in bits:
        if len(terms) > 2:
            rows = terms[-1].shape[0]
        terms = terms + [swap(sum_rows(terms, rows // 2, rows).astype(LOW), bit)]
        rows //= 2
    return terms


def scatter_end(sets, bits, further):
    rows = sets[0][-1].shape[0]
    more = []

    def total(low, high):
        value = jnp.concatenate([sum_rows(terms, low, high) for terms in sets], axis=1)
        for term in more:
            value = value + term[low:high].astype(F32)
        return value.astype(LOW)

    for bit in bits:
        more.append(swap(total(rows // 2, rows), bit))
        rows //= 2
    value = total(0, rows)
    for bit in further:
        value = sum_rows([value, swap(value, bit)], 0, rows).astype(LOW)
    return value


def tie(values):
    return lax.optimization_barrier(tuple(values))


def gather_rows(values, orders):
    for step in range(len(orders[0]) - 1):
        values = tie(
            jnp.concatenate([value, swap(value, order[step])]) for value, order in zip(values, orders)
        )
    return values


def per_device(
    tokens,
    w_qkv,
    b_query,
    b_value,
    w_out,
    b_out,
    gain_one,
    shift_one,
    w_up,
    b_up,
    w_down,
    b_down,
    gain_two,
    shift_two,
    cluster_perm,
    cluster_pairs,
    cotangent,
):
    count_blk = lax.axis_size("blk")
    my_index = lax.axis_index("blk")
    rows = tokens.shape[0]
    per_dev = rows // CLUS
    blocks = HEADS * per_dev
    requests = blocks * PAIRS
    capacity = max(2, (requests + count_blk - 1) // count_blk + 1)
    slots = count_blk * capacity
    pair_width = 2 * HEAD_DIM
    ff = w_up.shape[1]
    local_order = cluster_perm[0] - my_index * rows
    order_cols = local_order.T
    order_rows = local_order[:, None, :]

    wanted = (
        cluster_pairs[0]
        .reshape(HEADS, count_blk, per_dev, PAIRS)
        .transpose(1, 0, 2, 3)
        .reshape(count_blk, requests)
    )
    positions = jnp.arange(requests, dtype=jnp.int32)
    before = positions[:, None] < positions[None, :]
    source = wanted // per_dev
    named = source == my_index
    rank = jnp.sum(named[:, :, None] & before[None], axis=1)
    head_of = positions // (per_dev * PAIRS)
    block_id = head_of[None, :] * per_dev + wanted % per_dev
    matches = named[:, :, None] & (
        rank[:, :, None] == jnp.arange(capacity, dtype=jnp.int32)[None, None, :]
    )
    chosen = jnp.sum(jnp.where(matches, block_id[:, :, None], 0), axis=1)

    smem = pl.BlockSpec(memory_space=pltpu.SMEM)
    vmem = pl.BlockSpec(memory_space=pltpu.VMEM)
    hbm = pl.BlockSpec(memory_space=pl.ANY)

    def column_block(at):
        return pl.BlockSpec((D, D), lambda step: (0, at))

    outgoing = pl.pallas_call(
        kv_kernel,
        grid=(1,),
        out_shape=jax.ShapeDtypeStruct((slots, CLUS, pair_width), LOW),
        in_specs=[smem, vmem, column_block(1), column_block(2), vmem, vmem],
        out_specs=hbm,
        scratch_shapes=[pltpu.VMEM((blocks, CLUS, pair_width), LOW), pltpu.SemaphoreType.DMA],
        compiler_params=params(),
        name="kv_kernel",
    )(chosen, tokens, w_qkv, w_qkv, b_value[None], order_cols)
    arrived = lax.all_to_all(
        outgoing.reshape(count_blk, capacity, CLUS, pair_width),
        "blk",
        split_axis=0,
        concat_axis=0,
        tiled=True,
    ).reshape(slots, CLUS, pair_width)

    info = chunk_places()
    queries = pl.pallas_call(
        q_kernel,
        grid=(1,),
        out_shape=jax.ShapeDtypeStruct((HEADS, rows, pair_width), LOW),
        in_specs=[vmem, column_block(0), vmem, vmem],
        out_specs=vmem,
        compiler_params=params(),
        name="q_kernel",
    )(tokens, w_qkv, b_query[None], order_cols)
    filled = jnp.any(matches, axis=1)
    segment = jnp.where(filled, chosen, blocks).reshape(-1)
    my_source = lax.dynamic_index_in_dim(wanted, my_index, 0, keepdims=False) // per_dev
    my_rank = jnp.sum((my_source[:, None] == my_source[None, :]) & before, axis=0)
    fetch = my_source * capacity + my_rank
    places = jnp.arange(rows, dtype=jnp.int32)
    inverse = jnp.sum(
        jnp.where(local_order[:, :, None] == places, places[None, :, None], 0), axis=1
    )[:, None, :]
    vecs = jnp.stack(
        [b_out, gain_one, shift_one, b_down, gain_two, shift_two, b_down, b_down]
    ).astype(F32)

    def low(*shape):
        return jax.ShapeDtypeStruct(shape, LOW)

    def full(*shape):
        return jax.ShapeDtypeStruct(shape, F32)

    (
        back, dq_sorted, attn, normed, active, grad_inner, grad_second, grad_branch, grad_resid,
        layer_out, sums,
    ) = pl.pallas_call(
        mid_kernel,
        out_shape=(
            low(slots, CLUS, pair_width), low(HEADS, rows, pair_width), low(rows, D), low(rows, D),
            low(rows, ff), low(rows, ff), low(rows, D), low(rows, D), full(rows, D), low(rows, D),
            full(16, D),
        ),
        in_specs=[smem, vmem, hbm, vmem, vmem, vmem, vmem, vmem, vmem, hbm, hbm, hbm],
        out_specs=(hbm,) * 10 + (vmem,),
        scratch_shapes=[
            pltpu.VMEM((requests, CLUS, pair_width), LOW),
            pltpu.VMEM((blocks, CLUS, PAIRS * CLUS), LOW),
            pltpu.VMEM((rows, D), LOW),
            pltpu.VMEM((2, rows, pair_width), LOW),
            pltpu.VMEM((D, D), LOW),
            pltpu.VMEM((D, ff), LOW),
            pltpu.VMEM((ff, D), LOW),
            pltpu.VMEM((rows, D), F32),
            pltpu.VMEM((rows, D), F32),
            pltpu.VMEM((rows, D), F32),
            pltpu.VMEM((rows, 1), F32),
            pltpu.VMEM((rows, D), LOW),
            pltpu.VMEM((rows, ff), LOW),
            pltpu.VMEM((rows, ff), LOW),
            pltpu.VMEM((rows, D), F32),
            pltpu.VMEM((rows, D), LOW),
            pltpu.VMEM((rows, D), LOW),
            pltpu.VMEM((rows, D), LOW),
            pltpu.VMEM((rows, D), F32),
            pltpu.VMEM((rows, D), LOW),
            pltpu.VMEM((HEADS, rows, pair_width), LOW),
            pltpu.SemaphoreType.DMA((HEADS // 2,)),
            pltpu.SemaphoreType.DMA((3,)),
            pltpu.SemaphoreType.DMA((9,)),
            pltpu.SemaphoreType.DMA,
        ],
        compiler_params=params(),
        name="mid_kernel",
    )(
        fetch, queries, arrived, order_rows, inverse, tokens, cotangent, vecs,
        b_up[None].astype(F32), w_out, w_up, w_down,
    )
    returned = lax.all_to_all(
        back.reshape(count_blk, capacity, CLUS, pair_width),
        "blk",
        split_axis=0,
        concat_axis=0,
        tiled=True,
    ).reshape(slots, CLUS, pair_width)

    further = further_bits(count_blk)

    def halves(kernel, operands, columns, scratch, more=(), name=None):
        return pl.pallas_call(
            kernel,
            out_shape=(low(D, columns), low(D, columns)) + more,
            in_specs=[smem] + [vmem] * (len(operands) - 1),
            out_specs=(hbm, hbm) + (vmem,) * len(more),
            scratch_shapes=scratch
            + [pltpu.VMEM((2, D, columns), LOW), pltpu.SemaphoreType.DMA((2,))],
            compiler_params=params(),
            cost_estimate=pl.CostEstimate(flops=1, bytes_accessed=1, transcendentals=0),
            name=name,
        )(*operands)

    half = D // 2
    turned = pltpu.VMEM((D, rows), LOW)
    up_give, up_keep = halves(
        up_kernel, (info, normed, grad_inner), ff // 2, [turned], name="up_kernel"
    )
    down_give, down_keep = halves(
        down_kernel, (info, active, grad_second), ff // 2, [], name="down_kernel"
    )
    oq_give, oq_keep, grad_q = halves(
        out_q_kernel,
        (info, attn, grad_branch, tokens, dq_sorted, order_rows, sums),
        D + LANES,
        [turned, turned],
        (low(rows, D),),
        name="out_q_kernel",
    )
    up = scatter_start([up_keep, swap(up_give, CORE)], (X, Y))
    down = scatter_start([down_keep, swap(down_give, CORE)], (X, Y))
    out_q = scatter_start([oq_keep, swap(oq_give, CORE)], (Y, X))

    returned, up[-1], down[-1], out_q[-1] = tie((returned, up[-1], down[-1], out_q[-1]))
    key_give, key_keep, value_give, value_keep, grad_kv = pl.pallas_call(
        key_value_kernel,
        out_shape=(low(D, half),) * 4 + (low(rows, 2 * D),),
        in_specs=[smem, smem, vmem, vmem, vmem],
        out_specs=(hbm,) * 4 + (vmem,),
        scratch_shapes=[
            pltpu.VMEM((blocks + 1, CLUS, pair_width), F32),
            turned,
            pltpu.VMEM((2, 2, D, half), LOW),
            pltpu.SemaphoreType.DMA((2, 2)),
        ],
        compiler_params=params(),
        name="key_value_kernel",
    )(info, segment, returned, order_rows, tokens)
    key = scatter_start([key_keep, swap(key_give, CORE)], (X, Y))
    value = scatter_start([value_keep, swap(value_give, CORE)], (Y, X))
    early = scatter_end([up, down, out_q], (Z0, Z1), further)
    late = scatter_end([key, value], (Z0, Z1), further)
    grad_proj = jnp.concatenate([grad_q, grad_kv], axis=1)
    grad_tokens = (grad_resid + nt(grad_proj, w_qkv)).astype(LOW)
    early, late, grad_tokens = tie((early, late, grad_tokens))
    wide = ff // 2
    up = early[:, :wide]
    down = early[:, wide : 2 * wide]
    rest = jnp.concatenate([early[:, 2 * wide :], late], axis=1)

    def spread_call(start, route, mine, other, outs):
        count = len(outs)
        return pl.pallas_call(
            partial(spread_kernel, start, route, count),
            out_shape=outs,
            in_specs=[smem, vmem, vmem],
            out_specs=(hbm,) * count,
            scratch_shapes=[
                pltpu.VMEM((2, CHUNKS // 2, D // CHUNKS, mine.shape[1]), F32),
                pltpu.SemaphoreType.DMA,
            ],
            compiler_params=params(),
            cost_estimate=pl.CostEstimate(flops=20_000_000_000, bytes_accessed=20_000_000, transcendentals=0),
            name=route.__name__,
        )(info, mine, other)

    orders = (ORDER_X, ORDER_Y, ORDER_Z)
    mine = gather_rows((up, down, rest), orders)
    last = [swap(value, order[-1]) for value, order in zip(mine, orders)]
    other = [swap(value, CORE) for value in mine]
    outs = []
    for at, (start, route, shapes) in enumerate(
        (
            (17, up_targets, (full(D, ff),)),
            (33, down_targets, (full(ff // D, D, D),)),
            (49, attention_targets, (full(D, D), full(D, 3 * D), full(CHUNKS, 8, LANES))),
        )
    ):
        outs += spread_call(start, route, mine[at], other[at], shapes)
    last_pieces = []
    for value in last:
        last_pieces += [value, swap(value, CORE)]
    sum_up, sum_down, sum_out, sum_qkv, vectors = pl.pallas_call(
        spread_last_kernel,
        out_shape=tuple(full(*out.shape) for out in outs),
        in_specs=[smem] + [hbm] * 11,
        out_specs=(hbm,) * 5,
        scratch_shapes=[pltpu.VMEM(piece.shape, LOW) for piece in last_pieces]
        + [
            pltpu.VMEM((2, CHUNKS // 2, D // CHUNKS, piece.shape[1]), F32)
            for piece in last_pieces[::2]
        ]
        + [
            pltpu.SemaphoreType.DMA((6,)),
            pltpu.SemaphoreType.DMA((3,)),
        ],
        input_output_aliases={7 + at: at for at in range(5)},
        compiler_params=params(),
        name="spread_last",
    )(info, *last_pieces, *outs)
    vectors = vectors[:, : D // LANES].reshape(CHUNKS, D)
    return (
        layer_out,
        grad_tokens,
        sum_qkv,
        vectors[7],
        vectors[6],
        sum_out,
        vectors[5],
        vectors[3],
        vectors[4],
        sum_up,
        vectors[8 : 8 + ff // D].reshape(ff),
        sum_down.reshape(ff, D),
        vectors[2],
        vectors[0],
        vectors[1],
    )


def solution(mesh):
    whole = P()
    rows = P(("dp", "blk"), None)
    return jax.shard_map(
        per_device,
        mesh=mesh,
        in_specs=(
            (rows,)
            + (whole,) * 13
            + (P("dp", None, "blk"), P("dp", None, None, None), rows)
        ),
        out_specs=(rows, rows) + (whole,) * 13,
        check_vma=False,
    )
```

```python
from functools import partial

import jax
import jax.numpy as jnp
from jax import lax
from jax.experimental import pallas as pl
from jax.experimental.pallas import tpu as pltpu
from jax.sharding import PartitionSpec as P

D = 768
HEADS = 12
HEAD_DIM = 64
CLUS = 128
PAIRS = 2
LANES = 128

F32 = jnp.float32
LOW = jnp.bfloat16


def nn(left, right):
    return jnp.dot(left, right, preferred_element_type=F32)


def nt(left, right):
    return lax.dot_general(left, right, (((1,), (1,)), ((), ())), preferred_element_type=F32)


def tn(left, right):
    return lax.dot_general(left, right, (((0,), (0,)), ((), ())), preferred_element_type=F32)


def as_row(vector):
    return vector[...].astype(F32).reshape(1, vector.shape[0])


def left_half(shape):
    return lax.broadcasted_iota(jnp.int32, shape, 1) < HEAD_DIM


def pick(hot):
    return jnp.where(hot, 1.0, 0.0).astype(LOW)


def params(megabytes=60):
    return pltpu.CompilerParams(vmem_limit_bytes=megabytes << 20)


def columns_of(perm, rows):
    local = lax.rem(perm, rows)
    return jnp.concatenate([local, local[: 16 - HEADS]]).T


def kv_kernel(tok, w_key, w_value, b_value, perm, chosen_in, out, blocks, chosen, chosen_sem, sem):
    fetch = pltpu.make_async_copy(chosen_in, chosen, chosen_sem)
    fetch.start()
    rows = tok.shape[0]
    order = columns_of(perm[0], rows)
    per_dev = rows // CLUS
    place = lax.broadcasted_iota(jnp.int32, (rows, rows), 1)
    left = left_half((rows, 2 * HEAD_DIM))
    inputs = tok[...]
    keys = nn(inputs, w_key[...])
    values = nn(inputs, w_value[...]) + as_row(b_value)
    joined = []
    for pair in range(HEADS // 2):
        two = slice(pair * 2 * HEAD_DIM, (pair + 1) * 2 * HEAD_DIM)
        key_two = keys[:, two]
        value_two = pltpu.roll(values[:, two], HEAD_DIM, 1)
        joined.append(jnp.where(left, key_two, value_two).astype(LOW))
        joined.append(jnp.where(left, value_two, key_two).astype(LOW))
    for quad in range(HEADS // 4):
        heads = range(quad * 4, quad * 4 + 4)
        hot = [pick(order[:, head : head + 1] == place) for head in heads]
        ranked = [nn(one, joined[head]).astype(LOW) for one, head in zip(hot, heads)]
        for head, value in zip(heads, ranked):
            blocks[head * per_dev : (head + 1) * per_dev] = value.reshape(per_dev, CLUS, 2 * HEAD_DIM)
    fetch.wait()
    devices, capacity = chosen.shape

    @pl.loop(0, devices)
    def _(device):
        for slot in range(capacity):
            pltpu.make_async_copy(
                blocks.at[chosen[device, slot]], out.at[device * capacity + slot], sem
            ).start()

    pltpu.make_async_copy(out, out, sem).wait()


def q_kernel(tok, w_query, b_query, perm, out):
    rows = tok.shape[0]
    order = columns_of(perm[0], rows)
    place = lax.broadcasted_iota(jnp.int32, (rows, rows), 1)
    left = left_half((rows, 2 * HEAD_DIM))
    inputs = tok[...]
    for quad in range(HEADS // 4):
        four = slice(quad * 4 * HEAD_DIM, (quad + 1) * 4 * HEAD_DIM)
        queries = nn(inputs, w_query[:, four]) + as_row(b_query)[:, four]
        queries = (queries.astype(LOW).astype(F32) * HEAD_DIM ** (-0.5)).astype(LOW)
        for pair in range(2):
            two = queries[:, pair * 2 * HEAD_DIM : (pair + 1) * 2 * HEAD_DIM]
            for odd in range(2):
                head = quad * 4 + pair * 2 + odd
                hot = pick(order[:, head : head + 1] == place)
                ranked = nn(hot, two)
                kept = jnp.where(left, 0.0, ranked) if odd else jnp.where(left, ranked, 0.0)
                out[head] = kept.astype(LOW)


ROW_TILE = 512
WIDE = 768
WIDE_FORTH = 1024
WIDE_BACK = 1536


def mid_kernel(
    fetch, queries, arrived, order, inverse, tok, cot,
    b_out, gain_one, shift_one, b_up, b_down, gain_two, shift_two, w_out_hbm, w_up_hbm, w_down_hbm,
    back, dq_out, attn_out, z_out, active_out, du_out, df_out, db_out, dh1_out, layer_out, sums,
    kv, probs, attn, mixed, w_out, w_up, w_down, hidden, z_full, n_one, r_one, z_low, active, slope,
    dh2, df, db, d_out, dh1, final, dq, kv_sem, w_sem, out_sem, back_sem,
):
    rows = tok.shape[0]
    per_dev = rows // CLUS
    pair_width = 2 * HEAD_DIM
    requests = fetch.shape[0]
    each = 2 * per_dev * PAIRS
    width = w_up.shape[1]
    tiles = rows // ROW_TILE
    left = left_half((CLUS, pair_width))
    left_rows = left_half((rows, pair_width))
    down = lax.broadcasted_iota(jnp.int32, (rows, rows), 0)

    @pl.loop(0, HEADS // 2)
    def _(group):
        for step in range(each):
            entry = group * each + step
            pltpu.make_async_copy(arrived.at[fetch[entry]], kv.at[entry], kv_sem.at[group]).start()

    loads = [
        pltpu.make_async_copy(source, target, w_sem.at[at])
        for at, (source, target) in enumerate(
            ((w_out_hbm, w_out), (w_up_hbm, w_up), (w_down_hbm, w_down))
        )
    ]
    for load in loads:
        load.start()
    stores = []

    def store(source, target):
        copy = pltpu.make_async_copy(source, target, out_sem.at[len(stores)])
        copy.start()
        stores.append(copy)

    @pl.loop(0, HEADS // 2)
    def _(group):
        span = kv.at[pl.ds(group * each, each)]
        pltpu.make_async_copy(span, span, kv_sem.at[group]).wait()
        units = [(odd, cluster) for odd in range(2) for cluster in range(per_dev)]
        clusters = [slice(cluster * CLUS, (cluster + 1) * CLUS) for cluster in range(per_dev)]
        index = [(2 * group + odd) * per_dev + cluster for odd, cluster in units]
        pair = [kv[pl.ds(unit * PAIRS, PAIRS)].reshape(PAIRS * CLUS, pair_width) for unit in index]
        scores = [
            nt(queries[2 * group + odd, clusters[cluster], :], both)
            for (odd, cluster), both in zip(units, pair)
        ]
        exponent = [jnp.exp(value - jnp.max(value, -1, keepdims=True)) for value in scores]
        low = [(value / jnp.sum(value, -1, keepdims=True)).astype(LOW) for value in exponent]
        for (odd, cluster), unit, value, both in zip(units, index, low, pair):
            probs[unit] = value
            value = nn(value, both)
            mixed[odd, clusters[cluster], :] = (
                jnp.where(left, value, 0.0) if odd else jnp.where(left, 0.0, value)
            ).astype(LOW)
        hot = jnp.concatenate([pick(down == order[2 * group + odd]) for odd in range(2)], axis=1)
        both = pltpu.roll(nn(hot, mixed[...].reshape(2 * rows, pair_width)), HEAD_DIM, 1)
        attn[:, pl.ds(pl.multiple_of(group * pair_width, pair_width), pair_width)] = both.astype(LOW)

    store(attn, attn_out)
    loads[0].wait()
    hidden[...] = nn(attn[...], w_out[...])

    @pl.loop(0, tiles)
    def _(tile):
        at = pl.ds(pl.multiple_of(tile * ROW_TILE, ROW_TILE), ROW_TILE)
        value = hidden[at, :] + (as_row(b_out) + tok[at, :].astype(F32))
        centred = value - jnp.mean(value, -1, keepdims=True)
        scale = lax.rsqrt(jnp.mean(centred * centred, -1, keepdims=True) + 1e-06)
        unit = centred * scale
        z = unit * as_row(gain_one) + as_row(shift_one)
        n_one[at, :] = unit
        r_one[at, :] = scale
        z_low[at, :] = z.astype(LOW)
        z_full[at, :] = z
        hidden[at, :] = z + as_row(b_down)

    store(z_low, z_out)
    loads[1].wait()
    loads[2].wait()

    @pl.loop(0, width // WIDE_FORTH)
    def _(step):
        at = pl.ds(pl.multiple_of(step * WIDE_FORTH, WIDE_FORTH), WIDE_FORTH)
        inner = nn(z_low[...], w_up[:, at]) + b_up[at].astype(F32).reshape(1, WIDE_FORTH)
        normal = 0.5 * (1.0 + lax.erf(inner * 0.7071067811865476))
        density = jnp.exp(inner * inner * -0.5) * 0.3989422804014327
        active[:, at] = (inner * normal).astype(LOW)
        slope[:, at] = (normal + inner * density).astype(LOW)
        hidden[...] += nn(active[:, at], w_down[at, :])

    store(active, active_out)
    sums[...] = jnp.zeros_like(sums)

    @pl.loop(0, tiles)
    def _(tile):
        at = pl.ds(pl.multiple_of(tile * ROW_TILE, ROW_TILE), ROW_TILE)
        value = hidden[at, :]
        centred = value - jnp.mean(value, -1, keepdims=True)
        scale = lax.rsqrt(jnp.mean(centred * centred, -1, keepdims=True) + 1e-06)
        unit = centred * scale
        final[at, :] = (unit * as_row(gain_two) + as_row(shift_two)).astype(LOW)
        grad = cot[at, :].astype(F32)
        lifted = grad * as_row(gain_two)
        back_grad = scale * (
            lifted - jnp.mean(lifted, -1, keepdims=True) - unit * jnp.mean(lifted * unit, -1, keepdims=True)
        )
        dh2[at, :] = back_grad
        low = back_grad.astype(LOW)
        df[at, :] = low
        sums[0:1, :] += jnp.sum(grad * unit, axis=0, keepdims=True)
        sums[1:2, :] += jnp.sum(grad, axis=0, keepdims=True)
        sums[2:3, :] += jnp.sum(low.astype(F32), axis=0, keepdims=True)

    store(final, layer_out)
    store(df, df_out)
    ones = jnp.ones((8, rows), LOW)

    @pl.loop(0, width // WIDE_BACK)
    def _(step):
        at = pl.ds(pl.multiple_of(step * WIDE_BACK, WIDE_BACK), WIDE_BACK)
        grad = (nt(df[...], w_down[at, :]) * slope[:, at].astype(F32)).astype(LOW)
        slope[:, at] = grad
        total = nn(ones, grad)
        for part in range(WIDE_BACK // D):
            row = 8 + step * (WIDE_BACK // D) + part
            sums[pl.ds(row, 1), :] = total[0:1, part * D : (part + 1) * D]
        dh2[...] += nt(slope[:, at], w_up[:, at])

    store(slope, du_out)

    @pl.loop(0, tiles)
    def _(tile):
        at = pl.ds(pl.multiple_of(tile * ROW_TILE, ROW_TILE), ROW_TILE)
        grad = dh2[at, :]
        unit = n_one[at, :]
        lifted = grad * as_row(gain_one)
        back_grad = r_one[at, :] * (
            lifted - jnp.mean(lifted, -1, keepdims=True) - unit * jnp.mean(lifted * unit, -1, keepdims=True)
        )
        dh1[at, :] = back_grad
        low = back_grad.astype(LOW)
        db[at, :] = low
        sums[3:4, :] += jnp.sum(grad * unit, axis=0, keepdims=True)
        sums[4:5, :] += jnp.sum(grad, axis=0, keepdims=True)
        sums[5:6, :] += jnp.sum(low.astype(F32), axis=0, keepdims=True)

    store(dh1, dh1_out)
    store(db, db_out)
    d_out[...] = nt(db[...], w_out[...]).astype(LOW)

    @pl.loop(0, HEADS // 2)
    def _(group):
        lanes = pl.ds(pl.multiple_of(group * pair_width, pair_width), pair_width)
        tile = d_out[:, lanes]
        grads = []
        for odd in range(2):
            turned = pltpu.roll(nn(pick(down == inverse[2 * group + odd]), tile), HEAD_DIM, 1)
            grads.append((jnp.where(left_rows, turned, 0.0) if odd else jnp.where(left_rows, 0.0, turned)).astype(LOW))
        units = [(odd, cluster) for odd in range(2) for cluster in range(per_dev)]
        clusters = [slice(cluster * CLUS, (cluster + 1) * CLUS) for cluster in range(per_dev)]
        index = [(2 * group + odd) * per_dev + cluster for odd, cluster in units]
        grad = [grads[odd][clusters[cluster]] for odd, cluster in units]
        query = [queries[2 * group + odd, clusters[cluster], :] for odd, cluster in units]
        pair = [kv[pl.ds(unit * PAIRS, PAIRS)].reshape(PAIRS * CLUS, pair_width) for unit in index]
        low = [probs[unit] for unit in index]
        d_probs = [nt(left_, right) for left_, right in zip(grad, pair)]
        wide = [value.astype(F32) for value in low]
        d_scores = [
            (value * (grad_ - jnp.sum(grad_ * value, -1, keepdims=True))).astype(LOW)
            for value, grad_ in zip(wide, d_probs)
        ]
        d_query = [nn(left_, right) * HEAD_DIM ** (-0.5) for left_, right in zip(d_scores, pair)]
        d_pair = [tn(a, b) + tn(c, d) for a, b, c, d in zip(d_scores, query, low, grad)]
        bias = [jnp.zeros((1, pair_width), F32)] * 2
        q_total = jnp.zeros((1, pair_width), F32)
        for (odd, cluster), unit, value, both in zip(units, index, d_query, d_pair):
            value = (jnp.where(left, 0.0, value) if odd else jnp.where(left, value, 0.0)).astype(LOW)
            dq[2 * group + odd, clusters[cluster], :] = value
            q_total += jnp.sum(value.astype(F32), axis=0, keepdims=True)
            bias[odd] += jnp.sum(both, axis=0, keepdims=True)
            kv[pl.ds(unit * PAIRS, PAIRS)] = both.astype(LOW).reshape(PAIRS, CLUS, pair_width)
        for step in range(each):
            entry = group * each + step
            pltpu.make_async_copy(kv.at[entry], back.at[fetch[entry]], back_sem).start()
        both = jnp.where(left_half((1, pair_width)), bias[1], bias[0])
        sums[7:8, lanes] = q_total
        sums[6:7, lanes] = pltpu.roll(jnp.broadcast_to(both, (8, pair_width)), HEAD_DIM, 1)[0:1]

    store(dq, dq_out)
    span = back.at[pl.ds(0, requests)]
    pltpu.make_async_copy(kv, span, back_sem).wait()
    for copy in stores:
        copy.wait()


CHUNKS = 16


def chunk_rows(at, size):
    return pl.ds(pl.multiple_of(at * size, size), size)


def place_chunks(source, target, info, sem, start=1):
    size = source.shape[0] // CHUNKS
    for chunk in range(CHUNKS):
        pltpu.make_async_copy(
            source.at[chunk * size : (chunk + 1) * size],
            target.at[chunk_rows(info[start + chunk], size)],
            sem,
        ).start()


def wait_chunks(source, target, sem):
    pltpu.make_async_copy(source, target, sem).wait()


def core_of(info, side):
    return info[0] if side else 1 - info[0]


def up_kernel(info, z_low, grad, give, keep, turned, buf, sem):
    half = keep.shape[1]
    turned[...] = z_low[...].T
    for side, out in ((0, give), (1, keep)):
        at = pl.ds(pl.multiple_of(core_of(info, side) * half, half), half)
        buf[side] = nn(turned[...], grad[:, at]).astype(LOW)
        place_chunks(buf.at[side], out, info, sem.at[side])
    for side, out in ((0, give), (1, keep)):
        wait_chunks(buf.at[side], out, sem.at[side])


def down_kernel(info, active, grad, give, keep, buf, sem):
    size = keep.shape[0]
    for side, out in ((0, give), (1, keep)):
        for part in range(keep.shape[1] // size):
            block = core_of(info, side) * (keep.shape[1] // size) + part
            at = pl.ds(pl.multiple_of(block * size, size), size)
            buf[side, :, part * size : (part + 1) * size] = nn(active[:, at].T, grad[...]).astype(LOW)
        place_chunks(buf.at[side], out, info, sem.at[side])
    for side, out in ((0, give), (1, keep)):
        wait_chunks(buf.at[side], out, sem.at[side])


def out_q_kernel(info, attn, db, tok, dq, order, sums, give, keep, grad_q, attn_t, tok_t, buf, sem):
    rows = tok.shape[0]
    half = D // 2
    down = lax.broadcasted_iota(jnp.int32, (rows, rows), 0)
    for pair in range(HEADS // 2):
        total = nn(pick(down == order[2 * pair]), dq[2 * pair])
        total += nn(pick(down == order[2 * pair + 1]), dq[2 * pair + 1])
        lanes = slice(pair * 2 * HEAD_DIM, (pair + 1) * 2 * HEAD_DIM)
        grad_q[:, lanes] = total.astype(LOW)
    attn_t[...] = attn[...].T
    tok_t[...] = tok[...].T
    size = D // CHUNKS
    filler = jnp.zeros((size - D // LANES, LANES), F32)
    for vector in range(CHUNKS):
        rows_of = [sums[vector : vector + 1, row * LANES : (row + 1) * LANES] for row in range(D // LANES)]
        value = jnp.concatenate(rows_of + [filler]).astype(LOW)
        for side in range(2):
            buf[side, vector * size : (vector + 1) * size, D:] = value
    for side, out in ((0, give), (1, keep)):
        at = pl.ds(pl.multiple_of(core_of(info, side) * half, half), half)
        buf[side, :, :half] = nn(attn_t[...], db[:, at]).astype(LOW)
        buf[side, :, half:D] = nn(tok_t[...], grad_q[:, at]).astype(LOW)
        place_chunks(buf.at[side], out, info, sem.at[side], 65)
    for side, out in ((0, give), (1, keep)):
        wait_chunks(buf.at[side], out, sem.at[side])


def key_value_kernel(
    info, segment, returned, order, tok, key_give, key_keep, value_give, value_keep, grad_kv, total, tok_t, buf, sem
):
    rows = tok.shape[0]
    half = D // 2
    per_dev = rows // CLUS
    pair_width = 2 * HEAD_DIM
    down = lax.broadcasted_iota(jnp.int32, (rows, rows), 0)
    left = left_half((rows, pair_width))
    total[...] = jnp.zeros_like(total)

    @pl.loop(0, segment.shape[0], unroll=4)
    def _(slot):
        block = segment[slot]
        total[block] += returned[slot].astype(F32)

    for quad in range(HEADS // 4):
        pairs = range(2 * quad, 2 * quad + 2)
        heads = range(4 * quad, 4 * quad + 4)
        hots = [pick(down == order[head]) for head in heads]
        summed = [
            total[head * per_dev : (head + 1) * per_dev].reshape(rows, pair_width).astype(LOW) for head in heads
        ]
        placed = [nn(hot, value) for hot, value in zip(hots, summed)]
        for at, pair in enumerate(pairs):
            even, odd = placed[2 * at], placed[2 * at + 1]
            grad_kv[:, pair * pair_width : (pair + 1) * pair_width] = jnp.where(left, even, odd).astype(LOW)
            values = pltpu.roll(jnp.where(left, odd, even), HEAD_DIM, 1)
            grad_kv[:, D + pair * pair_width : D + (pair + 1) * pair_width] = values.astype(LOW)
    tok_t[...] = tok[...].T
    outs = ((key_give, key_keep), (value_give, value_keep))
    for side in range(2):
        base = core_of(info, side) * half
        for part in range(2):
            at = pl.ds(pl.multiple_of(part * D + base, half), half)
            buf[part, side] = nn(tok_t[...], grad_kv[:, at]).astype(LOW)
            place_chunks(buf.at[part, side], outs[part][side], info, sem.at[part, side], 65 if part else 1)
    for side in range(2):
        for part in range(2):
            wait_chunks(buf.at[part, side], outs[part][side], sem.at[part, side])


def spread_start(info, start, pieces, targets, buf, sem):
    size = buf.shape[2]
    copies = []
    for at, piece in enumerate(pieces):
        core = core_of(info, 1 - at)
        for chunk in range(CHUNKS // 2):
            buf[at, chunk] = piece[chunk * size : (chunk + 1) * size].astype(F32)
            for lanes, target in targets(core, info[start + chunk], size, at == 0):
                copies.append(pltpu.make_async_copy(buf.at[at, chunk, : target.shape[0], lanes], target, sem))
                copies[-1].start()
    return copies


def spread(info, start, pieces, targets, buf, sem):
    for copy in spread_start(info, start, pieces, targets, buf, sem):
        copy.wait()


def up_targets(out, half):
    def targets(core, chunk, size, mine):
        rows = chunk_rows(chunk, size)
        yield pl.ds(0, half), out.at[rows, pl.ds(pl.multiple_of(core * half, half), half)]

    return targets


def down_targets(out, half):
    parts = half // D

    def targets(core, chunk, size, mine):
        rows = chunk_rows(chunk, size)
        for part in range(parts):
            yield pl.ds(part * D, D), out.at[core * parts + part, rows]

    return targets


def attention_targets(w_out, w_qkv, vectors, wide):
    half = D // 2

    def targets(core, chunk, size, mine):
        rows = chunk_rows(chunk, size)
        at = pl.ds(pl.multiple_of(core * half, half), half)
        yield pl.ds(0, half), w_out.at[rows, at]
        for part, lane in enumerate((half, D + LANES, D + LANES + half)):
            to = pl.ds(pl.multiple_of(part * D + core * half, half), half)
            yield pl.ds(lane, half), w_qkv.at[rows, to]
        if mine:
            yield pl.ds(D, LANES), vectors.at[chunk]

    return targets


def spread_kernel(start, route, count, info, mine, other, *refs):
    buf, sem = refs[-2:]
    spread(info, start, (mine, other), route(*refs[:count], mine.shape[1]), buf, sem)


def spread_last_kernel(info, *refs):
    pieces, outs, staged, bufs = refs[:6], refs[11:16], refs[16:22], refs[22:25]
    load_sem, sem = refs[25:]
    w_up, w_down, w_out, w_qkv, vectors = outs
    half = w_up.shape[1] // 2
    loads = []
    for at, (source, target) in enumerate(zip(pieces, staged)):
        loads.append(pltpu.make_async_copy(source, target, load_sem.at[at]))
        loads[-1].start()
    routes = (up_targets(w_up, half), down_targets(w_down, half), attention_targets(w_out, w_qkv, vectors, half))
    copies = []
    for at, (start, targets) in enumerate(zip((25, 41, 57), routes)):
        for load in loads[2 * at : 2 * at + 2]:
            load.wait()
        copies += spread_start(info, start, staged[2 * at : 2 * at + 2], targets, bufs[at], sem.at[at])
    for copy in copies:
        copy.wait()


X, Y, Z0, Z1 = ("dp", 1), ("blk", 2), ("blk", 4), ("blk", 8)
CORE = ("blk", 1)


def swap(value, bit):
    axis, distance = bit
    size = lax.axis_size(axis)
    return lax.ppermute(value, axis, [(i, i ^ distance) for i in range(size)])


def further_bits(count_blk):
    bits = []
    distance = 16
    while distance < count_blk:
        bits.append(("blk", distance))
        distance *= 2
    return bits


def chip_bits():
    return [(lax.axis_index(axis) // distance) % 2 for axis, distance in (X, Y, Z0, Z1)]


def chunk_places():
    x, y, z0, z1 = chip_bits()
    chip = x * 8 + y * 4 + z0 * 2 + z1
    core = lax.axis_index("blk") % 2
    every = jnp.arange(CHUNKS, dtype=jnp.int32)
    value = {X: 8, Y: 4, Z0: 2, Z1: 1}

    def from_order(order):
        at = sum(((every // 2**step) % 2) * value[bit] for step, bit in enumerate(order))
        return at ^ chip

    placed = every ^ chip
    x_y_swapped = placed % 4 + (placed // 8) * 4 + (placed // 4 % 2) * 8
    return jnp.concatenate(
        [core[None], placed]
        + [from_order(order) for order in (ORDER_X, ORDER_Y, ORDER_Z)]
        + [x_y_swapped]
    )


ORDER_X = (Z1, Z0, Y, X)
ORDER_Y = (Z1, X, Z0, Y)
ORDER_Z = (Z1, Y, X, Z0)


def sum_rows(terms, low, high):
    total = terms[0][low:high].astype(F32)
    for term in terms[1:]:
        total = total + term[low:high].astype(F32)
    return total


def to_send(terms):
    rows = min(term.shape[0] for term in terms)
    return sum_rows(terms, rows // 2, rows).astype(LOW)


def scatter_steps(terms, bits):
    for bit in bits:
        terms = terms + [swap(to_send(terms), bit)]
    return terms


def finish(terms, further):
    value = sum_rows(terms, 0, terms[-1].shape[0]).astype(LOW)
    for bit in further:
        value = sum_rows([value, swap(value, bit)], 0, value.shape[0]).astype(LOW)
    return value


def tie(values):
    return lax.optimization_barrier(tuple(values))


def gather_step(value, bit):
    return jnp.concatenate([value, swap(value, bit)])


def per_device(
    tokens,
    w_qkv,
    b_query,
    b_value,
    w_out,
    b_out,
    gain_one,
    shift_one,
    w_up,
    b_up,
    w_down,
    b_down,
    gain_two,
    shift_two,
    cluster_perm,
    cluster_pairs,
    cotangent,
):
    count_blk = lax.axis_size("blk")
    my_index = lax.axis_index("blk")
    rows = tokens.shape[0]
    per_dev = rows // CLUS
    blocks = HEADS * per_dev
    requests = blocks * PAIRS
    capacity = max(2, (requests + count_blk - 1) // count_blk + 1)
    slots = count_blk * capacity
    pair_width = 2 * HEAD_DIM
    ff = w_up.shape[1]
    local_order = cluster_perm[0] - my_index * rows
    order_rows = local_order[:, None, :]

    wanted = (
        cluster_pairs[0]
        .reshape(HEADS, count_blk, per_dev, PAIRS)
        .transpose(1, 0, 2, 3)
        .reshape(count_blk, requests)
    )
    positions = jnp.arange(requests, dtype=jnp.int32)
    before = positions[:, None] < positions[None, :]
    source = wanted // per_dev
    named = source == my_index
    rank = jnp.sum(named[:, :, None] & before[None], axis=1)
    head_of = positions // (per_dev * PAIRS)
    block_id = head_of[None, :] * per_dev + wanted % per_dev
    matches = named[:, :, None] & (
        rank[:, :, None] == jnp.arange(capacity, dtype=jnp.int32)[None, None, :]
    )
    chosen = jnp.sum(jnp.where(matches, block_id[:, :, None], 0), axis=1)

    smem = pl.BlockSpec(memory_space=pltpu.SMEM)
    vmem = pl.BlockSpec(memory_space=pltpu.VMEM)
    hbm = pl.BlockSpec(memory_space=pl.ANY)

    def column_block(at):
        return pl.BlockSpec((D, D), lambda step: (0, at))

    outgoing = pl.pallas_call(
        kv_kernel,
        grid=(1,),
        out_shape=jax.ShapeDtypeStruct((slots, CLUS, pair_width), LOW),
        in_specs=[vmem, column_block(1), column_block(2), vmem, vmem, vmem],
        out_specs=hbm,
        scratch_shapes=[
            pltpu.VMEM((blocks, CLUS, pair_width), LOW),
            pltpu.SMEM(chosen.shape, jnp.int32),
            pltpu.SemaphoreType.DMA,
            pltpu.SemaphoreType.DMA,
        ],
        compiler_params=params(),
        name="kv_kernel",
    )(tokens, w_qkv, w_qkv, b_value, cluster_perm, chosen)
    arrived = lax.all_to_all(
        outgoing.reshape(count_blk, capacity, CLUS, pair_width),
        "blk",
        split_axis=0,
        concat_axis=0,
        tiled=True,
    ).reshape(slots, CLUS, pair_width)

    info = chunk_places()
    queries = pl.pallas_call(
        q_kernel,
        grid=(1,),
        out_shape=jax.ShapeDtypeStruct((HEADS, rows, pair_width), LOW),
        in_specs=[vmem, column_block(0), vmem, vmem],
        out_specs=vmem,
        compiler_params=params(),
        name="q_kernel",
    )(tokens, w_qkv, b_query, cluster_perm)
    filled = jnp.any(matches, axis=1)
    segment = jnp.where(filled, chosen, blocks).reshape(-1)
    my_source = lax.dynamic_index_in_dim(wanted, my_index, 0, keepdims=False) // per_dev
    my_rank = jnp.sum((my_source[:, None] == my_source[None, :]) & before, axis=0)
    fetch = my_source * capacity + my_rank
    places = jnp.arange(rows, dtype=jnp.int32)
    inverse = jnp.sum(
        jnp.where(local_order[:, :, None] == places, places[None, :, None], 0), axis=1
    )[:, None, :]
    def low(*shape):
        return jax.ShapeDtypeStruct(shape, LOW)

    def full(*shape):
        return jax.ShapeDtypeStruct(shape, F32)

    (
        back, dq_sorted, attn, normed, active, grad_inner, grad_second, grad_branch, grad_resid,
        layer_out, sums,
    ) = pl.pallas_call(
        mid_kernel,
        out_shape=(
            low(slots, CLUS, pair_width), low(HEADS, rows, pair_width), low(rows, D), low(rows, D),
            low(rows, ff), low(rows, ff), low(rows, D), low(rows, D), full(rows, D), low(rows, D),
            full(16, D),
        ),
        in_specs=[smem, vmem, hbm] + [vmem] * 11 + [hbm] * 3,
        out_specs=(hbm,) * 10 + (vmem,),
        scratch_shapes=[
            pltpu.VMEM((requests, CLUS, pair_width), LOW),
            pltpu.VMEM((blocks, CLUS, PAIRS * CLUS), LOW),
            pltpu.VMEM((rows, D), LOW),
            pltpu.VMEM((2, rows, pair_width), LOW),
            pltpu.VMEM((D, D), LOW),
            pltpu.VMEM((D, ff), LOW),
            pltpu.VMEM((ff, D), LOW),
            pltpu.VMEM((rows, D), F32),
            pltpu.VMEM((rows, D), F32),
            pltpu.VMEM((rows, D), F32),
            pltpu.VMEM((rows, 1), F32),
            pltpu.VMEM((rows, D), LOW),
            pltpu.VMEM((rows, ff), LOW),
            pltpu.VMEM((rows, ff), LOW),
            pltpu.VMEM((rows, D), F32),
            pltpu.VMEM((rows, D), LOW),
            pltpu.VMEM((rows, D), LOW),
            pltpu.VMEM((rows, D), LOW),
            pltpu.VMEM((rows, D), F32),
            pltpu.VMEM((rows, D), LOW),
            pltpu.VMEM((HEADS, rows, pair_width), LOW),
            pltpu.SemaphoreType.DMA((HEADS // 2,)),
            pltpu.SemaphoreType.DMA((3,)),
            pltpu.SemaphoreType.DMA((9,)),
            pltpu.SemaphoreType.DMA,
        ],
        compiler_params=params(),
        name="mid_kernel",
    )(
        fetch, queries, arrived, order_rows, inverse, tokens, cotangent,
        b_out, gain_one, shift_one, b_up, b_down, gain_two, shift_two, w_out, w_up, w_down,
    )
    returned = lax.all_to_all(
        back.reshape(count_blk, capacity, CLUS, pair_width),
        "blk",
        split_axis=0,
        concat_axis=0,
        tiled=True,
    ).reshape(slots, CLUS, pair_width)

    further = further_bits(count_blk)

    def halves(kernel, operands, columns, scratch, more=(), name=None):
        return pl.pallas_call(
            kernel,
            out_shape=(low(D, columns), low(D, columns)) + more,
            in_specs=[smem] + [vmem] * (len(operands) - 1),
            out_specs=(hbm, hbm) + (vmem,) * len(more),
            scratch_shapes=scratch
            + [pltpu.VMEM((2, D, columns), LOW), pltpu.SemaphoreType.DMA((2,))],
            compiler_params=params(),
            cost_estimate=pl.CostEstimate(flops=1, bytes_accessed=1, transcendentals=0),
            name=name,
        )(*operands)

    half = D // 2
    turned = pltpu.VMEM((D, rows), LOW)
    up_give, up_keep = halves(
        up_kernel, (info, normed, grad_inner), ff // 2, [turned], name="up_kernel"
    )
    down_give, down_keep = halves(
        down_kernel, (info, active, grad_second), ff // 2, [], name="down_kernel"
    )
    oq_give, oq_keep, grad_q = halves(
        out_q_kernel,
        (info, attn, grad_branch, tokens, dq_sorted, order_rows, sums),
        D + LANES,
        [turned, turned],
        (low(rows, D),),
        name="out_q_kernel",
    )
    up = scatter_steps([up_keep, swap(up_give, CORE)], (X, Y))
    down = scatter_steps([down_keep, swap(down_give, CORE)], (X,))
    out_q = scatter_steps([oq_keep, swap(oq_give, CORE)], (Y, X))
    up_step = to_send(up)
    up_step, down[-1] = tie((up_step, down[-1]))
    down_step = to_send(down)

    returned, up_step, down_step, out_q[-1] = tie((returned, up_step, down_step, out_q[-1]))
    up = up + [swap(up_step, Z0)]
    down = down + [swap(down_step, Y)]
    key_give, key_keep, value_give, value_keep, grad_kv = pl.pallas_call(
        key_value_kernel,
        out_shape=(low(D, half),) * 4 + (low(rows, 2 * D),),
        in_specs=[smem, smem, vmem, vmem, vmem],
        out_specs=(hbm,) * 4 + (vmem,),
        scratch_shapes=[
            pltpu.VMEM((blocks + 1, CLUS, pair_width), F32),
            turned,
            pltpu.VMEM((2, 2, D, half), LOW),
            pltpu.SemaphoreType.DMA((2, 2)),
        ],
        compiler_params=params(),
        name="key_value_kernel",
    )(info, segment, returned, order_rows, tokens)
    down[-1], key_give, value_give = tie((down[-1], key_give, value_give))
    key = scatter_steps([key_keep, swap(key_give, CORE)], (X, Y))
    value = scatter_steps([value_keep, swap(value_give, CORE)], (Y, X))
    up = finish(scatter_steps(up, (Z1,)), further)
    down = finish(scatter_steps(down, (Z0, Z1)), further)
    out_q = finish(scatter_steps(out_q, (Z0, Z1)), further)
    late_given = swap(jnp.concatenate([to_send(key), to_send(value)], axis=1), Z0)
    key = key + [late_given[:, :half]]
    value = value + [late_given[:, half:]]
    late_given = swap(jnp.concatenate([to_send(key), to_send(value)], axis=1), Z1)
    key = finish(key + [late_given[:, :half]], further)
    value = finish(value + [late_given[:, half:]], further)
    thirds = [
        gather_step(third, Z1)
        for third in (
            up,
            down,
            jnp.concatenate([out_q, key, value], axis=1),
        )
    ]

    def spread_call(start, route, mine, other, outs):
        count = len(outs)
        return pl.pallas_call(
            partial(spread_kernel, start, route, count),
            out_shape=outs,
            in_specs=[smem, vmem, vmem],
            out_specs=(hbm,) * count,
            scratch_shapes=[
                pltpu.VMEM((2, CHUNKS // 2, D // CHUNKS, mine.shape[1]), F32),
                pltpu.SemaphoreType.DMA,
            ],
            compiler_params=params(),
            cost_estimate=pl.CostEstimate(flops=20_000_000_000, bytes_accessed=20_000_000, transcendentals=0),
            name=route.__name__,
        )(info, mine, other)

    orders = (ORDER_X, ORDER_Y, ORDER_Z)
    for step in (1, 2):
        thirds = tie(gather_step(value, order[step]) for value, order in zip(thirds, orders))
    grad_kv, *thirds = tie((grad_kv, *thirds))
    grad_proj = jnp.concatenate([grad_q, grad_kv], axis=1)
    grad_tokens = (grad_resid + nt(grad_proj, w_qkv)).astype(LOW)
    last = [swap(value, order[-1]) for value, order in zip(thirds, orders)]
    other = [swap(value, CORE) for value in thirds]
    outs = []
    for at, (start, route, shapes) in enumerate(
        (
            (17, up_targets, (full(D, ff),)),
            (33, down_targets, (full(ff // D, D, D),)),
            (49, attention_targets, (full(D, D), full(D, 3 * D), full(CHUNKS, 8, LANES))),
        )
    ):
        outs += spread_call(start, route, thirds[at], other[at], shapes)
    tied = tie((*last, *outs))
    last, outs = tied[: len(last)], tied[len(last) :]
    last_pieces = []
    for value in last:
        last_pieces += [value, swap(value, CORE)]
    sum_up, sum_down, sum_out, sum_qkv, vectors = pl.pallas_call(
        spread_last_kernel,
        out_shape=tuple(full(*out.shape) for out in outs),
        in_specs=[smem] + [hbm] * 11,
        out_specs=(hbm,) * 5,
        scratch_shapes=[pltpu.VMEM(piece.shape, LOW) for piece in last_pieces]
        + [
            pltpu.VMEM((2, CHUNKS // 2, D // CHUNKS, piece.shape[1]), F32)
            for piece in last_pieces[::2]
        ]
        + [
            pltpu.SemaphoreType.DMA((6,)),
            pltpu.SemaphoreType.DMA((3,)),
        ],
        input_output_aliases={7 + at: at for at in range(5)},
        compiler_params=params(),
        name="spread_last",
    )(info, *last_pieces, *outs)
    vectors = vectors[:, : D // LANES].reshape(CHUNKS, D)
    return (
        layer_out,
        grad_tokens,
        sum_qkv,
        vectors[7],
        vectors[6],
        sum_out,
        vectors[5],
        vectors[3],
        vectors[4],
        sum_up,
        vectors[8 : 8 + ff // D].reshape(ff),
        sum_down.reshape(ff, D),
        vectors[2],
        vectors[0],
        vectors[1],
    )


def solution(mesh):
    whole = P()
    rows = P(("dp", "blk"), None)
    return jax.shard_map(
        per_device,
        mesh=mesh,
        in_specs=(
            (rows,)
            + (whole,) * 13
            + (P("dp", None, "blk"), P("dp", None, None, None), rows)
        ),
        out_specs=(rows, rows) + (whole,) * 13,
        check_vma=False,
    )
```

```python
from functools import partial

import jax
import jax.numpy as jnp
from jax import lax
from jax.experimental import pallas as pl
from jax.experimental.pallas import tpu as pltpu
from jax.sharding import PartitionSpec as P

D = 768
HEADS = 12
HEAD_DIM = 64
CLUS = 128
PAIRS = 2
LANES = 128

F32 = jnp.float32
LOW = jnp.bfloat16


def nn(left, right):
    return jnp.dot(left, right, preferred_element_type=F32)


def nt(left, right):
    return lax.dot_general(left, right, (((1,), (1,)), ((), ())), preferred_element_type=F32)


def tn(left, right):
    return lax.dot_general(left, right, (((0,), (0,)), ((), ())), preferred_element_type=F32)


def as_row(vector):
    return vector[...].astype(F32).reshape(1, vector.shape[0])


def left_half(shape):
    return lax.broadcasted_iota(jnp.int32, shape, 1) < HEAD_DIM


def pick(hot):
    return jnp.where(hot, 1.0, 0.0).astype(LOW)


def params(megabytes=60):
    return pltpu.CompilerParams(vmem_limit_bytes=megabytes << 20)


def columns_of(perm, rows):
    local = lax.rem(perm, rows)
    return jnp.concatenate([local, local[: 16 - HEADS]]).T


def kv_kernel(tok, w_key, w_value, b_value, perm, chosen_in, out, blocks, chosen, chosen_sem, sem):
    fetch = pltpu.make_async_copy(chosen_in, chosen, chosen_sem)
    fetch.start()
    rows = tok.shape[0]
    order = columns_of(perm[0], rows)
    per_dev = rows // CLUS
    place = lax.broadcasted_iota(jnp.int32, (rows, rows), 1)
    left = left_half((rows, 2 * HEAD_DIM))
    inputs = tok[...]
    keys = nn(inputs, w_key[...])
    values = nn(inputs, w_value[...]) + as_row(b_value)
    joined = []
    for pair in range(HEADS // 2):
        two = slice(pair * 2 * HEAD_DIM, (pair + 1) * 2 * HEAD_DIM)
        key_two = keys[:, two]
        value_two = pltpu.roll(values[:, two], HEAD_DIM, 1)
        joined.append(jnp.where(left, key_two, value_two).astype(LOW))
        joined.append(jnp.where(left, value_two, key_two).astype(LOW))
    for quad in range(HEADS // 4):
        heads = range(quad * 4, quad * 4 + 4)
        hot = [pick(order[:, head : head + 1] == place) for head in heads]
        ranked = [nn(one, joined[head]).astype(LOW) for one, head in zip(hot, heads)]
        for head, value in zip(heads, ranked):
            blocks[head * per_dev : (head + 1) * per_dev] = value.reshape(per_dev, CLUS, 2 * HEAD_DIM)
    fetch.wait()
    devices, capacity = chosen.shape

    @pl.loop(0, devices)
    def _(device):
        for slot in range(capacity):
            pltpu.make_async_copy(
                blocks.at[chosen[device, slot]], out.at[device * capacity + slot], sem
            ).start()

    pltpu.make_async_copy(out, out, sem).wait()


def q_kernel(tok, w_query, b_query, perm, out):
    rows = tok.shape[0]
    order = columns_of(perm[0], rows)
    place = lax.broadcasted_iota(jnp.int32, (rows, rows), 1)
    left = left_half((rows, 2 * HEAD_DIM))
    inputs = tok[...]
    for quad in range(HEADS // 4):
        four = slice(quad * 4 * HEAD_DIM, (quad + 1) * 4 * HEAD_DIM)
        queries = nn(inputs, w_query[:, four]) + as_row(b_query)[:, four]
        queries = (queries.astype(LOW).astype(F32) * HEAD_DIM ** (-0.5)).astype(LOW)
        for pair in range(2):
            two = queries[:, pair * 2 * HEAD_DIM : (pair + 1) * 2 * HEAD_DIM]
            for odd in range(2):
                head = quad * 4 + pair * 2 + odd
                hot = pick(order[:, head : head + 1] == place)
                ranked = nn(hot, two)
                kept = jnp.where(left, 0.0, ranked) if odd else jnp.where(left, ranked, 0.0)
                out[head] = kept.astype(LOW)


ROW_TILE = 512
WIDE = 768
WIDE_FORTH = 1024
WIDE_BACK = 1536


def mid_kernel(
    fetch, queries, arrived, order, inverse, tok_hbm, cot_hbm,
    b_out, gain_one, shift_one, b_up, b_down, gain_two, shift_two, w_out_hbm, w_up_hbm, w_down_hbm,
    back, dq_out, attn_out, z_out, active_out, du_out, df_out, db_out, dh1_out, layer_out, sums,
    kv, probs, attn, mixed, w_out, w_up, w_down, hidden, z_full, n_one, r_one, z_low, active, slope,
    dh2, df, db, d_out, dh1, final, dq, tok, cot, kv_sem, w_sem, out_sem, back_sem,
):
    rows = tok_hbm.shape[0]
    per_dev = rows // CLUS
    pair_width = 2 * HEAD_DIM
    requests = fetch.shape[0]
    each = 2 * per_dev * PAIRS
    width = w_up.shape[1]
    tiles = rows // ROW_TILE
    left = left_half((CLUS, pair_width))
    left_rows = left_half((rows, pair_width))
    down = lax.broadcasted_iota(jnp.int32, (rows, rows), 0)

    @pl.loop(0, HEADS // 2)
    def _(group):
        for step in range(each):
            entry = group * each + step
            pltpu.make_async_copy(arrived.at[fetch[entry]], kv.at[entry], kv_sem.at[group]).start()

    loads = [
        pltpu.make_async_copy(source, target, w_sem.at[at])
        for at, (source, target) in enumerate(
            ((w_out_hbm, w_out), (tok_hbm, tok), (w_up_hbm, w_up), (w_down_hbm, w_down), (cot_hbm, cot))
        )
    ]
    for load in loads:
        load.start()
    stores = []

    def store(source, target):
        copy = pltpu.make_async_copy(source, target, out_sem.at[len(stores)])
        copy.start()
        stores.append(copy)

    @pl.loop(0, HEADS // 2)
    def _(group):
        span = kv.at[pl.ds(group * each, each)]
        pltpu.make_async_copy(span, span, kv_sem.at[group]).wait()
        units = [(odd, cluster) for odd in range(2) for cluster in range(per_dev)]
        clusters = [slice(cluster * CLUS, (cluster + 1) * CLUS) for cluster in range(per_dev)]
        index = [(2 * group + odd) * per_dev + cluster for odd, cluster in units]
        pair = [kv[pl.ds(unit * PAIRS, PAIRS)].reshape(PAIRS * CLUS, pair_width) for unit in index]
        scores = [
            nt(queries[2 * group + odd, clusters[cluster], :], both)
            for (odd, cluster), both in zip(units, pair)
        ]
        exponent = [jnp.exp(value - jnp.max(value, -1, keepdims=True)) for value in scores]
        low = [(value / jnp.sum(value, -1, keepdims=True)).astype(LOW) for value in exponent]
        for (odd, cluster), unit, value, both in zip(units, index, low, pair):
            probs[unit] = value
            value = nn(value, both)
            mixed[odd, clusters[cluster], :] = (
                jnp.where(left, value, 0.0) if odd else jnp.where(left, 0.0, value)
            ).astype(LOW)
        hot = jnp.concatenate([pick(down == order[2 * group + odd]) for odd in range(2)], axis=1)
        both = pltpu.roll(nn(hot, mixed[...].reshape(2 * rows, pair_width)), HEAD_DIM, 1)
        attn[:, pl.ds(pl.multiple_of(group * pair_width, pair_width), pair_width)] = both.astype(LOW)

    store(attn, attn_out)
    loads[0].wait()
    loads[1].wait()
    hidden[...] = nn(attn[...], w_out[...])

    @pl.loop(0, tiles)
    def _(tile):
        at = pl.ds(pl.multiple_of(tile * ROW_TILE, ROW_TILE), ROW_TILE)
        value = hidden[at, :] + (as_row(b_out) + tok[at, :].astype(F32))
        centred = value - jnp.mean(value, -1, keepdims=True)
        scale = lax.rsqrt(jnp.mean(centred * centred, -1, keepdims=True) + 1e-06)
        unit = centred * scale
        z = unit * as_row(gain_one) + as_row(shift_one)
        n_one[at, :] = unit
        r_one[at, :] = scale
        z_low[at, :] = z.astype(LOW)
        z_full[at, :] = z
        hidden[at, :] = z + as_row(b_down)

    store(z_low, z_out)
    loads[2].wait()
    loads[3].wait()

    @pl.loop(0, width // WIDE_FORTH)
    def _(step):
        at = pl.ds(pl.multiple_of(step * WIDE_FORTH, WIDE_FORTH), WIDE_FORTH)
        inner = nn(z_low[...], w_up[:, at]) + b_up[at].astype(F32).reshape(1, WIDE_FORTH)
        normal = 0.5 * (1.0 + lax.erf(inner * 0.7071067811865476))
        density = jnp.exp(inner * inner * -0.5) * 0.3989422804014327
        active[:, at] = (inner * normal).astype(LOW)
        slope[:, at] = (normal + inner * density).astype(LOW)
        hidden[...] += nn(active[:, at], w_down[at, :])

    store(active, active_out)
    loads[4].wait()
    sums[...] = jnp.zeros_like(sums)

    @pl.loop(0, tiles)
    def _(tile):
        at = pl.ds(pl.multiple_of(tile * ROW_TILE, ROW_TILE), ROW_TILE)
        value = hidden[at, :]
        centred = value - jnp.mean(value, -1, keepdims=True)
        scale = lax.rsqrt(jnp.mean(centred * centred, -1, keepdims=True) + 1e-06)
        unit = centred * scale
        final[at, :] = (unit * as_row(gain_two) + as_row(shift_two)).astype(LOW)
        grad = cot[at, :].astype(F32)
        lifted = grad * as_row(gain_two)
        back_grad = scale * (
            lifted - jnp.mean(lifted, -1, keepdims=True) - unit * jnp.mean(lifted * unit, -1, keepdims=True)
        )
        dh2[at, :] = back_grad
        low = back_grad.astype(LOW)
        df[at, :] = low
        sums[0:1, :] += jnp.sum(grad * unit, axis=0, keepdims=True)
        sums[1:2, :] += jnp.sum(grad, axis=0, keepdims=True)
        sums[2:3, :] += jnp.sum(low.astype(F32), axis=0, keepdims=True)

    store(final, layer_out)
    store(df, df_out)
    ones = jnp.ones((8, rows), LOW)

    @pl.loop(0, width // WIDE_BACK)
    def _(step):
        at = pl.ds(pl.multiple_of(step * WIDE_BACK, WIDE_BACK), WIDE_BACK)
        grad = (nt(df[...], w_down[at, :]) * slope[:, at].astype(F32)).astype(LOW)
        slope[:, at] = grad
        total = nn(ones, grad)
        for part in range(WIDE_BACK // D):
            row = 8 + step * (WIDE_BACK // D) + part
            sums[pl.ds(row, 1), :] = total[0:1, part * D : (part + 1) * D]
        dh2[...] += nt(slope[:, at], w_up[:, at])

    store(slope, du_out)

    @pl.loop(0, tiles)
    def _(tile):
        at = pl.ds(pl.multiple_of(tile * ROW_TILE, ROW_TILE), ROW_TILE)
        grad = dh2[at, :]
        unit = n_one[at, :]
        lifted = grad * as_row(gain_one)
        back_grad = r_one[at, :] * (
            lifted - jnp.mean(lifted, -1, keepdims=True) - unit * jnp.mean(lifted * unit, -1, keepdims=True)
        )
        dh1[at, :] = back_grad
        low = back_grad.astype(LOW)
        db[at, :] = low
        sums[3:4, :] += jnp.sum(grad * unit, axis=0, keepdims=True)
        sums[4:5, :] += jnp.sum(grad, axis=0, keepdims=True)
        sums[5:6, :] += jnp.sum(low.astype(F32), axis=0, keepdims=True)

    store(dh1, dh1_out)
    store(db, db_out)
    d_out[...] = nt(db[...], w_out[...]).astype(LOW)

    @pl.loop(0, HEADS // 2)
    def _(group):
        lanes = pl.ds(pl.multiple_of(group * pair_width, pair_width), pair_width)
        tile = d_out[:, lanes]
        grads = []
        for odd in range(2):
            turned = pltpu.roll(nn(pick(down == inverse[2 * group + odd]), tile), HEAD_DIM, 1)
            grads.append((jnp.where(left_rows, turned, 0.0) if odd else jnp.where(left_rows, 0.0, turned)).astype(LOW))
        units = [(odd, cluster) for odd in range(2) for cluster in range(per_dev)]
        clusters = [slice(cluster * CLUS, (cluster + 1) * CLUS) for cluster in range(per_dev)]
        index = [(2 * group + odd) * per_dev + cluster for odd, cluster in units]
        grad = [grads[odd][clusters[cluster]] for odd, cluster in units]
        query = [queries[2 * group + odd, clusters[cluster], :] for odd, cluster in units]
        pair = [kv[pl.ds(unit * PAIRS, PAIRS)].reshape(PAIRS * CLUS, pair_width) for unit in index]
        low = [probs[unit] for unit in index]
        d_probs = [nt(left_, right) for left_, right in zip(grad, pair)]
        wide = [value.astype(F32) for value in low]
        d_scores = [
            (value * (grad_ - jnp.sum(grad_ * value, -1, keepdims=True))).astype(LOW)
            for value, grad_ in zip(wide, d_probs)
        ]
        d_query = [nn(left_, right) * HEAD_DIM ** (-0.5) for left_, right in zip(d_scores, pair)]
        d_pair = [tn(a, b) + tn(c, d) for a, b, c, d in zip(d_scores, query, low, grad)]
        bias = [jnp.zeros((1, pair_width), F32)] * 2
        q_total = jnp.zeros((1, pair_width), F32)
        for (odd, cluster), unit, value, both in zip(units, index, d_query, d_pair):
            value = (jnp.where(left, 0.0, value) if odd else jnp.where(left, value, 0.0)).astype(LOW)
            dq[2 * group + odd, clusters[cluster], :] = value
            q_total += jnp.sum(value.astype(F32), axis=0, keepdims=True)
            bias[odd] += jnp.sum(both, axis=0, keepdims=True)
            kv[pl.ds(unit * PAIRS, PAIRS)] = both.astype(LOW).reshape(PAIRS, CLUS, pair_width)
        for step in range(each):
            entry = group * each + step
            pltpu.make_async_copy(kv.at[entry], back.at[fetch[entry]], back_sem).start()
        both = jnp.where(left_half((1, pair_width)), bias[1], bias[0])
        sums[7:8, lanes] = q_total
        sums[6:7, lanes] = pltpu.roll(jnp.broadcast_to(both, (8, pair_width)), HEAD_DIM, 1)[0:1]

    store(dq, dq_out)
    span = back.at[pl.ds(0, requests)]
    pltpu.make_async_copy(kv, span, back_sem).wait()
    for copy in stores:
        copy.wait()


CHUNKS = 16


def chunk_rows(at, size):
    return pl.ds(pl.multiple_of(at * size, size), size)


def place_chunks(source, target, info, sem, start=1):
    size = source.shape[0] // CHUNKS
    for chunk in range(CHUNKS):
        pltpu.make_async_copy(
            source.at[chunk * size : (chunk + 1) * size],
            target.at[chunk_rows(info[start + chunk], size)],
            sem,
        ).start()


def wait_chunks(source, target, sem):
    pltpu.make_async_copy(source, target, sem).wait()


def core_of(info, side):
    return info[0] if side else 1 - info[0]


def up_kernel(info, z_low, grad, give, keep, turned, buf, sem):
    half = keep.shape[1]
    turned[...] = z_low[...].T
    for side, out in ((0, give), (1, keep)):
        at = pl.ds(pl.multiple_of(core_of(info, side) * half, half), half)
        buf[side] = nn(turned[...], grad[:, at]).astype(LOW)
        place_chunks(buf.at[side], out, info, sem.at[side])
    for side, out in ((0, give), (1, keep)):
        wait_chunks(buf.at[side], out, sem.at[side])


def down_kernel(info, active, grad, give, keep, buf, sem):
    size = keep.shape[0]
    for side, out in ((0, give), (1, keep)):
        for part in range(keep.shape[1] // size):
            block = core_of(info, side) * (keep.shape[1] // size) + part
            at = pl.ds(pl.multiple_of(block * size, size), size)
            buf[side, :, part * size : (part + 1) * size] = nn(active[:, at].T, grad[...]).astype(LOW)
        place_chunks(buf.at[side], out, info, sem.at[side])
    for side, out in ((0, give), (1, keep)):
        wait_chunks(buf.at[side], out, sem.at[side])


def out_q_kernel(info, attn, db, tok, dq, order, sums, give, keep, grad_q, attn_t, tok_t, buf, sem):
    rows = tok.shape[0]
    half = D // 2
    down = lax.broadcasted_iota(jnp.int32, (rows, rows), 0)
    for pair in range(HEADS // 2):
        total = nn(pick(down == order[2 * pair]), dq[2 * pair])
        total += nn(pick(down == order[2 * pair + 1]), dq[2 * pair + 1])
        lanes = slice(pair * 2 * HEAD_DIM, (pair + 1) * 2 * HEAD_DIM)
        grad_q[:, lanes] = total.astype(LOW)
    attn_t[...] = attn[...].T
    tok_t[...] = tok[...].T
    size = D // CHUNKS
    filler = jnp.zeros((size - D // LANES, LANES), F32)
    for vector in range(CHUNKS):
        rows_of = [sums[vector : vector + 1, row * LANES : (row + 1) * LANES] for row in range(D // LANES)]
        value = jnp.concatenate(rows_of + [filler]).astype(LOW)
        for side in range(2):
            buf[side, vector * size : (vector + 1) * size, D:] = value
    for side, out in ((0, give), (1, keep)):
        at = pl.ds(pl.multiple_of(core_of(info, side) * half, half), half)
        buf[side, :, :half] = nn(attn_t[...], db[:, at]).astype(LOW)
        buf[side, :, half:D] = nn(tok_t[...], grad_q[:, at]).astype(LOW)
        place_chunks(buf.at[side], out, info, sem.at[side])
    for side, out in ((0, give), (1, keep)):
        wait_chunks(buf.at[side], out, sem.at[side])


def key_value_kernel(
    info, segment, returned_hbm, order, tok, key_give, key_keep, value_give, value_keep, grad_kv_hbm,
    returned, total, tok_t, grad_kv, buf, load_sem, kv_sem, sem,
):
    rows = tok.shape[0]
    half = D // 2
    per_dev = rows // CLUS
    pair_width = 2 * HEAD_DIM
    devices = load_sem.shape[0]
    capacity = segment.shape[0] // devices

    def load(device):
        span = pl.ds(device * capacity, capacity)
        return pltpu.make_async_copy(returned_hbm.at[span], returned.at[span], load_sem.at[device])

    @pl.loop(0, devices)
    def _(device):
        load(device).start()

    down = lax.broadcasted_iota(jnp.int32, (rows, rows), 0)
    left = left_half((rows, pair_width))
    total[...] = jnp.zeros_like(total)
    tok_t[...] = tok[...].T

    @pl.loop(0, devices)
    def _(device):
        load(device).wait()
        for step in range(capacity):
            slot = device * capacity + step
            block = segment[slot]
            total[block] += returned[slot].astype(F32)

    for quad in range(HEADS // 4):
        pairs = range(2 * quad, 2 * quad + 2)
        heads = range(4 * quad, 4 * quad + 4)
        hots = [pick(down == order[head]) for head in heads]
        summed = [
            total[head * per_dev : (head + 1) * per_dev].reshape(rows, pair_width).astype(LOW) for head in heads
        ]
        placed = [nn(hot, value) for hot, value in zip(hots, summed)]
        for at, pair in enumerate(pairs):
            even, odd = placed[2 * at], placed[2 * at + 1]
            grad_kv[:, pair * pair_width : (pair + 1) * pair_width] = jnp.where(left, even, odd).astype(LOW)
            values = pltpu.roll(jnp.where(left, odd, even), HEAD_DIM, 1)
            grad_kv[:, D + pair * pair_width : D + (pair + 1) * pair_width] = values.astype(LOW)
    stored = pltpu.make_async_copy(grad_kv, grad_kv_hbm, kv_sem)
    stored.start()
    outs = ((key_give, key_keep), (value_give, value_keep))
    for side in range(2):
        base = core_of(info, side) * half
        parts = [grad_kv[:, pl.ds(pl.multiple_of(part * D + base, half), half)] for part in range(2)]
        value = nn(tok_t[...], jnp.concatenate(parts, axis=1)).astype(LOW)
        for part in range(2):
            buf[part, side] = value[:, part * half : (part + 1) * half]
            place_chunks(buf.at[part, side], outs[part][side], info, sem.at[part, side], 65 if part else 1)
    for side in range(2):
        for part in range(2):
            wait_chunks(buf.at[part, side], outs[part][side], sem.at[part, side])
    stored.wait()


def spread_start(info, start, pieces, targets, buf, sem):
    size = buf.shape[2]
    copies = []
    for at, piece in enumerate(pieces):
        core = core_of(info, 1 - at)
        for chunk in range(buf.shape[1]):
            buf[at, chunk] = piece[chunk * size : (chunk + 1) * size].astype(F32)
            for lanes, target in targets(core, chunk_rows(info[start + chunk], size)):
                copies.append(pltpu.make_async_copy(buf.at[at, chunk, :, lanes], target, sem))
                copies[-1].start()
    return copies


def up_targets(out, half):
    def targets(core, rows):
        yield pl.ds(0, half), out.at[rows, pl.ds(pl.multiple_of(core * half, half), half)]

    return targets


def down_targets(out, half):
    parts = half // D

    def targets(core, rows):
        for part in range(parts):
            yield pl.ds(part * D, D), out.at[core * parts + part, rows]

    return targets


def attention_targets(w_out, w_qkv):
    half = D // 2

    def targets(core, rows):
        at = pl.ds(pl.multiple_of(core * half, half), half)
        yield pl.ds(0, half), w_out.at[rows, at]
        for part, lane in enumerate((half, D + LANES, D + LANES + half)):
            to = pl.ds(pl.multiple_of(part * D + core * half, half), half)
            yield pl.ds(lane, half), w_qkv.at[rows, to]

    return targets


def spread_groups(groups, info, pieces, outs, staged, bufs, load_sem, sem):
    w_up, w_down, w_out, w_qkv = outs
    half = w_up.shape[1] // 2
    routes = (up_targets(w_up, half), down_targets(w_down, half), attention_targets(w_out, w_qkv))
    loads = []
    for at, (source, target) in enumerate(zip(pieces, staged)):
        loads.append(pltpu.make_async_copy(source, target, load_sem.at[at]))
        loads[-1].start()
    copies = []
    for at, (third, start) in enumerate(groups):
        for load in loads[2 * at : 2 * at + 2]:
            load.wait()
        copies += spread_start(info, start, staged[2 * at : 2 * at + 2], routes[third], bufs[at], sem.at[at])
    return copies


def spread_kernel(groups, info, *refs):
    pairs = len(groups)
    pieces, scratch = refs[: 2 * pairs], refs[-3 * pairs - 2 :]
    outs = refs[-3 * pairs - 6 : -3 * pairs - 2]
    staged, bufs = scratch[: 2 * pairs], scratch[2 * pairs : 3 * pairs]
    for copy in spread_groups(groups, info, pieces, outs, staged, bufs, *scratch[3 * pairs :]):
        copy.wait()


def spread_last_kernel(groups, start, info, *refs):
    pairs = len(groups)
    pieces, sources = refs[: 2 * pairs], refs[2 * pairs : 2 * pairs + 4]
    rest = refs[2 * pairs + 8 :]
    outs, vectors, rest = rest[:4], rest[4:13], rest[13:]
    staged, bufs = rest[: 2 * pairs], rest[2 * pairs : 3 * pairs]
    load_sem, sem, columns, table, column_sem = rest[3 * pairs :]
    loads = [
        pltpu.make_async_copy(source.at[:, D : D + LANES], columns.at[at], column_sem.at[at])
        for at, source in enumerate(sources)
    ]
    for load in loads:
        load.start()
    copies = spread_groups(groups, info, pieces, outs, staged, bufs, load_sem, sem)
    size = D // CHUNKS
    each = CHUNKS // len(sources)
    for at, load in enumerate(loads):
        load.wait()
        for chunk in range(each):
            table[info[start + at * each + chunk]] = columns[at, chunk * size : chunk * size + 16].astype(F32)

    def whole(vector):
        return jnp.concatenate([table[vector, row : row + 1] for row in range(D // LANES)], axis=1)

    for at, vector in enumerate(vectors):
        count = vector.shape[0] // D
        vector[...] = jnp.concatenate([whole(at + part) for part in range(count)], axis=1).reshape(count * D)
    for copy in copies:
        copy.wait()


X, Y, Z0, Z1 = ("dp", 1), ("blk", 2), ("blk", 4), ("blk", 8)
CORE = ("blk", 1)


def swap(value, bit):
    axis, distance = bit
    size = lax.axis_size(axis)
    return lax.ppermute(value, axis, [(i, i ^ distance) for i in range(size)])


def further_bits(count_blk):
    bits = []
    distance = 16
    while distance < count_blk:
        bits.append(("blk", distance))
        distance *= 2
    return bits


def chip_bits():
    return [(lax.axis_index(axis) // distance) % 2 for axis, distance in (X, Y, Z0, Z1)]


def chunk_places():
    x, y, z0, z1 = chip_bits()
    chip = x * 8 + y * 4 + z0 * 2 + z1
    core = lax.axis_index("blk") % 2
    every = jnp.arange(CHUNKS, dtype=jnp.int32)
    value = {X: 8, Y: 4, Z0: 2, Z1: 1}

    def from_order(order):
        at = sum(((every // 2**step) % 2) * value[bit] for step, bit in enumerate(order))
        return at ^ chip

    placed = every ^ chip
    x_y_swapped = placed % 4 + (placed // 8) * 4 + (placed // 4 % 2) * 8
    return jnp.concatenate(
        [core[None], placed]
        + [from_order(order) for order in (ORDER_X, ORDER_Y, ORDER_Z)]
        + [x_y_swapped]
    )


ORDER_X = (Z1, Z0, Y, X)
ORDER_Y = (Z1, X, Z0, Y)
ORDER_Z = (Z1, Y, X, Z0)


def sum_rows(terms, low, high):
    total = terms[0][low:high].astype(F32)
    for term in terms[1:]:
        total = total + term[low:high].astype(F32)
    return total


def to_send(terms):
    rows = min(term.shape[0] for term in terms)
    return sum_rows(terms, rows // 2, rows).astype(LOW)


def scatter_steps(terms, bits):
    for bit in bits:
        terms = terms + [swap(to_send(terms), bit)]
    return terms


def finish(terms, further):
    value = sum_rows(terms, 0, terms[-1].shape[0]).astype(LOW)
    for bit in further:
        value = sum_rows([value, swap(value, bit)], 0, value.shape[0]).astype(LOW)
    return value


def tie(values):
    return lax.optimization_barrier(tuple(values))


def gather_step(value, bit):
    return jnp.concatenate([value, swap(value, bit)])


def per_device(
    tokens,
    w_qkv,
    b_query,
    b_value,
    w_out,
    b_out,
    gain_one,
    shift_one,
    w_up,
    b_up,
    w_down,
    b_down,
    gain_two,
    shift_two,
    cluster_perm,
    cluster_pairs,
    cotangent,
):
    count_blk = lax.axis_size("blk")
    my_index = lax.axis_index("blk")
    rows = tokens.shape[0]
    per_dev = rows // CLUS
    blocks = HEADS * per_dev
    requests = blocks * PAIRS
    capacity = max(2, (requests + count_blk - 1) // count_blk + 1)
    slots = count_blk * capacity
    pair_width = 2 * HEAD_DIM
    ff = w_up.shape[1]
    local_order = cluster_perm[0] - my_index * rows
    order_rows = local_order[:, None, :]

    wanted = (
        cluster_pairs[0]
        .reshape(HEADS, count_blk, per_dev, PAIRS)
        .transpose(1, 0, 2, 3)
        .reshape(count_blk, requests)
    )
    positions = jnp.arange(requests, dtype=jnp.int32)
    before = positions[:, None] < positions[None, :]
    source = wanted // per_dev
    named = source == my_index
    rank = jnp.sum(named[:, :, None] & before[None], axis=1)
    head_of = positions // (per_dev * PAIRS)
    block_id = head_of[None, :] * per_dev + wanted % per_dev
    matches = named[:, :, None] & (
        rank[:, :, None] == jnp.arange(capacity, dtype=jnp.int32)[None, None, :]
    )
    chosen = jnp.sum(jnp.where(matches, block_id[:, :, None], 0), axis=1)

    smem = pl.BlockSpec(memory_space=pltpu.SMEM)
    vmem = pl.BlockSpec(memory_space=pltpu.VMEM)
    hbm = pl.BlockSpec(memory_space=pl.ANY)

    def column_block(at):
        return pl.BlockSpec((D, D), lambda step: (0, at))

    outgoing = pl.pallas_call(
        kv_kernel,
        grid=(1,),
        out_shape=jax.ShapeDtypeStruct((slots, CLUS, pair_width), LOW),
        in_specs=[vmem, column_block(1), column_block(2), vmem, vmem, vmem],
        out_specs=hbm,
        scratch_shapes=[
            pltpu.VMEM((blocks, CLUS, pair_width), LOW),
            pltpu.SMEM(chosen.shape, jnp.int32),
            pltpu.SemaphoreType.DMA,
            pltpu.SemaphoreType.DMA,
        ],
        compiler_params=params(),
        name="kv_kernel",
    )(tokens, w_qkv, w_qkv, b_value, cluster_perm, chosen)
    arrived = lax.all_to_all(
        outgoing.reshape(count_blk, capacity, CLUS, pair_width),
        "blk",
        split_axis=0,
        concat_axis=0,
        tiled=True,
    ).reshape(slots, CLUS, pair_width)

    info = chunk_places()
    queries = pl.pallas_call(
        q_kernel,
        grid=(1,),
        out_shape=jax.ShapeDtypeStruct((HEADS, rows, pair_width), LOW),
        in_specs=[vmem, column_block(0), vmem, vmem],
        out_specs=vmem,
        compiler_params=params(),
        name="q_kernel",
    )(tokens, w_qkv, b_query, cluster_perm)
    filled = jnp.any(matches, axis=1)
    segment = jnp.where(filled, chosen, blocks).reshape(-1)
    my_source = lax.dynamic_index_in_dim(wanted, my_index, 0, keepdims=False) // per_dev
    my_rank = jnp.sum((my_source[:, None] == my_source[None, :]) & before, axis=0)
    fetch = my_source * capacity + my_rank
    places = jnp.arange(rows, dtype=jnp.int32)
    inverse = jnp.sum(
        jnp.where(local_order[:, :, None] == places, places[None, :, None], 0), axis=1
    )[:, None, :]
    def low(*shape):
        return jax.ShapeDtypeStruct(shape, LOW)

    def full(*shape):
        return jax.ShapeDtypeStruct(shape, F32)

    (
        back, dq_sorted, attn, normed, active, grad_inner, grad_second, grad_branch, grad_resid,
        layer_out, sums,
    ) = pl.pallas_call(
        mid_kernel,
        out_shape=(
            low(slots, CLUS, pair_width), low(HEADS, rows, pair_width), low(rows, D), low(rows, D),
            low(rows, ff), low(rows, ff), low(rows, D), low(rows, D), full(rows, D), low(rows, D),
            full(16, D),
        ),
        in_specs=[smem, vmem, hbm, vmem, vmem, hbm, hbm] + [vmem] * 7 + [hbm] * 3,
        out_specs=(hbm,) * 10 + (vmem,),
        scratch_shapes=[
            pltpu.VMEM((requests, CLUS, pair_width), LOW),
            pltpu.VMEM((blocks, CLUS, PAIRS * CLUS), LOW),
            pltpu.VMEM((rows, D), LOW),
            pltpu.VMEM((2, rows, pair_width), LOW),
            pltpu.VMEM((D, D), LOW),
            pltpu.VMEM((D, ff), LOW),
            pltpu.VMEM((ff, D), LOW),
            pltpu.VMEM((rows, D), F32),
            pltpu.VMEM((rows, D), F32),
            pltpu.VMEM((rows, D), F32),
            pltpu.VMEM((rows, 1), F32),
            pltpu.VMEM((rows, D), LOW),
            pltpu.VMEM((rows, ff), LOW),
            pltpu.VMEM((rows, ff), LOW),
            pltpu.VMEM((rows, D), F32),
            pltpu.VMEM((rows, D), LOW),
            pltpu.VMEM((rows, D), LOW),
            pltpu.VMEM((rows, D), LOW),
            pltpu.VMEM((rows, D), F32),
            pltpu.VMEM((rows, D), LOW),
            pltpu.VMEM((HEADS, rows, pair_width), LOW),
            pltpu.VMEM((rows, D), LOW),
            pltpu.VMEM((rows, D), LOW),
            pltpu.SemaphoreType.DMA((HEADS // 2,)),
            pltpu.SemaphoreType.DMA((5,)),
            pltpu.SemaphoreType.DMA((9,)),
            pltpu.SemaphoreType.DMA,
        ],
        compiler_params=params(),
        name="mid_kernel",
    )(
        fetch, queries, arrived, order_rows, inverse, tokens, cotangent,
        b_out, gain_one, shift_one, b_up, b_down, gain_two, shift_two, w_out, w_up, w_down,
    )
    returned = lax.all_to_all(
        back.reshape(count_blk, capacity, CLUS, pair_width),
        "blk",
        split_axis=0,
        concat_axis=0,
        tiled=True,
    ).reshape(slots, CLUS, pair_width)

    further = further_bits(count_blk)

    def halves(kernel, operands, columns, scratch, more=(), name=None):
        return pl.pallas_call(
            kernel,
            out_shape=(low(D, columns), low(D, columns)) + more,
            in_specs=[smem] + [vmem] * (len(operands) - 1),
            out_specs=(hbm, hbm) + (vmem,) * len(more),
            scratch_shapes=scratch
            + [pltpu.VMEM((2, D, columns), LOW), pltpu.SemaphoreType.DMA((2,))],
            compiler_params=params(),
            cost_estimate=pl.CostEstimate(flops=1, bytes_accessed=1, transcendentals=0),
            name=name,
        )(*operands)

    half = D // 2
    turned = pltpu.VMEM((D, rows), LOW)
    up_give, up_keep = halves(
        up_kernel, (info, normed, grad_inner), ff // 2, [turned], name="up_kernel"
    )
    down_give, down_keep = halves(
        down_kernel, (info, active, grad_second), ff // 2, [], name="down_kernel"
    )
    up = [up_keep, swap(up_give, CORE)]
    up_step, attn = tie((to_send(up), attn))
    oq_give, oq_keep, grad_q = halves(
        out_q_kernel,
        (info, attn, grad_branch, tokens, dq_sorted, order_rows, sums),
        D + LANES,
        [turned, turned],
        (low(rows, D),),
        name="out_q_kernel",
    )
    up = scatter_steps(up + [swap(up_step, X)], (Y,))
    down = scatter_steps([down_keep, swap(down_give, CORE)], (X,))
    out_q = scatter_steps([oq_keep, swap(oq_give, CORE)], (X,))
    up_step = to_send(up)
    up_step, down[-1] = tie((up_step, down[-1]))
    down_step = to_send(down)

    returned, up_step, down_step, out_q[-1] = tie((returned, up_step, down_step, out_q[-1]))
    up = up + [swap(up_step, Z0)]
    down = down + [swap(down_step, Y)]
    out_q = scatter_steps(out_q, (Y,))
    key_give, key_keep, value_give, value_keep, grad_kv = pl.pallas_call(
        key_value_kernel,
        out_shape=(low(D, half),) * 4 + (low(rows, 2 * D),),
        in_specs=[smem, smem, hbm, vmem, vmem],
        out_specs=(hbm,) * 5,
        scratch_shapes=[
            pltpu.VMEM((slots, CLUS, pair_width), LOW),
            pltpu.VMEM((blocks + 1, CLUS, pair_width), F32),
            turned,
            pltpu.VMEM((rows, 2 * D), LOW),
            pltpu.VMEM((2, 2, D, half), LOW),
            pltpu.SemaphoreType.DMA((count_blk,)),
            pltpu.SemaphoreType.DMA,
            pltpu.SemaphoreType.DMA((2, 2)),
        ],
        compiler_params=params(),
        name="key_value_kernel",
    )(info, segment, returned, order_rows, tokens)
    down[-1], key_give, value_give = tie((down[-1], key_give, value_give))
    key = scatter_steps([key_keep, swap(key_give, CORE)], (X, Y))
    value = scatter_steps([value_keep, swap(value_give, CORE)], (Y, X))
    up = finish(scatter_steps(up, (Z1,)), further)
    down = finish(scatter_steps(down, (Z0, Z1)), further)
    out_q = finish(scatter_steps(out_q, (Z0, Z1)), further)
    late_given = swap(jnp.concatenate([to_send(key), to_send(value)], axis=1), Z0)
    key = key + [late_given[:, :half]]
    value = value + [late_given[:, half:]]
    late_given = swap(jnp.concatenate([to_send(key), to_send(value)], axis=1), Z1)
    key = finish(key + [late_given[:, :half]], further)
    value = finish(value + [late_given[:, half:]], further)
    thirds = [
        gather_step(third, Z1)
        for third in (
            up,
            down,
            jnp.concatenate([out_q, key, value], axis=1),
        )
    ]

    orders = (ORDER_X, ORDER_Y, ORDER_Z)
    starts = (17, 33, 49)
    weights = (full(D, ff), full(ff // D, D, D), full(D, D), full(D, 3 * D))

    def swap_all(values, step):
        return [swap(value, order[step]) for value, order in zip(values, orders)]

    def spread_scratch(pieces):
        rows_each = D // CHUNKS
        return (
            [pltpu.VMEM(piece.shape, LOW) for piece in pieces]
            + [
                pltpu.VMEM((2, piece.shape[0] // rows_each, rows_each, piece.shape[1]), F32)
                for piece in pieces[::2]
            ]
            + [
                pltpu.SemaphoreType.DMA((len(pieces),)),
                pltpu.SemaphoreType.DMA((len(pieces) // 2,)),
            ]
        )

    def with_other(sets):
        return [array for value in sets for array in (value, swap(value, CORE))]

    def spread(sets, offsets, outs=()):
        pieces = with_other(sets)
        groups = tuple((third, starts[third] + offset) for offset in offsets for third in range(3))
        return pl.pallas_call(
            partial(spread_kernel, groups),
            out_shape=weights,
            in_specs=[smem] + [hbm] * (len(pieces) + len(outs)),
            out_specs=(hbm,) * 4,
            scratch_shapes=spread_scratch(pieces),
            input_output_aliases={1 + len(pieces) + at: at for at in range(len(outs))},
            compiler_params=params(),
            name="spread",
        )(info, *pieces, *outs)

    thirds = list(tie(gather_step(value, order[1]) for value, order in zip(thirds, orders)))
    third_step = swap_all(thirds, 2)
    fourth_step = swap_all(thirds, 3)
    outs = spread(thirds, (0,))
    tied = tie((*third_step, grad_kv))
    third_step, grad_kv = list(tied[:3]), tied[3]
    last_step = swap_all(third_step, 3)
    grad_proj = jnp.concatenate([grad_q, grad_kv], axis=1)
    grad_tokens = (grad_resid + nt(grad_proj, w_qkv)).astype(LOW)
    tied = tie((*fourth_step, *outs, grad_tokens))
    fourth_step, outs, grad_tokens = list(tied[:3]), tied[3:7], tied[7]
    outs = spread(third_step + fourth_step, (4, 8), outs)
    tied = tie((*last_step, *outs))
    last_step, outs = list(tied[:3]), tied[3:]
    pieces = with_other(last_step)
    sum_up, sum_down, sum_out, sum_qkv, *vectors = pl.pallas_call(
        partial(spread_last_kernel, tuple((third, starts[third] + 12) for third in range(3)), starts[2]),
        out_shape=weights + (full(D),) * 8 + (full(ff),),
        in_specs=[smem] + [hbm] * (len(pieces) + 8),
        out_specs=(hbm,) * 4 + (vmem,) * 9,
        scratch_shapes=spread_scratch(pieces)
        + [
            pltpu.VMEM((4, D // 4, LANES), LOW),
            pltpu.VMEM((CHUNKS, 16, LANES), F32),
            pltpu.SemaphoreType.DMA((4,)),
        ],
        input_output_aliases={1 + len(pieces) + 4 + at: at for at in range(4)},
        compiler_params=params(),
        name="spread_last",
    )(info, *pieces, thirds[2], third_step[2], fourth_step[2], last_step[2], *outs)
    return (
        layer_out,
        grad_tokens,
        sum_qkv,
        vectors[7],
        vectors[6],
        sum_out,
        vectors[5],
        vectors[3],
        vectors[4],
        sum_up,
        vectors[8],
        sum_down.reshape(ff, D),
        vectors[2],
        vectors[0],
        vectors[1],
    )


def solution(mesh):
    whole = P()
    rows = P(("dp", "blk"), None)
    return jax.shard_map(
        per_device,
        mesh=mesh,
        in_specs=(
            (rows,)
            + (whole,) * 13
            + (P("dp", None, "blk"), P("dp", None, None, None), rows)
        ),
        out_specs=(rows, rows) + (whole,) * 13,
        check_vma=False,
    )
```

```python
from functools import partial

import jax
import jax.numpy as jnp
from jax import lax
from jax.experimental import pallas as pl
from jax.experimental.pallas import tpu as pltpu
from jax.sharding import PartitionSpec as P

D = 768
HEADS = 12
HEAD_DIM = 64
CLUS = 128
PAIRS = 2
LANES = 128

F32 = jnp.float32
LOW = jnp.bfloat16


def nn(left, right):
    return jnp.dot(left, right, preferred_element_type=F32)


def nt(left, right):
    return lax.dot_general(left, right, (((1,), (1,)), ((), ())), preferred_element_type=F32)


def tn(left, right):
    return lax.dot_general(left, right, (((0,), (0,)), ((), ())), preferred_element_type=F32)


def as_row(vector):
    return vector[...].astype(F32).reshape(1, vector.shape[0])


def left_half(shape):
    return lax.broadcasted_iota(jnp.int32, shape, 1) < HEAD_DIM


def pick(hot):
    return jnp.where(hot, 1.0, 0.0).astype(LOW)


def params(megabytes=60):
    return pltpu.CompilerParams(vmem_limit_bytes=megabytes << 20)


def columns_of(perm, rows):
    local = lax.rem(perm, rows)
    return jnp.concatenate([local, local[: 16 - HEADS]]).T


def kv_kernel(tok, w_key, w_value, b_value, perm, chosen_in, out, blocks, chosen, chosen_sem, sem):
    fetch = pltpu.make_async_copy(chosen_in, chosen, chosen_sem)
    fetch.start()
    rows = tok.shape[0]
    order = columns_of(perm[0], rows)
    per_dev = rows // CLUS
    place = lax.broadcasted_iota(jnp.int32, (rows, rows), 1)
    left = left_half((rows, 2 * HEAD_DIM))
    inputs = tok[...]
    keys = nn(inputs, w_key[...])
    values = nn(inputs, w_value[...]) + as_row(b_value)
    joined = []
    for pair in range(HEADS // 2):
        two = slice(pair * 2 * HEAD_DIM, (pair + 1) * 2 * HEAD_DIM)
        key_two = keys[:, two]
        value_two = pltpu.roll(values[:, two], HEAD_DIM, 1)
        joined.append(jnp.where(left, key_two, value_two).astype(LOW))
        joined.append(jnp.where(left, value_two, key_two).astype(LOW))
    for quad in range(HEADS // 4):
        heads = range(quad * 4, quad * 4 + 4)
        hot = [pick(order[:, head : head + 1] == place) for head in heads]
        ranked = [nn(one, joined[head]).astype(LOW) for one, head in zip(hot, heads)]
        for head, value in zip(heads, ranked):
            blocks[head * per_dev : (head + 1) * per_dev] = value.reshape(per_dev, CLUS, 2 * HEAD_DIM)
    fetch.wait()
    devices, capacity = chosen.shape

    @pl.loop(0, devices)
    def _(device):
        for slot in range(capacity):
            pltpu.make_async_copy(
                blocks.at[chosen[device, slot]], out.at[device * capacity + slot], sem
            ).start()

    pltpu.make_async_copy(out, out, sem).wait()


def q_kernel(tok, w_query, b_query, perm, out):
    rows = tok.shape[0]
    order = columns_of(perm[0], rows)
    place = lax.broadcasted_iota(jnp.int32, (rows, rows), 1)
    left = left_half((rows, 2 * HEAD_DIM))
    inputs = tok[...]
    for quad in range(HEADS // 4):
        four = slice(quad * 4 * HEAD_DIM, (quad + 1) * 4 * HEAD_DIM)
        queries = nn(inputs, w_query[:, four]) + as_row(b_query)[:, four]
        queries = (queries.astype(LOW).astype(F32) * HEAD_DIM ** (-0.5)).astype(LOW)
        for pair in range(2):
            two = queries[:, pair * 2 * HEAD_DIM : (pair + 1) * 2 * HEAD_DIM]
            for odd in range(2):
                head = quad * 4 + pair * 2 + odd
                hot = pick(order[:, head : head + 1] == place)
                ranked = nn(hot, two)
                kept = jnp.where(left, 0.0, ranked) if odd else jnp.where(left, ranked, 0.0)
                out[head] = kept.astype(LOW)


ROW_TILE = 512
WIDE = 768
WIDE_FORTH = 1024
WIDE_BACK = 1536


def mid_kernel(
    fetch, queries, arrived, order, inverse, tok_hbm, cot_hbm,
    b_out, gain_one, shift_one, b_up, b_down, gain_two, shift_two, w_out_hbm, w_up_hbm, w_down_hbm,
    back, dq_out, attn_out, z_out, active_out, du_out, df_out, db_out, dh1_out, layer_out, sums,
    kv, probs, attn, mixed, w_out, w_up, w_down, hidden, z_full, n_one, r_one, z_low, active, slope,
    dh2, df, db, d_out, dh1, final, dq, tok, cot, kv_sem, w_sem, out_sem, back_sem,
):
    rows = tok_hbm.shape[0]
    per_dev = rows // CLUS
    pair_width = 2 * HEAD_DIM
    requests = fetch.shape[0]
    each = 2 * per_dev * PAIRS
    width = w_up.shape[1]
    tiles = rows // ROW_TILE
    left = left_half((CLUS, pair_width))
    left_rows = left_half((rows, pair_width))
    down = lax.broadcasted_iota(jnp.int32, (rows, rows), 0)

    @pl.loop(0, HEADS // 2)
    def _(group):
        for step in range(each):
            entry = group * each + step
            pltpu.make_async_copy(arrived.at[fetch[entry]], kv.at[entry], kv_sem.at[group]).start()

    loads = [
        pltpu.make_async_copy(source, target, w_sem.at[at])
        for at, (source, target) in enumerate(
            ((w_out_hbm, w_out), (tok_hbm, tok), (w_up_hbm, w_up), (w_down_hbm, w_down), (cot_hbm, cot))
        )
    ]
    for load in loads:
        load.start()
    stores = []

    def store(source, target):
        copy = pltpu.make_async_copy(source, target, out_sem.at[len(stores)])
        copy.start()
        stores.append(copy)

    @pl.loop(0, HEADS // 2)
    def _(group):
        span = kv.at[pl.ds(group * each, each)]
        pltpu.make_async_copy(span, span, kv_sem.at[group]).wait()
        units = [(odd, cluster) for odd in range(2) for cluster in range(per_dev)]
        clusters = [slice(cluster * CLUS, (cluster + 1) * CLUS) for cluster in range(per_dev)]
        index = [(2 * group + odd) * per_dev + cluster for odd, cluster in units]
        pair = [kv[pl.ds(unit * PAIRS, PAIRS)].reshape(PAIRS * CLUS, pair_width) for unit in index]
        scores = [
            nt(queries[2 * group + odd, clusters[cluster], :], both)
            for (odd, cluster), both in zip(units, pair)
        ]
        exponent = [jnp.exp(value - jnp.max(value, -1, keepdims=True)) for value in scores]
        low = [(value / jnp.sum(value, -1, keepdims=True)).astype(LOW) for value in exponent]
        for (odd, cluster), unit, value, both in zip(units, index, low, pair):
            probs[unit] = value
            value = nn(value, both)
            mixed[odd, clusters[cluster], :] = (
                jnp.where(left, value, 0.0) if odd else jnp.where(left, 0.0, value)
            ).astype(LOW)
        hot = jnp.concatenate([pick(down == order[2 * group + odd]) for odd in range(2)], axis=1)
        both = pltpu.roll(nn(hot, mixed[...].reshape(2 * rows, pair_width)), HEAD_DIM, 1)
        attn[:, pl.ds(pl.multiple_of(group * pair_width, pair_width), pair_width)] = both.astype(LOW)

    store(attn, attn_out)
    loads[0].wait()
    loads[1].wait()
    hidden[...] = nn(attn[...], w_out[...])

    @pl.loop(0, tiles)
    def _(tile):
        at = pl.ds(pl.multiple_of(tile * ROW_TILE, ROW_TILE), ROW_TILE)
        value = hidden[at, :] + (as_row(b_out) + tok[at, :].astype(F32))
        centred = value - jnp.mean(value, -1, keepdims=True)
        scale = lax.rsqrt(jnp.mean(centred * centred, -1, keepdims=True) + 1e-06)
        unit = centred * scale
        z = unit * as_row(gain_one) + as_row(shift_one)
        n_one[at, :] = unit
        r_one[at, :] = scale
        z_low[at, :] = z.astype(LOW)
        z_full[at, :] = z
        hidden[at, :] = z + as_row(b_down)

    store(z_low, z_out)
    loads[2].wait()
    loads[3].wait()

    @pl.loop(0, width // WIDE_FORTH)
    def _(step):
        at = pl.ds(pl.multiple_of(step * WIDE_FORTH, WIDE_FORTH), WIDE_FORTH)
        inner = nn(z_low[...], w_up[:, at]) + b_up[at].astype(F32).reshape(1, WIDE_FORTH)
        normal = 0.5 * (1.0 + lax.erf(inner * 0.7071067811865476))
        density = jnp.exp(inner * inner * -0.5) * 0.3989422804014327
        active[:, at] = (inner * normal).astype(LOW)
        slope[:, at] = (normal + inner * density).astype(LOW)
        hidden[...] += nn(active[:, at], w_down[at, :])

    store(active, active_out)
    loads[4].wait()
    sums[...] = jnp.zeros_like(sums)

    @pl.loop(0, tiles)
    def _(tile):
        at = pl.ds(pl.multiple_of(tile * ROW_TILE, ROW_TILE), ROW_TILE)
        value = hidden[at, :]
        centred = value - jnp.mean(value, -1, keepdims=True)
        scale = lax.rsqrt(jnp.mean(centred * centred, -1, keepdims=True) + 1e-06)
        unit = centred * scale
        final[at, :] = (unit * as_row(gain_two) + as_row(shift_two)).astype(LOW)
        grad = cot[at, :].astype(F32)
        lifted = grad * as_row(gain_two)
        back_grad = scale * (
            lifted - jnp.mean(lifted, -1, keepdims=True) - unit * jnp.mean(lifted * unit, -1, keepdims=True)
        )
        dh2[at, :] = back_grad
        low = back_grad.astype(LOW)
        df[at, :] = low
        sums[0:1, :] += jnp.sum(grad * unit, axis=0, keepdims=True)
        sums[1:2, :] += jnp.sum(grad, axis=0, keepdims=True)
        sums[2:3, :] += jnp.sum(low.astype(F32), axis=0, keepdims=True)

    store(final, layer_out)
    store(df, df_out)
    ones = jnp.ones((8, rows), LOW)

    @pl.loop(0, width // WIDE_BACK)
    def _(step):
        at = pl.ds(pl.multiple_of(step * WIDE_BACK, WIDE_BACK), WIDE_BACK)
        grad = (nt(df[...], w_down[at, :]) * slope[:, at].astype(F32)).astype(LOW)
        slope[:, at] = grad
        total = nn(ones, grad)
        for part in range(WIDE_BACK // D):
            row = 8 + step * (WIDE_BACK // D) + part
            sums[pl.ds(row, 1), :] = total[0:1, part * D : (part + 1) * D]
        dh2[...] += nt(slope[:, at], w_up[:, at])

    store(slope, du_out)

    @pl.loop(0, tiles)
    def _(tile):
        at = pl.ds(pl.multiple_of(tile * ROW_TILE, ROW_TILE), ROW_TILE)
        grad = dh2[at, :]
        unit = n_one[at, :]
        lifted = grad * as_row(gain_one)
        back_grad = r_one[at, :] * (
            lifted - jnp.mean(lifted, -1, keepdims=True) - unit * jnp.mean(lifted * unit, -1, keepdims=True)
        )
        dh1[at, :] = back_grad
        low = back_grad.astype(LOW)
        db[at, :] = low
        sums[3:4, :] += jnp.sum(grad * unit, axis=0, keepdims=True)
        sums[4:5, :] += jnp.sum(grad, axis=0, keepdims=True)
        sums[5:6, :] += jnp.sum(low.astype(F32), axis=0, keepdims=True)

    store(dh1, dh1_out)
    store(db, db_out)
    d_out[...] = nt(db[...], w_out[...]).astype(LOW)

    @pl.loop(0, HEADS // 2)
    def _(group):
        lanes = pl.ds(pl.multiple_of(group * pair_width, pair_width), pair_width)
        tile = d_out[:, lanes]
        grads = []
        for odd in range(2):
            turned = pltpu.roll(nn(pick(down == inverse[2 * group + odd]), tile), HEAD_DIM, 1)
            grads.append((jnp.where(left_rows, turned, 0.0) if odd else jnp.where(left_rows, 0.0, turned)).astype(LOW))
        units = [(odd, cluster) for odd in range(2) for cluster in range(per_dev)]
        clusters = [slice(cluster * CLUS, (cluster + 1) * CLUS) for cluster in range(per_dev)]
        index = [(2 * group + odd) * per_dev + cluster for odd, cluster in units]
        grad = [grads[odd][clusters[cluster]] for odd, cluster in units]
        query = [queries[2 * group + odd, clusters[cluster], :] for odd, cluster in units]
        pair = [kv[pl.ds(unit * PAIRS, PAIRS)].reshape(PAIRS * CLUS, pair_width) for unit in index]
        low = [probs[unit] for unit in index]
        d_probs = [nt(left_, right) for left_, right in zip(grad, pair)]
        wide = [value.astype(F32) for value in low]
        d_scores = [
            (value * (grad_ - jnp.sum(grad_ * value, -1, keepdims=True))).astype(LOW)
            for value, grad_ in zip(wide, d_probs)
        ]
        d_query = [nn(left_, right) * HEAD_DIM ** (-0.5) for left_, right in zip(d_scores, pair)]
        d_pair = [tn(a, b) + tn(c, d) for a, b, c, d in zip(d_scores, query, low, grad)]
        bias = [jnp.zeros((1, pair_width), F32)] * 2
        q_total = jnp.zeros((1, pair_width), F32)
        for (odd, cluster), unit, value, both in zip(units, index, d_query, d_pair):
            value = (jnp.where(left, 0.0, value) if odd else jnp.where(left, value, 0.0)).astype(LOW)
            dq[2 * group + odd, clusters[cluster], :] = value
            q_total += jnp.sum(value.astype(F32), axis=0, keepdims=True)
            bias[odd] += jnp.sum(both, axis=0, keepdims=True)
            kv[pl.ds(unit * PAIRS, PAIRS)] = both.astype(LOW).reshape(PAIRS, CLUS, pair_width)
        for step in range(each):
            entry = group * each + step
            pltpu.make_async_copy(kv.at[entry], back.at[fetch[entry]], back_sem).start()
        both = jnp.where(left_half((1, pair_width)), bias[1], bias[0])
        sums[7:8, lanes] = q_total
        sums[6:7, lanes] = pltpu.roll(jnp.broadcast_to(both, (8, pair_width)), HEAD_DIM, 1)[0:1]

    store(dq, dq_out)
    span = back.at[pl.ds(0, requests)]
    pltpu.make_async_copy(kv, span, back_sem).wait()
    for copy in stores:
        copy.wait()


CHUNKS = 8
VECTORS = 16


def chunk_rows(at, size):
    return pl.ds(pl.multiple_of(at * size, size), size)


def place_chunks(source, target, info, sem, start=1):
    size = source.shape[0] // CHUNKS
    for chunk in range(CHUNKS):
        pltpu.make_async_copy(
            source.at[chunk * size : (chunk + 1) * size],
            target.at[chunk_rows(info[start + chunk], size)],
            sem,
        ).start()


def wait_chunks(source, target, sem):
    pltpu.make_async_copy(source, target, sem).wait()


def core_of(info, side):
    return info[0] if side else 1 - info[0]


def up_kernel(info, z_low, grad, give, keep, turned, buf, sem):
    half = keep.shape[1]
    turned[...] = z_low[...].T
    for side, out in ((0, give), (1, keep)):
        at = pl.ds(pl.multiple_of(core_of(info, side) * half, half), half)
        buf[side] = nn(turned[...], grad[:, at]).astype(LOW)
        place_chunks(buf.at[side], out, info, sem.at[side])
    for side, out in ((0, give), (1, keep)):
        wait_chunks(buf.at[side], out, sem.at[side])


def down_kernel(info, active, grad, give, keep, buf, sem):
    size = keep.shape[0]
    for side, out in ((0, give), (1, keep)):
        for part in range(keep.shape[1] // size):
            block = core_of(info, side) * (keep.shape[1] // size) + part
            at = pl.ds(pl.multiple_of(block * size, size), size)
            buf[side, :, part * size : (part + 1) * size] = nn(active[:, at].T, grad[...]).astype(LOW)
        place_chunks(buf.at[side], out, info, sem.at[side])
    for side, out in ((0, give), (1, keep)):
        wait_chunks(buf.at[side], out, sem.at[side])


def out_q_kernel(info, attn, db, tok, dq, order, sums, give, keep, grad_q, attn_t, tok_t, buf, sem):
    rows = tok.shape[0]
    half = D // 2
    down = lax.broadcasted_iota(jnp.int32, (rows, rows), 0)
    for pair in range(HEADS // 2):
        total = nn(pick(down == order[2 * pair]), dq[2 * pair])
        total += nn(pick(down == order[2 * pair + 1]), dq[2 * pair + 1])
        lanes = slice(pair * 2 * HEAD_DIM, (pair + 1) * 2 * HEAD_DIM)
        grad_q[:, lanes] = total.astype(LOW)
    attn_t[...] = attn[...].T
    tok_t[...] = tok[...].T
    size = D // VECTORS
    filler = jnp.zeros((size - D // LANES, LANES), F32)
    for vector in range(VECTORS):
        rows_of = [sums[vector : vector + 1, row * LANES : (row + 1) * LANES] for row in range(D // LANES)]
        value = jnp.concatenate(rows_of + [filler]).astype(LOW)
        for side in range(2):
            buf[side, vector * size : (vector + 1) * size, D:] = value
    for side, out in ((0, give), (1, keep)):
        at = pl.ds(pl.multiple_of(core_of(info, side) * half, half), half)
        buf[side, :, :half] = nn(attn_t[...], db[:, at]).astype(LOW)
        buf[side, :, half:D] = nn(tok_t[...], grad_q[:, at]).astype(LOW)
        place_chunks(buf.at[side], out, info, sem.at[side])
    for side, out in ((0, give), (1, keep)):
        wait_chunks(buf.at[side], out, sem.at[side])


def key_value_kernel(
    info, segment, returned_hbm, order, tok, key_give, key_keep, value_give, value_keep, grad_kv_hbm,
    returned, total, tok_t, grad_kv, buf, load_sem, kv_sem, sem,
):
    rows = tok.shape[0]
    half = D // 2
    per_dev = rows // CLUS
    pair_width = 2 * HEAD_DIM
    devices = load_sem.shape[0]
    capacity = segment.shape[0] // devices

    def load(device):
        span = pl.ds(device * capacity, capacity)
        return pltpu.make_async_copy(returned_hbm.at[span], returned.at[span], load_sem.at[device])

    @pl.loop(0, devices)
    def _(device):
        load(device).start()

    down = lax.broadcasted_iota(jnp.int32, (rows, rows), 0)
    left = left_half((rows, pair_width))
    total[...] = jnp.zeros_like(total)
    tok_t[...] = tok[...].T

    @pl.loop(0, devices)
    def _(device):
        load(device).wait()
        for step in range(capacity):
            slot = device * capacity + step
            block = segment[slot]
            total[block] += returned[slot].astype(F32)

    for quad in range(HEADS // 4):
        pairs = range(2 * quad, 2 * quad + 2)
        heads = range(4 * quad, 4 * quad + 4)
        hots = [pick(down == order[head]) for head in heads]
        summed = [
            total[head * per_dev : (head + 1) * per_dev].reshape(rows, pair_width).astype(LOW) for head in heads
        ]
        placed = [nn(hot, value) for hot, value in zip(hots, summed)]
        for at, pair in enumerate(pairs):
            even, odd = placed[2 * at], placed[2 * at + 1]
            grad_kv[:, pair * pair_width : (pair + 1) * pair_width] = jnp.where(left, even, odd).astype(LOW)
            values = pltpu.roll(jnp.where(left, odd, even), HEAD_DIM, 1)
            grad_kv[:, D + pair * pair_width : D + (pair + 1) * pair_width] = values.astype(LOW)
    stored = pltpu.make_async_copy(grad_kv, grad_kv_hbm, kv_sem)
    stored.start()
    outs = ((key_give, key_keep), (value_give, value_keep))
    for side in range(2):
        base = core_of(info, side) * half
        parts = [grad_kv[:, pl.ds(pl.multiple_of(part * D + base, half), half)] for part in range(2)]
        value = nn(tok_t[...], jnp.concatenate(parts, axis=1)).astype(LOW)
        for part in range(2):
            buf[part, side] = value[:, part * half : (part + 1) * half]
            place_chunks(buf.at[part, side], outs[part][side], info, sem.at[part, side], 33 if part else 1)
    for side in range(2):
        for part in range(2):
            wait_chunks(buf.at[part, side], outs[part][side], sem.at[part, side])
    stored.wait()


def spread_start(info, start, pieces, targets, buf, sem):
    size = buf.shape[2]
    copies = []
    for at, piece in enumerate(pieces):
        core = core_of(info, 1 - at)
        for chunk in range(buf.shape[1]):
            buf[at, chunk] = piece[chunk * size : (chunk + 1) * size].astype(F32)
            for lanes, target in targets(core, chunk_rows(info[start + chunk], size)):
                copies.append(pltpu.make_async_copy(buf.at[at, chunk, :, lanes], target, sem))
                copies[-1].start()
    return copies


def up_targets(out, half):
    def targets(core, rows):
        yield pl.ds(0, half), out.at[rows, pl.ds(pl.multiple_of(core * half, half), half)]

    return targets


def down_targets(out, half):
    parts = half // D

    def targets(core, rows):
        for part in range(parts):
            yield pl.ds(part * D, D), out.at[core * parts + part, rows]

    return targets


def attention_targets(w_out, w_qkv):
    half = D // 2

    def targets(core, rows):
        at = pl.ds(pl.multiple_of(core * half, half), half)
        yield pl.ds(0, half), w_out.at[rows, at]
        for part, lane in enumerate((half, D + LANES, D + LANES + half)):
            to = pl.ds(pl.multiple_of(part * D + core * half, half), half)
            yield pl.ds(lane, half), w_qkv.at[rows, to]

    return targets


def spread_groups(groups, info, pieces, outs, staged, bufs, load_sem, sem):
    w_up, w_down, w_out, w_qkv = outs
    half = w_up.shape[1] // 2
    routes = (up_targets(w_up, half), down_targets(w_down, half), attention_targets(w_out, w_qkv))
    loads = []
    for at, (source, target) in enumerate(zip(pieces, staged)):
        loads.append(pltpu.make_async_copy(source, target, load_sem.at[at]))
        loads[-1].start()
    copies = []
    for at, (third, start) in enumerate(groups):
        for load in loads[2 * at : 2 * at + 2]:
            load.wait()
        copies += spread_start(info, start, staged[2 * at : 2 * at + 2], routes[third], bufs[at], sem.at[at])
    return copies


def spread_kernel(groups, info, *refs):
    pairs = len(groups)
    pieces, scratch = refs[: 2 * pairs], refs[-3 * pairs - 2 :]
    outs = refs[-3 * pairs - 6 : -3 * pairs - 2]
    staged, bufs = scratch[: 2 * pairs], scratch[2 * pairs : 3 * pairs]
    for copy in spread_groups(groups, info, pieces, outs, staged, bufs, *scratch[3 * pairs :]):
        copy.wait()


def spread_last_kernel(groups, start, info, *refs):
    pairs = len(groups)
    pieces, sources = refs[: 2 * pairs], refs[2 * pairs : 2 * pairs + 4]
    rest = refs[2 * pairs + 8 :]
    outs, vectors, rest = rest[:4], rest[4:13], rest[13:]
    staged, bufs = rest[: 2 * pairs], rest[2 * pairs : 3 * pairs]
    load_sem, sem, columns, table, column_sem = rest[3 * pairs :]
    loads = [
        pltpu.make_async_copy(source.at[:, D : D + LANES], columns.at[at], column_sem.at[at])
        for at, source in enumerate(sources)
    ]
    for load in loads:
        load.start()
    copies = spread_groups(groups, info, pieces, outs, staged, bufs, load_sem, sem)
    size = D // VECTORS
    each = CHUNKS // len(sources)
    inside = VECTORS // CHUNKS
    for at, load in enumerate(loads):
        load.wait()
        for row in range(each * inside):
            vector = info[start + at * each + row // inside] * inside + row % inside
            table[vector] = columns[at, row * size : row * size + 16].astype(F32)

    def whole(vector):
        return jnp.concatenate([table[vector, row : row + 1] for row in range(D // LANES)], axis=1)

    for at, vector in enumerate(vectors):
        count = vector.shape[0] // D
        vector[...] = jnp.concatenate([whole(at + part) for part in range(count)], axis=1).reshape(count * D)
    for copy in copies:
        copy.wait()


X, Y, Z = ("dp", 1), ("blk", 2), ("blk", 4)
CORE = ("blk", 1)
ORDERS = ((Z, Y, X), (X, Z, Y), (Y, X, Z))


def swap(value, bit):
    axis, distance = bit
    size = lax.axis_size(axis)
    return lax.ppermute(value, axis, [(i, i ^ distance) for i in range(size)])


def further_bits(count_blk):
    bits = []
    distance = 8
    while distance < count_blk:
        bits.append(("blk", distance))
        distance *= 2
    return bits


def chunk_places():
    x, y, z = [(lax.axis_index(axis) // distance) % 2 for axis, distance in (X, Y, Z)]
    chip = x * 4 + y * 2 + z
    core = lax.axis_index("blk") % 2
    every = jnp.arange(CHUNKS, dtype=jnp.int32)
    value = {X: 4, Y: 2, Z: 1}

    def from_order(order):
        at = sum(((every // 2**step) % 2) * value[bit] for step, bit in enumerate(order))
        return at ^ chip

    placed = every ^ chip
    x_y_swapped = placed % 2 + (placed // 4) * 2 + (placed // 2 % 2) * 4
    return jnp.concatenate(
        [core[None], placed] + [from_order(order) for order in ORDERS] + [x_y_swapped]
    )


def sum_rows(terms, low, high):
    total = terms[0][low:high].astype(F32)
    for term in terms[1:]:
        total = total + term[low:high].astype(F32)
    return total


def to_send(terms):
    rows = min(term.shape[0] for term in terms)
    return sum_rows(terms, rows // 2, rows).astype(LOW)


def scatter_steps(terms, bits):
    for bit in bits:
        terms = terms + [swap(to_send(terms), bit)]
    return terms


def finish(terms, further):
    value = sum_rows(terms, 0, terms[-1].shape[0]).astype(LOW)
    for bit in further:
        value = sum_rows([value, swap(value, bit)], 0, value.shape[0]).astype(LOW)
    return value


def tie(values):
    return lax.optimization_barrier(tuple(values))


def gather_step(value, bit):
    return jnp.concatenate([value, swap(value, bit)])


def per_device(
    tokens,
    w_qkv,
    b_query,
    b_value,
    w_out,
    b_out,
    gain_one,
    shift_one,
    w_up,
    b_up,
    w_down,
    b_down,
    gain_two,
    shift_two,
    cluster_perm,
    cluster_pairs,
    cotangent,
):
    count_blk = lax.axis_size("blk")
    my_index = lax.axis_index("blk")
    rows = tokens.shape[0]
    per_dev = rows // CLUS
    blocks = HEADS * per_dev
    requests = blocks * PAIRS
    capacity = max(2, (requests + count_blk - 1) // count_blk + 1)
    slots = count_blk * capacity
    pair_width = 2 * HEAD_DIM
    ff = w_up.shape[1]
    local_order = cluster_perm[0] - my_index * rows
    order_rows = local_order[:, None, :]

    wanted = (
        cluster_pairs[0]
        .reshape(HEADS, count_blk, per_dev, PAIRS)
        .transpose(1, 0, 2, 3)
        .reshape(count_blk, requests)
    )
    positions = jnp.arange(requests, dtype=jnp.int32)
    before = positions[:, None] < positions[None, :]
    source = wanted // per_dev
    named = source == my_index
    rank = jnp.sum(named[:, :, None] & before[None], axis=1)
    head_of = positions // (per_dev * PAIRS)
    block_id = head_of[None, :] * per_dev + wanted % per_dev
    matches = named[:, :, None] & (
        rank[:, :, None] == jnp.arange(capacity, dtype=jnp.int32)[None, None, :]
    )
    chosen = jnp.sum(jnp.where(matches, block_id[:, :, None], 0), axis=1)

    smem = pl.BlockSpec(memory_space=pltpu.SMEM)
    vmem = pl.BlockSpec(memory_space=pltpu.VMEM)
    hbm = pl.BlockSpec(memory_space=pl.ANY)

    def column_block(at):
        return pl.BlockSpec((D, D), lambda step: (0, at))

    outgoing = pl.pallas_call(
        kv_kernel,
        grid=(1,),
        out_shape=jax.ShapeDtypeStruct((slots, CLUS, pair_width), LOW),
        in_specs=[vmem, column_block(1), column_block(2), vmem, vmem, vmem],
        out_specs=hbm,
        scratch_shapes=[
            pltpu.VMEM((blocks, CLUS, pair_width), LOW),
            pltpu.SMEM(chosen.shape, jnp.int32),
            pltpu.SemaphoreType.DMA,
            pltpu.SemaphoreType.DMA,
        ],
        compiler_params=params(),
        name="kv_kernel",
    )(tokens, w_qkv, w_qkv, b_value, cluster_perm, chosen)
    arrived = lax.all_to_all(
        outgoing.reshape(count_blk, capacity, CLUS, pair_width),
        "blk",
        split_axis=0,
        concat_axis=0,
        tiled=True,
    ).reshape(slots, CLUS, pair_width)

    info = chunk_places()
    queries = pl.pallas_call(
        q_kernel,
        grid=(1,),
        out_shape=jax.ShapeDtypeStruct((HEADS, rows, pair_width), LOW),
        in_specs=[vmem, column_block(0), vmem, vmem],
        out_specs=vmem,
        compiler_params=params(),
        name="q_kernel",
    )(tokens, w_qkv, b_query, cluster_perm)
    filled = jnp.any(matches, axis=1)
    segment = jnp.where(filled, chosen, blocks).reshape(-1)
    my_source = lax.dynamic_index_in_dim(wanted, my_index, 0, keepdims=False) // per_dev
    my_rank = jnp.sum((my_source[:, None] == my_source[None, :]) & before, axis=0)
    fetch = my_source * capacity + my_rank
    places = jnp.arange(rows, dtype=jnp.int32)
    inverse = jnp.sum(
        jnp.where(local_order[:, :, None] == places, places[None, :, None], 0), axis=1
    )[:, None, :]
    def low(*shape):
        return jax.ShapeDtypeStruct(shape, LOW)

    def full(*shape):
        return jax.ShapeDtypeStruct(shape, F32)

    (
        back, dq_sorted, attn, normed, active, grad_inner, grad_second, grad_branch, grad_resid,
        layer_out, sums,
    ) = pl.pallas_call(
        mid_kernel,
        out_shape=(
            low(slots, CLUS, pair_width), low(HEADS, rows, pair_width), low(rows, D), low(rows, D),
            low(rows, ff), low(rows, ff), low(rows, D), low(rows, D), full(rows, D), low(rows, D),
            full(16, D),
        ),
        in_specs=[smem, vmem, hbm, vmem, vmem, hbm, hbm] + [vmem] * 7 + [hbm] * 3,
        out_specs=(hbm,) * 10 + (vmem,),
        scratch_shapes=[
            pltpu.VMEM((requests, CLUS, pair_width), LOW),
            pltpu.VMEM((blocks, CLUS, PAIRS * CLUS), LOW),
            pltpu.VMEM((rows, D), LOW),
            pltpu.VMEM((2, rows, pair_width), LOW),
            pltpu.VMEM((D, D), LOW),
            pltpu.VMEM((D, ff), LOW),
            pltpu.VMEM((ff, D), LOW),
            pltpu.VMEM((rows, D), F32),
            pltpu.VMEM((rows, D), F32),
            pltpu.VMEM((rows, D), F32),
            pltpu.VMEM((rows, 1), F32),
            pltpu.VMEM((rows, D), LOW),
            pltpu.VMEM((rows, ff), LOW),
            pltpu.VMEM((rows, ff), LOW),
            pltpu.VMEM((rows, D), F32),
            pltpu.VMEM((rows, D), LOW),
            pltpu.VMEM((rows, D), LOW),
            pltpu.VMEM((rows, D), LOW),
            pltpu.VMEM((rows, D), F32),
            pltpu.VMEM((rows, D), LOW),
            pltpu.VMEM((HEADS, rows, pair_width), LOW),
            pltpu.VMEM((rows, D), LOW),
            pltpu.VMEM((rows, D), LOW),
            pltpu.SemaphoreType.DMA((HEADS // 2,)),
            pltpu.SemaphoreType.DMA((5,)),
            pltpu.SemaphoreType.DMA((9,)),
            pltpu.SemaphoreType.DMA,
        ],
        compiler_params=params(),
        name="mid_kernel",
    )(
        fetch, queries, arrived, order_rows, inverse, tokens, cotangent,
        b_out, gain_one, shift_one, b_up, b_down, gain_two, shift_two, w_out, w_up, w_down,
    )
    returned = lax.all_to_all(
        back.reshape(count_blk, capacity, CLUS, pair_width),
        "blk",
        split_axis=0,
        concat_axis=0,
        tiled=True,
    ).reshape(slots, CLUS, pair_width)

    further = further_bits(count_blk)

    def halves(kernel, operands, columns, scratch, more=(), name=None):
        return pl.pallas_call(
            kernel,
            out_shape=(low(D, columns), low(D, columns)) + more,
            in_specs=[smem] + [vmem] * (len(operands) - 1),
            out_specs=(hbm, hbm) + (vmem,) * len(more),
            scratch_shapes=scratch
            + [pltpu.VMEM((2, D, columns), LOW), pltpu.SemaphoreType.DMA((2,))],
            compiler_params=params(),
            cost_estimate=pl.CostEstimate(flops=1, bytes_accessed=1, transcendentals=0),
            name=name,
        )(*operands)

    half = D // 2
    turned = pltpu.VMEM((D, rows), LOW)
    up_give, up_keep = halves(
        up_kernel, (info, normed, grad_inner), ff // 2, [turned], name="up_kernel"
    )
    down_give, down_keep = halves(
        down_kernel, (info, active, grad_second), ff // 2, [], name="down_kernel"
    )
    up = [up_keep, swap(up_give, CORE)]
    up_step, attn = tie((to_send(up), attn))
    oq_give, oq_keep, grad_q = halves(
        out_q_kernel,
        (info, attn, grad_branch, tokens, dq_sorted, order_rows, sums),
        D + LANES,
        [turned, turned],
        (low(rows, D),),
        name="out_q_kernel",
    )
    up = scatter_steps(up + [swap(up_step, X)], (Y,))
    down = scatter_steps([down_keep, swap(down_give, CORE)], (X,))
    out_q = scatter_steps([oq_keep, swap(oq_give, CORE)], (X,))
    up_step = to_send(up)
    up_step, down[-1] = tie((up_step, down[-1]))
    down_step = to_send(down)

    returned, up_step, down_step, out_q[-1] = tie((returned, up_step, down_step, out_q[-1]))
    up = up + [swap(up_step, Z)]
    down = down + [swap(down_step, Y)]
    out_q = scatter_steps(out_q, (Y,))
    key_give, key_keep, value_give, value_keep, grad_kv = pl.pallas_call(
        key_value_kernel,
        out_shape=(low(D, half),) * 4 + (low(rows, 2 * D),),
        in_specs=[smem, smem, hbm, vmem, vmem],
        out_specs=(hbm,) * 5,
        scratch_shapes=[
            pltpu.VMEM((slots, CLUS, pair_width), LOW),
            pltpu.VMEM((blocks + 1, CLUS, pair_width), F32),
            turned,
            pltpu.VMEM((rows, 2 * D), LOW),
            pltpu.VMEM((2, 2, D, half), LOW),
            pltpu.SemaphoreType.DMA((count_blk,)),
            pltpu.SemaphoreType.DMA,
            pltpu.SemaphoreType.DMA((2, 2)),
        ],
        compiler_params=params(),
        name="key_value_kernel",
    )(info, segment, returned, order_rows, tokens)
    down[-1], key_give, value_give = tie((down[-1], key_give, value_give))
    key = scatter_steps([key_keep, swap(key_give, CORE)], (X, Y))
    value = scatter_steps([value_keep, swap(value_give, CORE)], (Y, X))
    late_given = swap(jnp.concatenate([to_send(key), to_send(value)], axis=1), Z)
    key = key + [late_given[:, :half]]
    value = value + [late_given[:, half:]]
    up = finish(up, further)
    down = finish(scatter_steps(down, (Z,)), further)
    out_q = finish(scatter_steps(out_q, (Z,)), further)
    both = jnp.concatenate([sum_rows(terms, 0, terms[-1].shape[0]) for terms in (key, value)], axis=1)
    both = finish([both.astype(LOW)], further)
    thirds = (up, down, jnp.concatenate([out_q, both], axis=1))

    starts = (9, 17, 25)
    weights = (full(D, ff), full(ff // D, D, D), full(D, D), full(D, 3 * D))

    def swap_all(values, step):
        return [swap(value, order[step]) for value, order in zip(values, ORDERS)]

    def spread_scratch(pieces):
        rows_each = D // CHUNKS
        return (
            [pltpu.VMEM(piece.shape, LOW) for piece in pieces]
            + [
                pltpu.VMEM((2, piece.shape[0] // rows_each, rows_each, piece.shape[1]), F32)
                for piece in pieces[::2]
            ]
            + [
                pltpu.SemaphoreType.DMA((len(pieces),)),
                pltpu.SemaphoreType.DMA((len(pieces) // 2,)),
            ]
        )

    def with_other(sets):
        return [array for value in sets for array in (value, swap(value, CORE))]

    def spread(sets, offsets, outs=()):
        pieces = with_other(sets)
        groups = tuple((third, starts[third] + offset) for offset in offsets for third in range(3))
        return pl.pallas_call(
            partial(spread_kernel, groups),
            out_shape=weights,
            in_specs=[smem] + [hbm] * (len(pieces) + len(outs)),
            out_specs=(hbm,) * 4,
            scratch_shapes=spread_scratch(pieces),
            input_output_aliases={1 + len(pieces) + at: at for at in range(len(outs))},
            compiler_params=params(),
            name="spread",
        )(info, *pieces, *outs)

    thirds = list(tie(gather_step(value, order[0]) for value, order in zip(thirds, ORDERS)))
    third_step = swap_all(thirds, 1)
    fourth_step = swap_all(thirds, 2)
    outs = spread(thirds, (0,))
    tied = tie((*third_step, grad_kv))
    third_step, grad_kv = list(tied[:3]), tied[3]
    last_step = swap_all(third_step, 2)
    grad_proj = jnp.concatenate([grad_q, grad_kv], axis=1)
    grad_tokens = (grad_resid + nt(grad_proj, w_qkv)).astype(LOW)
    tied = tie((*fourth_step, *outs, grad_tokens))
    fourth_step, outs, grad_tokens = list(tied[:3]), tied[3:7], tied[7]
    outs = spread(third_step + fourth_step, (2, 4), outs)
    tied = tie((*last_step, *outs))
    last_step, outs = list(tied[:3]), tied[3:]
    pieces = with_other(last_step)
    sum_up, sum_down, sum_out, sum_qkv, *vectors = pl.pallas_call(
        partial(spread_last_kernel, tuple((third, starts[third] + 6) for third in range(3)), starts[2]),
        out_shape=weights + (full(D),) * 8 + (full(ff),),
        in_specs=[smem] + [hbm] * (len(pieces) + 8),
        out_specs=(hbm,) * 4 + (vmem,) * 9,
        scratch_shapes=spread_scratch(pieces)
        + [
            pltpu.VMEM((4, D // 4, LANES), LOW),
            pltpu.VMEM((VECTORS, 16, LANES), F32),
            pltpu.SemaphoreType.DMA((4,)),
        ],
        input_output_aliases={1 + len(pieces) + 4 + at: at for at in range(4)},
        compiler_params=params(),
        name="spread_last",
    )(info, *pieces, thirds[2], third_step[2], fourth_step[2], last_step[2], *outs)
    return (
        layer_out,
        grad_tokens,
        sum_qkv,
        vectors[7],
        vectors[6],
        sum_out,
        vectors[5],
        vectors[3],
        vectors[4],
        sum_up,
        vectors[8],
        sum_down.reshape(ff, D),
        vectors[2],
        vectors[0],
        vectors[1],
    )


def solution(mesh):
    whole = P()
    rows = P(("dp", "blk"), None)
    return jax.shard_map(
        per_device,
        mesh=mesh,
        in_specs=(
            (rows,)
            + (whole,) * 13
            + (P("dp", None, "blk"), P("dp", None, None, None), rows)
        ),
        out_specs=(rows, rows) + (whole,) * 13,
        check_vma=False,
    )
```

```python
from functools import partial

import jax
import jax.numpy as jnp
from jax import lax
from jax.experimental import pallas as pl
from jax.experimental.pallas import tpu as pltpu
from jax.sharding import PartitionSpec as P

D = 768
HEADS = 12
HEAD_DIM = 64
CLUS = 128
PAIRS = 2
LANES = 128

F32 = jnp.float32
LOW = jnp.bfloat16


def nn(left, right):
    return jnp.dot(left, right, preferred_element_type=F32)


def nt(left, right):
    return lax.dot_general(left, right, (((1,), (1,)), ((), ())), preferred_element_type=F32)


def tn(left, right):
    return lax.dot_general(left, right, (((0,), (0,)), ((), ())), preferred_element_type=F32)


def as_row(vector):
    return vector[...].astype(F32).reshape(1, vector.shape[0])


def left_half(shape):
    return lax.broadcasted_iota(jnp.int32, shape, 1) < HEAD_DIM


def pick(hot):
    return jnp.where(hot, 1.0, 0.0).astype(LOW)


def params(megabytes=60):
    return pltpu.CompilerParams(vmem_limit_bytes=megabytes << 20)


def columns_of(perm, rows):
    local = lax.rem(perm, rows)
    return jnp.concatenate([local, local[: 16 - HEADS]]).T


def kv_kernel(tok, w_key, w_value, b_value, perm, chosen_in, out, blocks, chosen, chosen_sem, sem):
    fetch = pltpu.make_async_copy(chosen_in, chosen, chosen_sem)
    fetch.start()
    rows = tok.shape[0]
    order = columns_of(perm[0], rows)
    per_dev = rows // CLUS
    place = lax.broadcasted_iota(jnp.int32, (rows, rows), 1)
    left = left_half((rows, 2 * HEAD_DIM))
    inputs = tok[...]
    keys = nn(inputs, w_key[...])
    values = nn(inputs, w_value[...]) + as_row(b_value)
    joined = []
    for pair in range(HEADS // 2):
        two = slice(pair * 2 * HEAD_DIM, (pair + 1) * 2 * HEAD_DIM)
        key_two = keys[:, two]
        value_two = pltpu.roll(values[:, two], HEAD_DIM, 1)
        joined.append(jnp.where(left, key_two, value_two).astype(LOW))
        joined.append(jnp.where(left, value_two, key_two).astype(LOW))
    for quad in range(HEADS // 4):
        heads = range(quad * 4, quad * 4 + 4)
        hot = [pick(order[:, head : head + 1] == place) for head in heads]
        ranked = [nn(one, joined[head]).astype(LOW) for one, head in zip(hot, heads)]
        for head, value in zip(heads, ranked):
            blocks[head * per_dev : (head + 1) * per_dev] = value.reshape(per_dev, CLUS, 2 * HEAD_DIM)
    fetch.wait()
    devices, capacity = chosen.shape

    @pl.loop(0, devices)
    def _(device):
        for slot in range(capacity):
            pltpu.make_async_copy(
                blocks.at[chosen[device, slot]], out.at[device * capacity + slot], sem
            ).start()

    pltpu.make_async_copy(out, out, sem).wait()


def q_kernel(tok, w_query, b_query, perm, out):
    rows = tok.shape[0]
    order = columns_of(perm[0], rows)
    place = lax.broadcasted_iota(jnp.int32, (rows, rows), 1)
    left = left_half((rows, 2 * HEAD_DIM))
    inputs = tok[...]
    for quad in range(HEADS // 4):
        four = slice(quad * 4 * HEAD_DIM, (quad + 1) * 4 * HEAD_DIM)
        queries = nn(inputs, w_query[:, four]) + as_row(b_query)[:, four]
        queries = (queries.astype(LOW).astype(F32) * HEAD_DIM ** (-0.5)).astype(LOW)
        for pair in range(2):
            two = queries[:, pair * 2 * HEAD_DIM : (pair + 1) * 2 * HEAD_DIM]
            for odd in range(2):
                head = quad * 4 + pair * 2 + odd
                hot = pick(order[:, head : head + 1] == place)
                ranked = nn(hot, two)
                kept = jnp.where(left, 0.0, ranked) if odd else jnp.where(left, ranked, 0.0)
                out[head] = kept.astype(LOW)


ROW_TILE = 512
WIDE = 768
WIDE_FORTH = 1024
WIDE_BACK = 1536


def mid_kernel(
    fetch, queries, arrived, order, inverse, tok_hbm, cot_hbm,
    b_out, gain_one, shift_one, b_up, b_down, gain_two, shift_two, w_out_hbm, w_up_hbm, w_down_hbm,
    back, dq_out, attn_out, z_out, active_out, du_out, df_out, db_out, dh1_out, layer_out, sums,
    kv, probs, attn, mixed, w_out, w_up, w_down, hidden, z_full, n_one, r_one, z_low, active, slope,
    dh2, df, db, d_out, dh1, final, dq, tok, cot, kv_sem, w_sem, out_sem, back_sem,
):
    rows = tok_hbm.shape[0]
    per_dev = rows // CLUS
    pair_width = 2 * HEAD_DIM
    requests = fetch.shape[0]
    each = 2 * per_dev * PAIRS
    width = w_up.shape[1]
    tiles = rows // ROW_TILE
    left = left_half((CLUS, pair_width))
    left_rows = left_half((rows, pair_width))
    down = lax.broadcasted_iota(jnp.int32, (rows, rows), 0)

    @pl.loop(0, HEADS // 2)
    def _(group):
        for step in range(each):
            entry = group * each + step
            pltpu.make_async_copy(arrived.at[fetch[entry]], kv.at[entry], kv_sem.at[group]).start()

    loads = [
        pltpu.make_async_copy(source, target, w_sem.at[at])
        for at, (source, target) in enumerate(
            ((w_out_hbm, w_out), (tok_hbm, tok), (w_up_hbm, w_up), (w_down_hbm, w_down), (cot_hbm, cot))
        )
    ]
    for load in loads:
        load.start()
    stores = []

    def store(source, target):
        copy = pltpu.make_async_copy(source, target, out_sem.at[len(stores)])
        copy.start()
        stores.append(copy)

    @pl.loop(0, HEADS // 2)
    def _(group):
        span = kv.at[pl.ds(group * each, each)]
        pltpu.make_async_copy(span, span, kv_sem.at[group]).wait()
        units = [(odd, cluster) for odd in range(2) for cluster in range(per_dev)]
        clusters = [slice(cluster * CLUS, (cluster + 1) * CLUS) for cluster in range(per_dev)]
        index = [(2 * group + odd) * per_dev + cluster for odd, cluster in units]
        pair = [kv[pl.ds(unit * PAIRS, PAIRS)].reshape(PAIRS * CLUS, pair_width) for unit in index]
        scores = [
            nt(queries[2 * group + odd, clusters[cluster], :], both)
            for (odd, cluster), both in zip(units, pair)
        ]
        exponent = [jnp.exp(value - jnp.max(value, -1, keepdims=True)) for value in scores]
        low = [(value / jnp.sum(value, -1, keepdims=True)).astype(LOW) for value in exponent]
        for (odd, cluster), unit, value, both in zip(units, index, low, pair):
            probs[unit] = value
            value = nn(value, both)
            mixed[odd, clusters[cluster], :] = (
                jnp.where(left, value, 0.0) if odd else jnp.where(left, 0.0, value)
            ).astype(LOW)
        hot = jnp.concatenate([pick(down == order[2 * group + odd]) for odd in range(2)], axis=1)
        both = pltpu.roll(nn(hot, mixed[...].reshape(2 * rows, pair_width)), HEAD_DIM, 1)
        attn[:, pl.ds(pl.multiple_of(group * pair_width, pair_width), pair_width)] = both.astype(LOW)

    store(attn, attn_out)
    loads[0].wait()
    loads[1].wait()
    hidden[...] = nn(attn[...], w_out[...])

    @pl.loop(0, tiles)
    def _(tile):
        at = pl.ds(pl.multiple_of(tile * ROW_TILE, ROW_TILE), ROW_TILE)
        value = hidden[at, :] + (as_row(b_out) + tok[at, :].astype(F32))
        centred = value - jnp.mean(value, -1, keepdims=True)
        scale = lax.rsqrt(jnp.mean(centred * centred, -1, keepdims=True) + 1e-06)
        unit = centred * scale
        z = unit * as_row(gain_one) + as_row(shift_one)
        n_one[at, :] = unit
        r_one[at, :] = scale
        z_low[at, :] = z.astype(LOW)
        z_full[at, :] = z
        hidden[at, :] = z + as_row(b_down)

    store(z_low, z_out)
    loads[2].wait()
    loads[3].wait()

    @pl.loop(0, width // WIDE_FORTH)
    def _(step):
        at = pl.ds(pl.multiple_of(step * WIDE_FORTH, WIDE_FORTH), WIDE_FORTH)
        inner = nn(z_low[...], w_up[:, at]) + b_up[at].astype(F32).reshape(1, WIDE_FORTH)
        normal = 0.5 * (1.0 + lax.erf(inner * 0.7071067811865476))
        density = jnp.exp(inner * inner * -0.5) * 0.3989422804014327
        active[:, at] = (inner * normal).astype(LOW)
        slope[:, at] = (normal + inner * density).astype(LOW)
        hidden[...] += nn(active[:, at], w_down[at, :])

    store(active, active_out)
    loads[4].wait()
    sums[...] = jnp.zeros_like(sums)

    @pl.loop(0, tiles)
    def _(tile):
        at = pl.ds(pl.multiple_of(tile * ROW_TILE, ROW_TILE), ROW_TILE)
        value = hidden[at, :]
        centred = value - jnp.mean(value, -1, keepdims=True)
        scale = lax.rsqrt(jnp.mean(centred * centred, -1, keepdims=True) + 1e-06)
        unit = centred * scale
        final[at, :] = (unit * as_row(gain_two) + as_row(shift_two)).astype(LOW)
        grad = cot[at, :].astype(F32)
        lifted = grad * as_row(gain_two)
        back_grad = scale * (
            lifted - jnp.mean(lifted, -1, keepdims=True) - unit * jnp.mean(lifted * unit, -1, keepdims=True)
        )
        dh2[at, :] = back_grad
        low = back_grad.astype(LOW)
        df[at, :] = low
        sums[0:1, :] += jnp.sum(grad * unit, axis=0, keepdims=True)
        sums[1:2, :] += jnp.sum(grad, axis=0, keepdims=True)
        sums[2:3, :] += jnp.sum(low.astype(F32), axis=0, keepdims=True)

    store(final, layer_out)
    store(df, df_out)
    ones = jnp.ones((8, rows), LOW)

    @pl.loop(0, width // WIDE_BACK)
    def _(step):
        at = pl.ds(pl.multiple_of(step * WIDE_BACK, WIDE_BACK), WIDE_BACK)
        grad = (nt(df[...], w_down[at, :]) * slope[:, at].astype(F32)).astype(LOW)
        slope[:, at] = grad
        total = nn(ones, grad)
        for part in range(WIDE_BACK // D):
            row = 8 + step * (WIDE_BACK // D) + part
            sums[pl.ds(row, 1), :] = total[0:1, part * D : (part + 1) * D]
        dh2[...] += nt(slope[:, at], w_up[:, at])

    store(slope, du_out)

    @pl.loop(0, tiles)
    def _(tile):
        at = pl.ds(pl.multiple_of(tile * ROW_TILE, ROW_TILE), ROW_TILE)
        grad = dh2[at, :]
        unit = n_one[at, :]
        lifted = grad * as_row(gain_one)
        back_grad = r_one[at, :] * (
            lifted - jnp.mean(lifted, -1, keepdims=True) - unit * jnp.mean(lifted * unit, -1, keepdims=True)
        )
        dh1[at, :] = back_grad
        low = back_grad.astype(LOW)
        db[at, :] = low
        sums[3:4, :] += jnp.sum(grad * unit, axis=0, keepdims=True)
        sums[4:5, :] += jnp.sum(grad, axis=0, keepdims=True)
        sums[5:6, :] += jnp.sum(low.astype(F32), axis=0, keepdims=True)

    store(dh1, dh1_out)
    store(db, db_out)
    d_out[...] = nt(db[...], w_out[...]).astype(LOW)

    @pl.loop(0, HEADS // 2)
    def _(group):
        lanes = pl.ds(pl.multiple_of(group * pair_width, pair_width), pair_width)
        tile = d_out[:, lanes]
        grads = []
        for odd in range(2):
            turned = pltpu.roll(nn(pick(down == inverse[2 * group + odd]), tile), HEAD_DIM, 1)
            grads.append((jnp.where(left_rows, turned, 0.0) if odd else jnp.where(left_rows, 0.0, turned)).astype(LOW))
        units = [(odd, cluster) for odd in range(2) for cluster in range(per_dev)]
        clusters = [slice(cluster * CLUS, (cluster + 1) * CLUS) for cluster in range(per_dev)]
        index = [(2 * group + odd) * per_dev + cluster for odd, cluster in units]
        grad = [grads[odd][clusters[cluster]] for odd, cluster in units]
        query = [queries[2 * group + odd, clusters[cluster], :] for odd, cluster in units]
        pair = [kv[pl.ds(unit * PAIRS, PAIRS)].reshape(PAIRS * CLUS, pair_width) for unit in index]
        low = [probs[unit] for unit in index]
        d_probs = [nt(left_, right) for left_, right in zip(grad, pair)]
        wide = [value.astype(F32) for value in low]
        d_scores = [
            (value * (grad_ - jnp.sum(grad_ * value, -1, keepdims=True))).astype(LOW)
            for value, grad_ in zip(wide, d_probs)
        ]
        d_query = [nn(left_, right) * HEAD_DIM ** (-0.5) for left_, right in zip(d_scores, pair)]
        d_pair = [tn(a, b) + tn(c, d) for a, b, c, d in zip(d_scores, query, low, grad)]
        bias = [jnp.zeros((1, pair_width), F32)] * 2
        q_total = jnp.zeros((1, pair_width), F32)
        for (odd, cluster), unit, value, both in zip(units, index, d_query, d_pair):
            value = (jnp.where(left, 0.0, value) if odd else jnp.where(left, value, 0.0)).astype(LOW)
            dq[2 * group + odd, clusters[cluster], :] = value
            q_total += jnp.sum(value.astype(F32), axis=0, keepdims=True)
            bias[odd] += jnp.sum(both, axis=0, keepdims=True)
            kv[pl.ds(unit * PAIRS, PAIRS)] = both.astype(LOW).reshape(PAIRS, CLUS, pair_width)
        for step in range(each):
            entry = group * each + step
            pltpu.make_async_copy(kv.at[entry], back.at[fetch[entry]], back_sem).start()
        both = jnp.where(left_half((1, pair_width)), bias[1], bias[0])
        sums[7:8, lanes] = q_total
        sums[6:7, lanes] = pltpu.roll(jnp.broadcast_to(both, (8, pair_width)), HEAD_DIM, 1)[0:1]

    store(dq, dq_out)
    span = back.at[pl.ds(0, requests)]
    pltpu.make_async_copy(kv, span, back_sem).wait()
    for copy in stores:
        copy.wait()


CHUNKS = 8
VECTORS = 16


def chunk_rows(at, size):
    return pl.ds(pl.multiple_of(at * size, size), size)


def place_chunks(source, target, info, sem, start=1):
    size = source.shape[0] // CHUNKS
    for chunk in range(CHUNKS):
        pltpu.make_async_copy(
            source.at[chunk * size : (chunk + 1) * size],
            target.at[chunk_rows(info[start + chunk], size)],
            sem,
        ).start()


def wait_chunks(source, target, sem):
    pltpu.make_async_copy(source, target, sem).wait()


def core_of(info, side):
    return info[0] if side else 1 - info[0]


def up_kernel(info, z_low, grad, give, keep, turned, buf, sem):
    half = keep.shape[1]
    turned[...] = z_low[...].T
    for side, out in ((0, give), (1, keep)):
        at = pl.ds(pl.multiple_of(core_of(info, side) * half, half), half)
        buf[side] = nn(turned[...], grad[:, at]).astype(LOW)
        place_chunks(buf.at[side], out, info, sem.at[side])
    for side, out in ((0, give), (1, keep)):
        wait_chunks(buf.at[side], out, sem.at[side])


def down_kernel(info, active, grad, give, keep, buf, sem):
    size = keep.shape[0]
    for side, out in ((0, give), (1, keep)):
        for part in range(keep.shape[1] // size):
            block = core_of(info, side) * (keep.shape[1] // size) + part
            at = pl.ds(pl.multiple_of(block * size, size), size)
            buf[side, :, part * size : (part + 1) * size] = nn(active[:, at].T, grad[...]).astype(LOW)
        place_chunks(buf.at[side], out, info, sem.at[side])
    for side, out in ((0, give), (1, keep)):
        wait_chunks(buf.at[side], out, sem.at[side])


def out_q_kernel(info, attn, db, tok, dq, order, sums, give, keep, grad_q, attn_t, tok_t, buf, sem):
    rows = tok.shape[0]
    half = D // 2
    down = lax.broadcasted_iota(jnp.int32, (rows, rows), 0)
    for pair in range(HEADS // 2):
        total = nn(pick(down == order[2 * pair]), dq[2 * pair])
        total += nn(pick(down == order[2 * pair + 1]), dq[2 * pair + 1])
        lanes = slice(pair * 2 * HEAD_DIM, (pair + 1) * 2 * HEAD_DIM)
        grad_q[:, lanes] = total.astype(LOW)
    attn_t[...] = attn[...].T
    tok_t[...] = tok[...].T
    size = D // VECTORS
    filler = jnp.zeros((size - D // LANES, LANES), F32)
    for vector in range(VECTORS):
        rows_of = [sums[vector : vector + 1, row * LANES : (row + 1) * LANES] for row in range(D // LANES)]
        value = jnp.concatenate(rows_of + [filler]).astype(LOW)
        for side in range(2):
            buf[side, vector * size : (vector + 1) * size, D:] = value
    for side, out in ((0, give), (1, keep)):
        at = pl.ds(pl.multiple_of(core_of(info, side) * half, half), half)
        buf[side, :, :half] = nn(attn_t[...], db[:, at]).astype(LOW)
        buf[side, :, half:D] = nn(tok_t[...], grad_q[:, at]).astype(LOW)
        place_chunks(buf.at[side], out, info, sem.at[side])
    for side, out in ((0, give), (1, keep)):
        wait_chunks(buf.at[side], out, sem.at[side])


def key_value_kernel(
    info, segment, returned_hbm, order, tok, key_give, key_keep, value_give, value_keep, grad_kv_hbm,
    returned, total, tok_t, grad_kv, buf, load_sem, kv_sem, sem,
):
    rows = tok.shape[0]
    half = D // 2
    per_dev = rows // CLUS
    pair_width = 2 * HEAD_DIM
    devices = load_sem.shape[0]
    capacity = segment.shape[0] // devices

    def load(device):
        span = pl.ds(device * capacity, capacity)
        return pltpu.make_async_copy(returned_hbm.at[span], returned.at[span], load_sem.at[device])

    @pl.loop(0, devices)
    def _(device):
        load(device).start()

    down = lax.broadcasted_iota(jnp.int32, (rows, rows), 0)
    left = left_half((rows, pair_width))
    total[...] = jnp.zeros_like(total)
    tok_t[...] = tok[...].T

    @pl.loop(0, devices)
    def _(device):
        load(device).wait()
        for step in range(capacity):
            slot = device * capacity + step
            block = segment[slot]
            total[block] += returned[slot].astype(F32)

    for quad in range(HEADS // 4):
        pairs = range(2 * quad, 2 * quad + 2)
        heads = range(4 * quad, 4 * quad + 4)
        hots = [pick(down == order[head]) for head in heads]
        summed = [
            total[head * per_dev : (head + 1) * per_dev].reshape(rows, pair_width).astype(LOW) for head in heads
        ]
        placed = [nn(hot, value) for hot, value in zip(hots, summed)]
        for at, pair in enumerate(pairs):
            even, odd = placed[2 * at], placed[2 * at + 1]
            grad_kv[:, pair * pair_width : (pair + 1) * pair_width] = jnp.where(left, even, odd).astype(LOW)
            values = pltpu.roll(jnp.where(left, odd, even), HEAD_DIM, 1)
            grad_kv[:, D + pair * pair_width : D + (pair + 1) * pair_width] = values.astype(LOW)
    stored = pltpu.make_async_copy(grad_kv, grad_kv_hbm, kv_sem)
    stored.start()
    outs = ((key_give, key_keep), (value_give, value_keep))
    for side in range(2):
        base = core_of(info, side) * half
        parts = [grad_kv[:, pl.ds(pl.multiple_of(part * D + base, half), half)] for part in range(2)]
        value = nn(tok_t[...], jnp.concatenate(parts, axis=1)).astype(LOW)
        for part in range(2):
            buf[part, side] = value[:, part * half : (part + 1) * half]
            place_chunks(buf.at[part, side], outs[part][side], info, sem.at[part, side], 33 if part else 1)
    for side in range(2):
        for part in range(2):
            wait_chunks(buf.at[part, side], outs[part][side], sem.at[part, side])
    stored.wait()


def spread_start(info, start, pieces, targets, buf, sem):
    size = buf.shape[2]
    copies = []
    for at, piece in enumerate(pieces):
        core = core_of(info, 1 - at)
        for chunk in range(buf.shape[1]):
            buf[at, chunk] = piece[chunk * size : (chunk + 1) * size].astype(F32)
            for lanes, target in targets(core, chunk_rows(info[start + chunk], size)):
                copies.append(pltpu.make_async_copy(buf.at[at, chunk, :, lanes], target, sem))
                copies[-1].start()
    return copies


def up_targets(out, half):
    def targets(core, rows):
        yield pl.ds(0, half), out.at[rows, pl.ds(pl.multiple_of(core * half, half), half)]

    return targets


def down_targets(out, half):
    parts = half // D

    def targets(core, rows):
        for part in range(parts):
            yield pl.ds(part * D, D), out.at[core * parts + part, rows]

    return targets


def attention_targets(w_out, w_qkv):
    half = D // 2

    def targets(core, rows):
        at = pl.ds(pl.multiple_of(core * half, half), half)
        yield pl.ds(0, half), w_out.at[rows, at]
        for part, lane in enumerate((half, D + LANES, D + LANES + half)):
            to = pl.ds(pl.multiple_of(part * D + core * half, half), half)
            yield pl.ds(lane, half), w_qkv.at[rows, to]

    return targets


def spread_groups(groups, info, pieces, outs, bufs, sem):
    w_up, w_down, w_out, w_qkv = outs
    half = w_up.shape[1] // 2
    routes = (up_targets(w_up, half), down_targets(w_down, half), attention_targets(w_out, w_qkv))
    copies = []
    for at, (third, start) in enumerate(groups):
        copies += spread_start(info, start, pieces[2 * at : 2 * at + 2], routes[third], bufs[at], sem.at[at])
    return copies


def spread_kernel(groups, info, *refs):
    pairs = len(groups)
    pieces, bufs, sem = refs[: 2 * pairs], refs[-pairs - 1 : -1], refs[-1]
    outs = refs[-pairs - 5 : -pairs - 1]
    for copy in spread_groups(groups, info, pieces, outs, bufs, sem):
        copy.wait()


def spread_last_kernel(groups, start, info, *refs):
    pairs = len(groups)
    pieces, sources = refs[: 2 * pairs], refs[2 * pairs : 2 * pairs + 4]
    rest = refs[2 * pairs + 8 :]
    outs, vectors, rest = rest[:4], rest[4:13], rest[13:]
    bufs = rest[:pairs]
    sem, columns, table, column_sem = rest[pairs:]
    loads = [
        pltpu.make_async_copy(source.at[:, D : D + LANES], columns.at[at], column_sem.at[at])
        for at, source in enumerate(sources)
    ]
    for load in loads:
        load.start()
    copies = spread_groups(groups, info, pieces, outs, bufs, sem)
    size = D // VECTORS
    each = CHUNKS // len(sources)
    inside = VECTORS // CHUNKS
    for at, load in enumerate(loads):
        load.wait()
        for row in range(each * inside):
            vector = info[start + at * each + row // inside] * inside + row % inside
            table[vector] = columns[at, row * size : row * size + 16].astype(F32)

    def whole(vector):
        return jnp.concatenate([table[vector, row : row + 1] for row in range(D // LANES)], axis=1)

    for at, vector in enumerate(vectors):
        count = vector.shape[0] // D
        vector[...] = jnp.concatenate([whole(at + part) for part in range(count)], axis=1).reshape(count * D)
    for copy in copies:
        copy.wait()


X, Y, Z = ("dp", 1), ("blk", 2), ("blk", 4)
CORE = ("blk", 1)
ORDERS = ((Z, Y, X), (X, Z, Y), (Y, X, Z))


def swap(value, bit):
    axis, distance = bit
    size = lax.axis_size(axis)
    return lax.ppermute(value, axis, [(i, i ^ distance) for i in range(size)])


def further_bits(count_blk):
    bits = []
    distance = 8
    while distance < count_blk:
        bits.append(("blk", distance))
        distance *= 2
    return bits


def chunk_places():
    x, y, z = [(lax.axis_index(axis) // distance) % 2 for axis, distance in (X, Y, Z)]
    chip = x * 4 + y * 2 + z
    core = lax.axis_index("blk") % 2
    every = jnp.arange(CHUNKS, dtype=jnp.int32)
    value = {X: 4, Y: 2, Z: 1}

    def from_order(order):
        at = sum(((every // 2**step) % 2) * value[bit] for step, bit in enumerate(order))
        return at ^ chip

    placed = every ^ chip
    x_y_swapped = placed % 2 + (placed // 4) * 2 + (placed // 2 % 2) * 4
    return jnp.concatenate(
        [core[None], placed] + [from_order(order) for order in ORDERS] + [x_y_swapped]
    )


def sum_rows(terms, low, high):
    total = terms[0][low:high].astype(F32)
    for term in terms[1:]:
        total = total + term[low:high].astype(F32)
    return total


def to_send(terms):
    rows = min(term.shape[0] for term in terms)
    return sum_rows(terms, rows // 2, rows).astype(LOW)


def scatter_steps(terms, bits):
    for bit in bits:
        terms = terms + [swap(to_send(terms), bit)]
    return terms


def finish(terms, further):
    value = sum_rows(terms, 0, terms[-1].shape[0]).astype(LOW)
    for bit in further:
        value = sum_rows([value, swap(value, bit)], 0, value.shape[0]).astype(LOW)
    return value


def tie(values):
    return lax.optimization_barrier(tuple(values))


def gather_step(value, bit):
    return jnp.concatenate([value, swap(value, bit)])


def per_device(
    tokens,
    w_qkv,
    b_query,
    b_value,
    w_out,
    b_out,
    gain_one,
    shift_one,
    w_up,
    b_up,
    w_down,
    b_down,
    gain_two,
    shift_two,
    cluster_perm,
    cluster_pairs,
    cotangent,
):
    count_blk = lax.axis_size("blk")
    my_index = lax.axis_index("blk")
    rows = tokens.shape[0]
    per_dev = rows // CLUS
    blocks = HEADS * per_dev
    requests = blocks * PAIRS
    capacity = max(2, (requests + count_blk - 1) // count_blk + 1)
    slots = count_blk * capacity
    pair_width = 2 * HEAD_DIM
    ff = w_up.shape[1]
    local_order = cluster_perm[0] - my_index * rows
    order_rows = local_order[:, None, :]

    wanted = (
        cluster_pairs[0]
        .reshape(HEADS, count_blk, per_dev, PAIRS)
        .transpose(1, 0, 2, 3)
        .reshape(count_blk, requests)
    )
    positions = jnp.arange(requests, dtype=jnp.int32)
    before = positions[:, None] < positions[None, :]
    source = wanted // per_dev
    named = source == my_index
    rank = jnp.sum(named[:, :, None] & before[None], axis=1)
    head_of = positions // (per_dev * PAIRS)
    block_id = head_of[None, :] * per_dev + wanted % per_dev
    matches = named[:, :, None] & (
        rank[:, :, None] == jnp.arange(capacity, dtype=jnp.int32)[None, None, :]
    )
    chosen = jnp.sum(jnp.where(matches, block_id[:, :, None], 0), axis=1)

    smem = pl.BlockSpec(memory_space=pltpu.SMEM)
    vmem = pl.BlockSpec(memory_space=pltpu.VMEM)
    hbm = pl.BlockSpec(memory_space=pl.ANY)

    def column_block(at):
        return pl.BlockSpec((D, D), lambda step: (0, at))

    outgoing = pl.pallas_call(
        kv_kernel,
        grid=(1,),
        out_shape=jax.ShapeDtypeStruct((slots, CLUS, pair_width), LOW),
        in_specs=[vmem, column_block(1), column_block(2), vmem, vmem, vmem],
        out_specs=hbm,
        scratch_shapes=[
            pltpu.VMEM((blocks, CLUS, pair_width), LOW),
            pltpu.SMEM(chosen.shape, jnp.int32),
            pltpu.SemaphoreType.DMA,
            pltpu.SemaphoreType.DMA,
        ],
        compiler_params=params(),
        name="kv_kernel",
    )(tokens, w_qkv, w_qkv, b_value, cluster_perm, chosen)
    arrived = lax.all_to_all(
        outgoing.reshape(count_blk, capacity, CLUS, pair_width),
        "blk",
        split_axis=0,
        concat_axis=0,
        tiled=True,
    ).reshape(slots, CLUS, pair_width)

    info = chunk_places()
    queries = pl.pallas_call(
        q_kernel,
        grid=(1,),
        out_shape=jax.ShapeDtypeStruct((HEADS, rows, pair_width), LOW),
        in_specs=[vmem, column_block(0), vmem, vmem],
        out_specs=vmem,
        compiler_params=params(),
        name="q_kernel",
    )(tokens, w_qkv, b_query, cluster_perm)
    filled = jnp.any(matches, axis=1)
    segment = jnp.where(filled, chosen, blocks).reshape(-1)
    my_source = lax.dynamic_index_in_dim(wanted, my_index, 0, keepdims=False) // per_dev
    my_rank = jnp.sum((my_source[:, None] == my_source[None, :]) & before, axis=0)
    fetch = my_source * capacity + my_rank
    places = jnp.arange(rows, dtype=jnp.int32)
    inverse = jnp.sum(
        jnp.where(local_order[:, :, None] == places, places[None, :, None], 0), axis=1
    )[:, None, :]
    def low(*shape):
        return jax.ShapeDtypeStruct(shape, LOW)

    def full(*shape):
        return jax.ShapeDtypeStruct(shape, F32)

    (
        back, dq_sorted, attn, normed, active, grad_inner, grad_second, grad_branch, grad_resid,
        layer_out, sums,
    ) = pl.pallas_call(
        mid_kernel,
        out_shape=(
            low(slots, CLUS, pair_width), low(HEADS, rows, pair_width), low(rows, D), low(rows, D),
            low(rows, ff), low(rows, ff), low(rows, D), low(rows, D), full(rows, D), low(rows, D),
            full(16, D),
        ),
        in_specs=[smem, vmem, hbm, vmem, vmem, hbm, hbm] + [vmem] * 7 + [hbm] * 3,
        out_specs=(hbm,) * 10 + (vmem,),
        scratch_shapes=[
            pltpu.VMEM((requests, CLUS, pair_width), LOW),
            pltpu.VMEM((blocks, CLUS, PAIRS * CLUS), LOW),
            pltpu.VMEM((rows, D), LOW),
            pltpu.VMEM((2, rows, pair_width), LOW),
            pltpu.VMEM((D, D), LOW),
            pltpu.VMEM((D, ff), LOW),
            pltpu.VMEM((ff, D), LOW),
            pltpu.VMEM((rows, D), F32),
            pltpu.VMEM((rows, D), F32),
            pltpu.VMEM((rows, D), F32),
            pltpu.VMEM((rows, 1), F32),
            pltpu.VMEM((rows, D), LOW),
            pltpu.VMEM((rows, ff), LOW),
            pltpu.VMEM((rows, ff), LOW),
            pltpu.VMEM((rows, D), F32),
            pltpu.VMEM((rows, D), LOW),
            pltpu.VMEM((rows, D), LOW),
            pltpu.VMEM((rows, D), LOW),
            pltpu.VMEM((rows, D), F32),
            pltpu.VMEM((rows, D), LOW),
            pltpu.VMEM((HEADS, rows, pair_width), LOW),
            pltpu.VMEM((rows, D), LOW),
            pltpu.VMEM((rows, D), LOW),
            pltpu.SemaphoreType.DMA((HEADS // 2,)),
            pltpu.SemaphoreType.DMA((5,)),
            pltpu.SemaphoreType.DMA((9,)),
            pltpu.SemaphoreType.DMA,
        ],
        compiler_params=params(),
        name="mid_kernel",
    )(
        fetch, queries, arrived, order_rows, inverse, tokens, cotangent,
        b_out, gain_one, shift_one, b_up, b_down, gain_two, shift_two, w_out, w_up, w_down,
    )
    returned = lax.all_to_all(
        back.reshape(count_blk, capacity, CLUS, pair_width),
        "blk",
        split_axis=0,
        concat_axis=0,
        tiled=True,
    ).reshape(slots, CLUS, pair_width)

    further = further_bits(count_blk)

    def halves(kernel, operands, columns, scratch, more=(), name=None):
        return pl.pallas_call(
            kernel,
            out_shape=(low(D, columns), low(D, columns)) + more,
            in_specs=[smem] + [vmem] * (len(operands) - 1),
            out_specs=(hbm, hbm) + (vmem,) * len(more),
            scratch_shapes=scratch
            + [pltpu.VMEM((2, D, columns), LOW), pltpu.SemaphoreType.DMA((2,))],
            compiler_params=params(),
            cost_estimate=pl.CostEstimate(flops=1, bytes_accessed=1, transcendentals=0),
            name=name,
        )(*operands)

    half = D // 2
    turned = pltpu.VMEM((D, rows), LOW)
    up_give, up_keep = halves(
        up_kernel, (info, normed, grad_inner), ff // 2, [turned], name="up_kernel"
    )
    down_give, down_keep = halves(
        down_kernel, (info, active, grad_second), ff // 2, [], name="down_kernel"
    )
    up = [up_keep, swap(up_give, CORE)]
    up_step, attn = tie((to_send(up), attn))
    oq_give, oq_keep, grad_q = halves(
        out_q_kernel,
        (info, attn, grad_branch, tokens, dq_sorted, order_rows, sums),
        D + LANES,
        [turned, turned],
        (low(rows, D),),
        name="out_q_kernel",
    )
    up = scatter_steps(up + [swap(up_step, X)], (Y,))
    down = scatter_steps([down_keep, swap(down_give, CORE)], (X,))
    out_q = scatter_steps([oq_keep, swap(oq_give, CORE)], (X,))
    up_step = to_send(up)
    up_step, down[-1] = tie((up_step, down[-1]))
    down_step = to_send(down)

    returned, up_step, down_step, out_q[-1] = tie((returned, up_step, down_step, out_q[-1]))
    up = up + [swap(up_step, Z)]
    down = down + [swap(down_step, Y)]
    out_q = scatter_steps(out_q, (Y,))
    key_give, key_keep, value_give, value_keep, grad_kv = pl.pallas_call(
        key_value_kernel,
        out_shape=(low(D, half),) * 4 + (low(rows, 2 * D),),
        in_specs=[smem, smem, hbm, vmem, vmem],
        out_specs=(hbm,) * 5,
        scratch_shapes=[
            pltpu.VMEM((slots, CLUS, pair_width), LOW),
            pltpu.VMEM((blocks + 1, CLUS, pair_width), F32),
            turned,
            pltpu.VMEM((rows, 2 * D), LOW),
            pltpu.VMEM((2, 2, D, half), LOW),
            pltpu.SemaphoreType.DMA((count_blk,)),
            pltpu.SemaphoreType.DMA,
            pltpu.SemaphoreType.DMA((2, 2)),
        ],
        compiler_params=params(),
        name="key_value_kernel",
    )(info, segment, returned, order_rows, tokens)
    down[-1], key_give, value_give = tie((down[-1], key_give, value_give))
    key = scatter_steps([key_keep, swap(key_give, CORE)], (X, Y))
    value = scatter_steps([value_keep, swap(value_give, CORE)], (Y, X))
    late_given = swap(jnp.concatenate([to_send(key), to_send(value)], axis=1), Z)
    key = key + [late_given[:, :half]]
    value = value + [late_given[:, half:]]
    up = finish(up, further)
    down = finish(scatter_steps(down, (Z,)), further)
    out_q = finish(scatter_steps(out_q, (Z,)), further)
    both = jnp.concatenate([sum_rows(terms, 0, terms[-1].shape[0]) for terms in (key, value)], axis=1)
    both = finish([both.astype(LOW)], further)
    thirds = (up, down, jnp.concatenate([out_q, both], axis=1))

    starts = (9, 17, 25)
    weights = (full(D, ff), full(ff // D, D, D), full(D, D), full(D, 3 * D))

    def swap_all(values, step):
        return [swap(value, order[step]) for value, order in zip(values, ORDERS)]

    def spread_scratch(pieces):
        rows_each = D // CHUNKS
        return (
            [
                pltpu.VMEM((2, piece.shape[0] // rows_each, rows_each, piece.shape[1]), F32)
                for piece in pieces[::2]
            ]
            + [pltpu.SemaphoreType.DMA((len(pieces) // 2,))]
        )

    def with_other(sets):
        return [array for value in sets for array in (value, swap(value, CORE))]

    def spread(sets, offsets, outs=()):
        pieces = with_other(sets)
        groups = tuple((third, starts[third] + offset) for offset in offsets for third in range(3))
        return pl.pallas_call(
            partial(spread_kernel, groups),
            out_shape=weights,
            in_specs=[smem] + [vmem] * len(pieces) + [hbm] * len(outs),
            out_specs=(hbm,) * 4,
            scratch_shapes=spread_scratch(pieces),
            input_output_aliases={1 + len(pieces) + at: at for at in range(len(outs))},
            compiler_params=params(32),
            name="spread",
        )(info, *pieces, *outs)

    thirds = list(tie(gather_step(value, order[0]) for value, order in zip(thirds, ORDERS)))
    third_step = swap_all(thirds, 1)
    fourth_step = swap_all(thirds, 2)
    outs = spread(thirds, (0,))
    tied = tie((*third_step, grad_kv))
    third_step, grad_kv = list(tied[:3]), tied[3]
    last_step = swap_all(third_step, 2)
    grad_proj = jnp.concatenate([grad_q, grad_kv], axis=1)
    grad_tokens = (grad_resid + nt(grad_proj, w_qkv)).astype(LOW)
    tied = tie((*fourth_step, *outs, grad_tokens))
    fourth_step, outs, grad_tokens = list(tied[:3]), tied[3:7], tied[7]
    outs = spread(third_step + fourth_step, (2, 4), outs)
    tied = tie((*last_step, *outs))
    last_step, outs = list(tied[:3]), tied[3:]
    pieces = with_other(last_step)
    sum_up, sum_down, sum_out, sum_qkv, *vectors = pl.pallas_call(
        partial(spread_last_kernel, tuple((third, starts[third] + 6) for third in range(3)), starts[2]),
        out_shape=weights + (full(D),) * 8 + (full(ff),),
        in_specs=[smem] + [vmem] * len(pieces) + [hbm] * 8,
        out_specs=(hbm,) * 4 + (vmem,) * 9,
        scratch_shapes=spread_scratch(pieces)
        + [
            pltpu.VMEM((4, D // 4, LANES), LOW),
            pltpu.VMEM((VECTORS, 16, LANES), F32),
            pltpu.SemaphoreType.DMA((4,)),
        ],
        input_output_aliases={1 + len(pieces) + 4 + at: at for at in range(4)},
        compiler_params=params(24),
        name="spread_last",
    )(info, *pieces, thirds[2], third_step[2], fourth_step[2], last_step[2], *outs)
    return (
        layer_out,
        grad_tokens,
        sum_qkv,
        vectors[7],
        vectors[6],
        sum_out,
        vectors[5],
        vectors[3],
        vectors[4],
        sum_up,
        vectors[8],
        sum_down.reshape(ff, D),
        vectors[2],
        vectors[0],
        vectors[1],
    )


def solution(mesh):
    whole = P()
    rows = P(("dp", "blk"), None)
    return jax.shard_map(
        per_device,
        mesh=mesh,
        in_specs=(
            (rows,)
            + (whole,) * 13
            + (P("dp", None, "blk"), P("dp", None, None, None), rows)
        ),
        out_specs=(rows, rows) + (whole,) * 13,
        check_vma=False,
    )
```

```python
from functools import partial

import jax
import jax.numpy as jnp
from jax import lax
from jax.experimental import pallas as pl
from jax.experimental.pallas import tpu as pltpu
from jax.sharding import PartitionSpec as P

D = 768
HEADS = 12
HEAD_DIM = 64
CLUS = 128
PAIRS = 2
LANES = 128

F32 = jnp.float32
LOW = jnp.bfloat16


def nn(left, right):
    return jnp.dot(left, right, preferred_element_type=F32)


def nt(left, right):
    return lax.dot_general(left, right, (((1,), (1,)), ((), ())), preferred_element_type=F32)


def tn(left, right):
    return lax.dot_general(left, right, (((0,), (0,)), ((), ())), preferred_element_type=F32)


def as_row(vector):
    return vector[...].astype(F32).reshape(1, vector.shape[0])


def left_half(shape):
    return lax.broadcasted_iota(jnp.int32, shape, 1) < HEAD_DIM


def pick(hot):
    return jnp.where(hot, 1.0, 0.0).astype(LOW)


def params(megabytes=60):
    return pltpu.CompilerParams(vmem_limit_bytes=megabytes << 20)


def columns_of(perm, rows):
    every = [perm[head] for head in range(HEADS)] + [perm[0]] * (16 - HEADS)
    return lax.rem(jnp.concatenate(every), rows).T


def kv_kernel(tok, w_key, w_value, b_value, perm, chosen_in, out, blocks, chosen, chosen_sem, sem):
    fetch = pltpu.make_async_copy(chosen_in, chosen, chosen_sem)
    fetch.start()
    rows = tok.shape[0]
    order = columns_of(perm, rows)
    per_dev = rows // CLUS
    place = lax.broadcasted_iota(jnp.int32, (rows, rows), 1)
    left = left_half((rows, 2 * HEAD_DIM))
    inputs = tok[...]
    keys = nn(inputs, w_key[...])
    values = nn(inputs, w_value[...]) + as_row(b_value)
    joined = []
    for pair in range(HEADS // 2):
        two = slice(pair * 2 * HEAD_DIM, (pair + 1) * 2 * HEAD_DIM)
        key_two = keys[:, two]
        value_two = pltpu.roll(values[:, two], HEAD_DIM, 1)
        joined.append(jnp.where(left, key_two, value_two).astype(LOW))
        joined.append(jnp.where(left, value_two, key_two).astype(LOW))
    for quad in range(HEADS // 4):
        heads = range(quad * 4, quad * 4 + 4)
        hot = [pick(order[:, head : head + 1] == place) for head in heads]
        ranked = [nn(one, joined[head]).astype(LOW) for one, head in zip(hot, heads)]
        for head, value in zip(heads, ranked):
            blocks[head * per_dev : (head + 1) * per_dev] = value.reshape(per_dev, CLUS, 2 * HEAD_DIM)
    fetch.wait()
    devices, capacity = chosen.shape

    @pl.loop(0, devices)
    def _(device):
        for slot in range(capacity):
            pltpu.make_async_copy(
                blocks.at[chosen[device, slot]], out.at[device * capacity + slot], sem
            ).start()

    pltpu.make_async_copy(out, out, sem).wait()


def q_kernel(tok, w_query, b_query, perm, out):
    rows = tok.shape[0]
    order = columns_of(perm, rows)
    place = lax.broadcasted_iota(jnp.int32, (rows, rows), 1)
    left = left_half((rows, 2 * HEAD_DIM))
    inputs = tok[...]
    for quad in range(HEADS // 4):
        four = slice(quad * 4 * HEAD_DIM, (quad + 1) * 4 * HEAD_DIM)
        queries = nn(inputs, w_query[:, four]) + as_row(b_query)[:, four]
        queries = (queries.astype(LOW).astype(F32) * HEAD_DIM ** (-0.5)).astype(LOW)
        for pair in range(2):
            two = queries[:, pair * 2 * HEAD_DIM : (pair + 1) * 2 * HEAD_DIM]
            for odd in range(2):
                head = quad * 4 + pair * 2 + odd
                hot = pick(order[:, head : head + 1] == place)
                ranked = nn(hot, two)
                kept = jnp.where(left, 0.0, ranked) if odd else jnp.where(left, ranked, 0.0)
                out[head] = kept.astype(LOW)


ROW_TILE = 512
WIDE = 768
WIDE_FORTH = 1024
WIDE_BACK = 1536


def mid_kernel(
    fetch, queries, arrived, order, inverse, tok_hbm, cot_hbm,
    b_out, gain_one, shift_one, b_up, b_down, gain_two, shift_two, w_out_hbm, w_up_hbm, w_down_hbm,
    back, dq_out, attn_out, z_out, active_out, du_out, df_out, db_out, dh1_out, layer_out, sums,
    kv, probs, attn, mixed, w_out, w_up, w_down, hidden, n_one, r_one, z_low, active, slope,
    dh2, df, db, d_out, dh1, final, dq, tok, cot, kv_sem, w_sem, out_sem, back_sem,
):
    rows = tok_hbm.shape[0]
    per_dev = rows // CLUS
    pair_width = 2 * HEAD_DIM
    requests = fetch.shape[0]
    each = 2 * per_dev * PAIRS
    width = w_up.shape[1]
    tiles = rows // ROW_TILE
    left = left_half((CLUS, pair_width))
    left_rows = left_half((rows, pair_width))
    down = lax.broadcasted_iota(jnp.int32, (rows, rows), 0)

    @pl.loop(0, HEADS // 2)
    def _(group):
        for step in range(each):
            entry = group * each + step
            pltpu.make_async_copy(arrived.at[fetch[entry]], kv.at[entry], kv_sem.at[group]).start()

    loads = [
        pltpu.make_async_copy(source, target, w_sem.at[at])
        for at, (source, target) in enumerate(
            ((w_out_hbm, w_out), (tok_hbm, tok), (w_up_hbm, w_up), (w_down_hbm, w_down), (cot_hbm, cot))
        )
    ]
    for load in loads:
        load.start()
    stores = []

    def store(source, target):
        copy = pltpu.make_async_copy(source, target, out_sem.at[len(stores)])
        copy.start()
        stores.append(copy)

    @pl.loop(0, HEADS // 2)
    def _(group):
        span = kv.at[pl.ds(group * each, each)]
        pltpu.make_async_copy(span, span, kv_sem.at[group]).wait()
        units = [(odd, cluster) for odd in range(2) for cluster in range(per_dev)]
        clusters = [slice(cluster * CLUS, (cluster + 1) * CLUS) for cluster in range(per_dev)]
        index = [(2 * group + odd) * per_dev + cluster for odd, cluster in units]
        pair = [kv[pl.ds(unit * PAIRS, PAIRS)].reshape(PAIRS * CLUS, pair_width) for unit in index]
        scores = [
            nt(queries[2 * group + odd, clusters[cluster], :], both)
            for (odd, cluster), both in zip(units, pair)
        ]
        exponent = [jnp.exp(value - jnp.max(value, -1, keepdims=True)) for value in scores]
        low = [(value / jnp.sum(value, -1, keepdims=True)).astype(LOW) for value in exponent]
        for (odd, cluster), unit, value, both in zip(units, index, low, pair):
            probs[unit] = value
            value = nn(value, both)
            mixed[odd, clusters[cluster], :] = (
                jnp.where(left, value, 0.0) if odd else jnp.where(left, 0.0, value)
            ).astype(LOW)
        hot = jnp.concatenate([pick(down == order[2 * group + odd]) for odd in range(2)], axis=1)
        both = pltpu.roll(nn(hot, mixed[...].reshape(2 * rows, pair_width)), HEAD_DIM, 1)
        attn[:, pl.ds(pl.multiple_of(group * pair_width, pair_width), pair_width)] = both.astype(LOW)

    store(attn, attn_out)
    loads[0].wait()
    loads[1].wait()
    hidden[...] = nn(attn[...], w_out[...])

    @pl.loop(0, tiles)
    def _(tile):
        at = pl.ds(pl.multiple_of(tile * ROW_TILE, ROW_TILE), ROW_TILE)
        value = hidden[at, :] + (as_row(b_out) + tok[at, :].astype(F32))
        centred = value - jnp.mean(value, -1, keepdims=True)
        scale = lax.rsqrt(jnp.mean(centred * centred, -1, keepdims=True) + 1e-06)
        unit = centred * scale
        z = unit * as_row(gain_one) + as_row(shift_one)
        n_one[at, :] = unit
        r_one[at, :] = scale
        z_low[at, :] = z.astype(LOW)
        hidden[at, :] = z + as_row(b_down)

    store(z_low, z_out)
    loads[2].wait()
    loads[3].wait()

    @pl.loop(0, width // WIDE_FORTH)
    def _(step):
        at = pl.ds(pl.multiple_of(step * WIDE_FORTH, WIDE_FORTH), WIDE_FORTH)
        inner = nn(z_low[...], w_up[:, at]) + b_up[at].astype(F32).reshape(1, WIDE_FORTH)
        normal = 0.5 * (1.0 + lax.erf(inner * 0.7071067811865476))
        density = jnp.exp(inner * inner * -0.5) * 0.3989422804014327
        active[:, at] = (inner * normal).astype(LOW)
        slope[:, at] = (normal + inner * density).astype(LOW)
        hidden[...] += nn(active[:, at], w_down[at, :])

    store(active, active_out)
    loads[4].wait()
    sums[...] = jnp.zeros_like(sums)

    @pl.loop(0, tiles)
    def _(tile):
        at = pl.ds(pl.multiple_of(tile * ROW_TILE, ROW_TILE), ROW_TILE)
        value = hidden[at, :]
        centred = value - jnp.mean(value, -1, keepdims=True)
        scale = lax.rsqrt(jnp.mean(centred * centred, -1, keepdims=True) + 1e-06)
        unit = centred * scale
        final[at, :] = (unit * as_row(gain_two) + as_row(shift_two)).astype(LOW)
        grad = cot[at, :].astype(F32)
        lifted = grad * as_row(gain_two)
        back_grad = scale * (
            lifted - jnp.mean(lifted, -1, keepdims=True) - unit * jnp.mean(lifted * unit, -1, keepdims=True)
        )
        dh2[at, :] = back_grad
        low = back_grad.astype(LOW)
        df[at, :] = low
        sums[0:1, :] += jnp.sum(grad * unit, axis=0, keepdims=True)
        sums[1:2, :] += jnp.sum(grad, axis=0, keepdims=True)
        sums[2:3, :] += jnp.sum(low.astype(F32), axis=0, keepdims=True)

    store(final, layer_out)
    store(df, df_out)
    ones = jnp.ones((8, rows), LOW)

    @pl.loop(0, width // WIDE_BACK)
    def _(step):
        at = pl.ds(pl.multiple_of(step * WIDE_BACK, WIDE_BACK), WIDE_BACK)
        grad = (nt(df[...], w_down[at, :]) * slope[:, at].astype(F32)).astype(LOW)
        slope[:, at] = grad
        total = nn(ones, grad)
        for part in range(WIDE_BACK // D):
            row = 8 + step * (WIDE_BACK // D) + part
            sums[pl.ds(row, 1), :] = total[0:1, part * D : (part + 1) * D]
        dh2[...] += nt(slope[:, at], w_up[:, at])

    store(slope, du_out)

    @pl.loop(0, tiles)
    def _(tile):
        at = pl.ds(pl.multiple_of(tile * ROW_TILE, ROW_TILE), ROW_TILE)
        grad = dh2[at, :]
        unit = n_one[at, :]
        lifted = grad * as_row(gain_one)
        back_grad = r_one[at, :] * (
            lifted - jnp.mean(lifted, -1, keepdims=True) - unit * jnp.mean(lifted * unit, -1, keepdims=True)
        )
        dh1[at, :] = back_grad
        low = back_grad.astype(LOW)
        db[at, :] = low
        sums[3:4, :] += jnp.sum(grad * unit, axis=0, keepdims=True)
        sums[4:5, :] += jnp.sum(grad, axis=0, keepdims=True)
        sums[5:6, :] += jnp.sum(low.astype(F32), axis=0, keepdims=True)

    store(dh1, dh1_out)
    store(db, db_out)
    d_out[...] = nt(db[...], w_out[...]).astype(LOW)

    @pl.loop(0, HEADS // 2)
    def _(group):
        lanes = pl.ds(pl.multiple_of(group * pair_width, pair_width), pair_width)
        tile = d_out[:, lanes]
        grads = []
        for odd in range(2):
            turned = pltpu.roll(nn(pick(down == inverse[2 * group + odd]), tile), HEAD_DIM, 1)
            grads.append((jnp.where(left_rows, turned, 0.0) if odd else jnp.where(left_rows, 0.0, turned)).astype(LOW))
        units = [(odd, cluster) for odd in range(2) for cluster in range(per_dev)]
        clusters = [slice(cluster * CLUS, (cluster + 1) * CLUS) for cluster in range(per_dev)]
        index = [(2 * group + odd) * per_dev + cluster for odd, cluster in units]
        grad = [grads[odd][clusters[cluster]] for odd, cluster in units]
        query = [queries[2 * group + odd, clusters[cluster], :] for odd, cluster in units]
        pair = [kv[pl.ds(unit * PAIRS, PAIRS)].reshape(PAIRS * CLUS, pair_width) for unit in index]
        low = [probs[unit] for unit in index]
        d_probs = [nt(left_, right) for left_, right in zip(grad, pair)]
        wide = [value.astype(F32) for value in low]
        d_scores = [
            (value * (grad_ - jnp.sum(grad_ * value, -1, keepdims=True))).astype(LOW)
            for value, grad_ in zip(wide, d_probs)
        ]
        d_query = [nn(left_, right) * HEAD_DIM ** (-0.5) for left_, right in zip(d_scores, pair)]
        d_pair = [tn(a, b) + tn(c, d) for a, b, c, d in zip(d_scores, query, low, grad)]
        bias = [jnp.zeros((1, pair_width), F32)] * 2
        q_total = jnp.zeros((1, pair_width), F32)
        for (odd, cluster), unit, value, both in zip(units, index, d_query, d_pair):
            value = (jnp.where(left, 0.0, value) if odd else jnp.where(left, value, 0.0)).astype(LOW)
            dq[2 * group + odd, clusters[cluster], :] = value
            q_total += jnp.sum(value.astype(F32), axis=0, keepdims=True)
            bias[odd] += jnp.sum(both, axis=0, keepdims=True)
            kv[pl.ds(unit * PAIRS, PAIRS)] = both.astype(LOW).reshape(PAIRS, CLUS, pair_width)
        for step in range(each):
            entry = group * each + step
            pltpu.make_async_copy(kv.at[entry], back.at[fetch[entry]], back_sem).start()
        both = jnp.where(left_half((1, pair_width)), bias[1], bias[0])
        sums[7:8, lanes] = q_total
        sums[6:7, lanes] = pltpu.roll(jnp.broadcast_to(both, (8, pair_width)), HEAD_DIM, 1)[0:1]

    store(dq, dq_out)
    span = back.at[pl.ds(0, requests)]
    pltpu.make_async_copy(kv, span, back_sem).wait()
    for copy in stores:
        copy.wait()


CHUNKS = 8
VECTORS = 16


def chunk_rows(at, size):
    return pl.ds(pl.multiple_of(at * size, size), size)


def place_chunks(source, target, info, sem, start=1):
    size = source.shape[0] // CHUNKS
    for chunk in range(CHUNKS):
        pltpu.make_async_copy(
            source.at[chunk * size : (chunk + 1) * size],
            target.at[chunk_rows(info[start + chunk], size)],
            sem,
        ).start()


def wait_chunks(source, target, sem):
    pltpu.make_async_copy(source, target, sem).wait()


def core_of(info, side):
    return info[0] if side else 1 - info[0]


def up_kernel(info, z_low, grad, give, keep, turned, buf, sem):
    half = keep.shape[1]
    turned[...] = z_low[...].T
    for side, out in ((0, give), (1, keep)):
        at = pl.ds(pl.multiple_of(core_of(info, side) * half, half), half)
        buf[side] = nn(turned[...], grad[:, at]).astype(LOW)
        place_chunks(buf.at[side], out, info, sem.at[side])
    for side, out in ((0, give), (1, keep)):
        wait_chunks(buf.at[side], out, sem.at[side])


def down_kernel(info, active, grad, give, keep, buf, sem):
    size = keep.shape[0]
    for side, out in ((0, give), (1, keep)):
        for part in range(keep.shape[1] // size):
            block = core_of(info, side) * (keep.shape[1] // size) + part
            at = pl.ds(pl.multiple_of(block * size, size), size)
            buf[side, :, part * size : (part + 1) * size] = nn(active[:, at].T, grad[...]).astype(LOW)
        place_chunks(buf.at[side], out, info, sem.at[side])
    for side, out in ((0, give), (1, keep)):
        wait_chunks(buf.at[side], out, sem.at[side])


def out_q_kernel(info, attn, db, tok, dq, order, sums, give, keep, grad_q, attn_t, tok_t, buf, sem):
    rows = tok.shape[0]
    half = D // 2
    down = lax.broadcasted_iota(jnp.int32, (rows, rows), 0)
    for pair in range(HEADS // 2):
        total = nn(pick(down == order[2 * pair]), dq[2 * pair])
        total += nn(pick(down == order[2 * pair + 1]), dq[2 * pair + 1])
        lanes = slice(pair * 2 * HEAD_DIM, (pair + 1) * 2 * HEAD_DIM)
        grad_q[:, lanes] = total.astype(LOW)
    attn_t[...] = attn[...].T
    tok_t[...] = tok[...].T
    size = D // VECTORS
    filler = jnp.zeros((size - D // LANES, LANES), F32)
    for vector in range(VECTORS):
        rows_of = [sums[vector : vector + 1, row * LANES : (row + 1) * LANES] for row in range(D // LANES)]
        value = jnp.concatenate(rows_of + [filler]).astype(LOW)
        for side in range(2):
            buf[side, vector * size : (vector + 1) * size, D:] = value
    for side, out in ((0, give), (1, keep)):
        at = pl.ds(pl.multiple_of(core_of(info, side) * half, half), half)
        buf[side, :, :half] = nn(attn_t[...], db[:, at]).astype(LOW)
        buf[side, :, half:D] = nn(tok_t[...], grad_q[:, at]).astype(LOW)
        place_chunks(buf.at[side], out, info, sem.at[side])
    for side, out in ((0, give), (1, keep)):
        wait_chunks(buf.at[side], out, sem.at[side])


def key_value_kernel(
    info, segment, returned_hbm, order, tok, key_give, key_keep, value_give, value_keep, grad_kv_hbm,
    returned, total, tok_t, grad_kv, buf, load_sem, kv_sem, sem,
):
    rows = tok.shape[0]
    half = D // 2
    per_dev = rows // CLUS
    pair_width = 2 * HEAD_DIM
    devices = load_sem.shape[0]
    capacity = segment.shape[0] // devices

    def load(device):
        span = pl.ds(device * capacity, capacity)
        return pltpu.make_async_copy(returned_hbm.at[span], returned.at[span], load_sem.at[device])

    @pl.loop(0, devices)
    def _(device):
        load(device).start()

    down = lax.broadcasted_iota(jnp.int32, (rows, rows), 0)
    left = left_half((rows, pair_width))
    total[...] = jnp.zeros_like(total)
    tok_t[...] = tok[...].T

    @pl.loop(0, devices)
    def _(device):
        load(device).wait()
        for step in range(capacity):
            slot = device * capacity + step
            block = segment[slot]
            total[block] += returned[slot].astype(F32)

    for quad in range(HEADS // 4):
        pairs = range(2 * quad, 2 * quad + 2)
        heads = range(4 * quad, 4 * quad + 4)
        hots = [pick(down == order[head]) for head in heads]
        summed = [
            total[head * per_dev : (head + 1) * per_dev].reshape(rows, pair_width).astype(LOW) for head in heads
        ]
        placed = [nn(hot, value) for hot, value in zip(hots, summed)]
        for at, pair in enumerate(pairs):
            even, odd = placed[2 * at], placed[2 * at + 1]
            grad_kv[:, pair * pair_width : (pair + 1) * pair_width] = jnp.where(left, even, odd).astype(LOW)
            values = pltpu.roll(jnp.where(left, odd, even), HEAD_DIM, 1)
            grad_kv[:, D + pair * pair_width : D + (pair + 1) * pair_width] = values.astype(LOW)
    stored = pltpu.make_async_copy(grad_kv, grad_kv_hbm, kv_sem)
    stored.start()
    outs = ((key_give, key_keep), (value_give, value_keep))
    for side in range(2):
        base = core_of(info, side) * half
        parts = [grad_kv[:, pl.ds(pl.multiple_of(part * D + base, half), half)] for part in range(2)]
        value = nn(tok_t[...], jnp.concatenate(parts, axis=1)).astype(LOW)
        for part in range(2):
            buf[part, side] = value[:, part * half : (part + 1) * half]
            place_chunks(buf.at[part, side], outs[part][side], info, sem.at[part, side], 33 if part else 1)
    for side in range(2):
        for part in range(2):
            wait_chunks(buf.at[part, side], outs[part][side], sem.at[part, side])
    stored.wait()


def spread_start(info, start, pieces, targets, buf, sem):
    size = buf.shape[2]
    copies = []
    for at, piece in enumerate(pieces):
        core = core_of(info, 1 - at)
        for chunk in range(buf.shape[1]):
            buf[at, chunk] = piece[chunk * size : (chunk + 1) * size].astype(F32)
            for lanes, target in targets(core, chunk_rows(info[start + chunk], size)):
                copies.append(pltpu.make_async_copy(buf.at[at, chunk, :, lanes], target, sem))
                copies[-1].start()
    return copies


def up_targets(out, half):
    def targets(core, rows):
        yield pl.ds(0, half), out.at[rows, pl.ds(pl.multiple_of(core * half, half), half)]

    return targets


def down_targets(out, half):
    parts = half // D

    def targets(core, rows):
        for part in range(parts):
            yield pl.ds(part * D, D), out.at[core * parts + part, rows]

    return targets


def attention_targets(w_out, w_qkv):
    half = D // 2

    def targets(core, rows):
        at = pl.ds(pl.multiple_of(core * half, half), half)
        yield pl.ds(0, half), w_out.at[rows, at]
        for part, lane in enumerate((half, D + LANES, D + LANES + half)):
            to = pl.ds(pl.multiple_of(part * D + core * half, half), half)
            yield pl.ds(lane, half), w_qkv.at[rows, to]

    return targets


def spread_groups(groups, info, pieces, outs, bufs, sem):
    w_up, w_down, w_out, w_qkv = outs
    half = w_up.shape[1] // 2
    routes = (up_targets(w_up, half), down_targets(w_down, half), attention_targets(w_out, w_qkv))
    copies = []
    for at, (third, start) in enumerate(groups):
        copies += spread_start(info, start, pieces[2 * at : 2 * at + 2], routes[third], bufs[at], sem.at[at])
    return copies


def spread_kernel(groups, info, *refs):
    pairs = len(groups)
    pieces, bufs, sem = refs[: 2 * pairs], refs[-pairs - 1 : -1], refs[-1]
    outs = refs[-pairs - 5 : -pairs - 1]
    for copy in spread_groups(groups, info, pieces, outs, bufs, sem):
        copy.wait()


def spread_last_kernel(groups, start, info, *refs):
    pairs = len(groups)
    pieces, sources = refs[: 2 * pairs], refs[2 * pairs : 2 * pairs + 4]
    rest = refs[2 * pairs + 8 :]
    outs, vectors, rest = rest[:4], rest[4:13], rest[13:]
    bufs = rest[:pairs]
    sem, columns, table, column_sem = rest[pairs:]
    loads = [
        pltpu.make_async_copy(source.at[:, D : D + LANES], columns.at[at], column_sem.at[at])
        for at, source in enumerate(sources)
    ]
    for load in loads:
        load.start()
    copies = spread_groups(groups, info, pieces, outs, bufs, sem)
    size = D // VECTORS
    each = CHUNKS // len(sources)
    inside = VECTORS // CHUNKS
    for at, load in enumerate(loads):
        load.wait()
        for row in range(each * inside):
            vector = info[start + at * each + row // inside] * inside + row % inside
            table[vector] = columns[at, row * size : row * size + 16].astype(F32)

    def whole(vector):
        return jnp.concatenate([table[vector, row : row + 1] for row in range(D // LANES)], axis=1)

    for at, vector in enumerate(vectors):
        count = vector.shape[0] // D
        vector[...] = jnp.concatenate([whole(at + part) for part in range(count)], axis=1).reshape(count * D)
    for copy in copies:
        copy.wait()


X, Y, Z = ("dp", 1), ("blk", 2), ("blk", 4)
CORE = ("blk", 1)
ORDERS = ((Z, Y, X), (X, Z, Y), (Y, X, Z))


def swap(value, bit):
    axis, distance = bit
    size = lax.axis_size(axis)
    return lax.ppermute(value, axis, [(i, i ^ distance) for i in range(size)])


def further_bits(count_blk):
    bits = []
    distance = 8
    while distance < count_blk:
        bits.append(("blk", distance))
        distance *= 2
    return bits


def chunk_places():
    x, y, z = [(lax.axis_index(axis) // distance) % 2 for axis, distance in (X, Y, Z)]
    chip = x * 4 + y * 2 + z
    core = lax.axis_index("blk") % 2
    every = jnp.arange(CHUNKS, dtype=jnp.int32)
    value = {X: 4, Y: 2, Z: 1}

    def from_order(order):
        at = sum(((every // 2**step) % 2) * value[bit] for step, bit in enumerate(order))
        return at ^ chip

    placed = every ^ chip
    x_y_swapped = placed % 2 + (placed // 4) * 2 + (placed // 2 % 2) * 4
    return jnp.concatenate(
        [core[None], placed] + [from_order(order) for order in ORDERS] + [x_y_swapped]
    )


def sum_rows(terms, low, high):
    total = terms[0][low:high].astype(F32)
    for term in terms[1:]:
        total = total + term[low:high].astype(F32)
    return total


def to_send(terms):
    rows = min(term.shape[0] for term in terms)
    return sum_rows(terms, rows // 2, rows).astype(LOW)


def scatter_steps(terms, bits):
    for bit in bits:
        terms = terms + [swap(to_send(terms), bit)]
    return terms


def finish(terms, further):
    value = sum_rows(terms, 0, terms[-1].shape[0]).astype(LOW)
    for bit in further:
        value = sum_rows([value, swap(value, bit)], 0, value.shape[0]).astype(LOW)
    return value


def tie(values):
    return lax.optimization_barrier(tuple(values))


def gather_step(value, bit):
    return jnp.concatenate([value, swap(value, bit)])


def per_device(
    tokens,
    w_qkv,
    b_query,
    b_value,
    w_out,
    b_out,
    gain_one,
    shift_one,
    w_up,
    b_up,
    w_down,
    b_down,
    gain_two,
    shift_two,
    cluster_perm,
    cluster_pairs,
    cotangent,
):
    count_blk = lax.axis_size("blk")
    my_index = lax.axis_index("blk")
    rows = tokens.shape[0]
    per_dev = rows // CLUS
    blocks = HEADS * per_dev
    requests = blocks * PAIRS
    capacity = max(2, (requests + count_blk - 1) // count_blk + 1)
    slots = count_blk * capacity
    pair_width = 2 * HEAD_DIM
    ff = w_up.shape[1]
    perm = cluster_perm.reshape(HEADS, 1, rows)
    local_order = cluster_perm[0] - my_index * rows
    order_rows = local_order[:, None, :]

    wanted = (
        cluster_pairs[0]
        .reshape(HEADS, count_blk, per_dev, PAIRS)
        .transpose(1, 0, 2, 3)
        .reshape(count_blk, requests)
    )
    positions = jnp.arange(requests, dtype=jnp.int32)
    before = positions[:, None] < positions[None, :]
    source = wanted // per_dev
    named = source == my_index
    rank = jnp.sum(named[:, :, None] & before[None], axis=1)
    head_of = positions // (per_dev * PAIRS)
    block_id = head_of[None, :] * per_dev + wanted % per_dev
    matches = named[:, :, None] & (
        rank[:, :, None] == jnp.arange(capacity, dtype=jnp.int32)[None, None, :]
    )
    chosen = jnp.sum(jnp.where(matches, block_id[:, :, None], 0), axis=1)

    smem = pl.BlockSpec(memory_space=pltpu.SMEM)
    vmem = pl.BlockSpec(memory_space=pltpu.VMEM)
    hbm = pl.BlockSpec(memory_space=pl.ANY)

    def column_block(at):
        return pl.BlockSpec((D, D), lambda step: (0, at))

    outgoing = pl.pallas_call(
        kv_kernel,
        grid=(1,),
        out_shape=jax.ShapeDtypeStruct((slots, CLUS, pair_width), LOW),
        in_specs=[vmem, column_block(1), column_block(2), vmem, vmem, vmem],
        out_specs=hbm,
        scratch_shapes=[
            pltpu.VMEM((blocks, CLUS, pair_width), LOW),
            pltpu.SMEM(chosen.shape, jnp.int32),
            pltpu.SemaphoreType.DMA,
            pltpu.SemaphoreType.DMA,
        ],
        compiler_params=params(),
        name="kv_kernel",
    )(tokens, w_qkv, w_qkv, b_value, perm, chosen)
    arrived = lax.all_to_all(
        outgoing.reshape(count_blk, capacity, CLUS, pair_width),
        "blk",
        split_axis=0,
        concat_axis=0,
        tiled=True,
    ).reshape(slots, CLUS, pair_width)

    info = chunk_places()
    queries = pl.pallas_call(
        q_kernel,
        grid=(1,),
        out_shape=jax.ShapeDtypeStruct((HEADS, rows, pair_width), LOW),
        in_specs=[vmem, column_block(0), vmem, vmem],
        out_specs=vmem,
        compiler_params=params(),
        name="q_kernel",
    )(tokens, w_qkv, b_query, perm)
    filled = jnp.any(matches, axis=1)
    segment = jnp.where(filled, chosen, blocks).reshape(-1)
    my_source = lax.dynamic_index_in_dim(wanted, my_index, 0, keepdims=False) // per_dev
    my_rank = jnp.sum((my_source[:, None] == my_source[None, :]) & before, axis=0)
    fetch = my_source * capacity + my_rank
    places = jnp.arange(rows, dtype=jnp.int32)
    inverse = jnp.sum(
        jnp.where(local_order[:, :, None] == places, places[None, :, None], 0), axis=1
    )[:, None, :]
    def low(*shape):
        return jax.ShapeDtypeStruct(shape, LOW)

    def full(*shape):
        return jax.ShapeDtypeStruct(shape, F32)

    (
        back, dq_sorted, attn, normed, active, grad_inner, grad_second, grad_branch, grad_resid,
        layer_out, sums,
    ) = pl.pallas_call(
        mid_kernel,
        out_shape=(
            low(slots, CLUS, pair_width), low(HEADS, rows, pair_width), low(rows, D), low(rows, D),
            low(rows, ff), low(rows, ff), low(rows, D), low(rows, D), full(rows, D), low(rows, D),
            full(16, D),
        ),
        in_specs=[smem, vmem, hbm, vmem, vmem, hbm, hbm] + [vmem] * 7 + [hbm] * 3,
        out_specs=(hbm,) * 10 + (vmem,),
        scratch_shapes=[
            pltpu.VMEM((requests, CLUS, pair_width), LOW),
            pltpu.VMEM((blocks, CLUS, PAIRS * CLUS), LOW),
            pltpu.VMEM((rows, D), LOW),
            pltpu.VMEM((2, rows, pair_width), LOW),
            pltpu.VMEM((D, D), LOW),
            pltpu.VMEM((D, ff), LOW),
            pltpu.VMEM((ff, D), LOW),
            pltpu.VMEM((rows, D), F32),
            pltpu.VMEM((rows, D), F32),
            pltpu.VMEM((rows, 1), F32),
            pltpu.VMEM((rows, D), LOW),
            pltpu.VMEM((rows, ff), LOW),
            pltpu.VMEM((rows, ff), LOW),
            pltpu.VMEM((rows, D), F32),
            pltpu.VMEM((rows, D), LOW),
            pltpu.VMEM((rows, D), LOW),
            pltpu.VMEM((rows, D), LOW),
            pltpu.VMEM((rows, D), F32),
            pltpu.VMEM((rows, D), LOW),
            pltpu.VMEM((HEADS, rows, pair_width), LOW),
            pltpu.VMEM((rows, D), LOW),
            pltpu.VMEM((rows, D), LOW),
            pltpu.SemaphoreType.DMA((HEADS // 2,)),
            pltpu.SemaphoreType.DMA((5,)),
            pltpu.SemaphoreType.DMA((9,)),
            pltpu.SemaphoreType.DMA,
        ],
        compiler_params=params(),
        name="mid_kernel",
    )(
        fetch, queries, arrived, order_rows, inverse, tokens, cotangent,
        b_out, gain_one, shift_one, b_up, b_down, gain_two, shift_two, w_out, w_up, w_down,
    )
    returned = lax.all_to_all(
        back.reshape(count_blk, capacity, CLUS, pair_width),
        "blk",
        split_axis=0,
        concat_axis=0,
        tiled=True,
    ).reshape(slots, CLUS, pair_width)

    further = further_bits(count_blk)

    def halves(kernel, operands, columns, scratch, more=(), name=None):
        return pl.pallas_call(
            kernel,
            out_shape=(low(D, columns), low(D, columns)) + more,
            in_specs=[smem] + [vmem] * (len(operands) - 1),
            out_specs=(hbm, hbm) + (vmem,) * len(more),
            scratch_shapes=scratch
            + [pltpu.VMEM((2, D, columns), LOW), pltpu.SemaphoreType.DMA((2,))],
            compiler_params=params(),
            cost_estimate=pl.CostEstimate(flops=1, bytes_accessed=1, transcendentals=0),
            name=name,
        )(*operands)

    half = D // 2
    turned = pltpu.VMEM((D, rows), LOW)
    up_give, up_keep = halves(
        up_kernel, (info, normed, grad_inner), ff // 2, [turned], name="up_kernel"
    )
    down_give, down_keep = halves(
        down_kernel, (info, active, grad_second), ff // 2, [], name="down_kernel"
    )
    up = [up_keep, swap(up_give, CORE)]
    up_step, attn = tie((to_send(up), attn))
    oq_give, oq_keep, grad_q = halves(
        out_q_kernel,
        (info, attn, grad_branch, tokens, dq_sorted, order_rows, sums),
        D + LANES,
        [turned, turned],
        (low(rows, D),),
        name="out_q_kernel",
    )
    up = scatter_steps(up + [swap(up_step, X)], (Y,))
    down = scatter_steps([down_keep, swap(down_give, CORE)], (X,))
    out_q = scatter_steps([oq_keep, swap(oq_give, CORE)], (X,))
    up_step = to_send(up)
    up_step, down[-1] = tie((up_step, down[-1]))
    down_step = to_send(down)

    returned, up_step, down_step, out_q[-1] = tie((returned, up_step, down_step, out_q[-1]))
    up = up + [swap(up_step, Z)]
    down = down + [swap(down_step, Y)]
    out_q = scatter_steps(out_q, (Y,))
    key_give, key_keep, value_give, value_keep, grad_kv = pl.pallas_call(
        key_value_kernel,
        out_shape=(low(D, half),) * 4 + (low(rows, 2 * D),),
        in_specs=[smem, smem, hbm, vmem, vmem],
        out_specs=(hbm,) * 5,
        scratch_shapes=[
            pltpu.VMEM((slots, CLUS, pair_width), LOW),
            pltpu.VMEM((blocks + 1, CLUS, pair_width), F32),
            turned,
            pltpu.VMEM((rows, 2 * D), LOW),
            pltpu.VMEM((2, 2, D, half), LOW),
            pltpu.SemaphoreType.DMA((count_blk,)),
            pltpu.SemaphoreType.DMA,
            pltpu.SemaphoreType.DMA((2, 2)),
        ],
        compiler_params=params(),
        name="key_value_kernel",
    )(info, segment, returned, order_rows, tokens)
    down[-1], key_give, value_give = tie((down[-1], key_give, value_give))
    key = scatter_steps([key_keep, swap(key_give, CORE)], (X, Y))
    value = scatter_steps([value_keep, swap(value_give, CORE)], (Y, X))
    late_given = swap(jnp.concatenate([to_send(key), to_send(value)], axis=1), Z)
    key = key + [late_given[:, :half]]
    value = value + [late_given[:, half:]]
    up = finish(up, further)
    down = finish(scatter_steps(down, (Z,)), further)
    out_q = finish(scatter_steps(out_q, (Z,)), further)
    both = jnp.concatenate([sum_rows(terms, 0, terms[-1].shape[0]) for terms in (key, value)], axis=1)
    both = finish([both.astype(LOW)], further)
    thirds = (up, down, jnp.concatenate([out_q, both], axis=1))

    starts = (9, 17, 25)
    weights = (full(D, ff), full(ff // D, D, D), full(D, D), full(D, 3 * D))

    def swap_all(values, step):
        return [swap(value, order[step]) for value, order in zip(values, ORDERS)]

    def spread_scratch(pieces):
        rows_each = D // CHUNKS
        return (
            [
                pltpu.VMEM((2, piece.shape[0] // rows_each, rows_each, piece.shape[1]), F32)
                for piece in pieces[::2]
            ]
            + [pltpu.SemaphoreType.DMA((len(pieces) // 2,))]
        )

    def with_other(sets):
        return [array for value in sets for array in (value, swap(value, CORE))]

    def spread(sets, offsets, outs=()):
        pieces = with_other(sets)
        groups = tuple((third, starts[third] + offset) for offset in offsets for third in range(3))
        return pl.pallas_call(
            partial(spread_kernel, groups),
            out_shape=weights,
            in_specs=[smem] + [vmem] * len(pieces) + [hbm] * len(outs),
            out_specs=(hbm,) * 4,
            scratch_shapes=spread_scratch(pieces),
            input_output_aliases={1 + len(pieces) + at: at for at in range(len(outs))},
            compiler_params=params(32),
            name="spread",
        )(info, *pieces, *outs)

    thirds = list(tie(gather_step(value, order[0]) for value, order in zip(thirds, ORDERS)))
    third_step = swap_all(thirds, 1)
    fourth_step = swap_all(thirds, 2)
    outs = spread(thirds, (0,))
    tied = tie((*third_step, grad_kv))
    third_step, grad_kv = list(tied[:3]), tied[3]
    last_step = swap_all(third_step, 2)
    grad_proj = jnp.concatenate([grad_q, grad_kv], axis=1)
    grad_tokens = (grad_resid + nt(grad_proj, w_qkv)).astype(LOW)
    tied = tie((*fourth_step, *outs, grad_tokens))
    fourth_step, outs, grad_tokens = list(tied[:3]), tied[3:7], tied[7]
    outs = spread(third_step + fourth_step, (2, 4), outs)
    tied = tie((*last_step, *outs))
    last_step, outs = list(tied[:3]), tied[3:]
    pieces = with_other(last_step)
    sum_up, sum_down, sum_out, sum_qkv, *vectors = pl.pallas_call(
        partial(spread_last_kernel, tuple((third, starts[third] + 6) for third in range(3)), starts[2]),
        out_shape=weights + (full(D),) * 8 + (full(ff),),
        in_specs=[smem] + [vmem] * len(pieces) + [hbm] * 8,
        out_specs=(hbm,) * 4 + (vmem,) * 9,
        scratch_shapes=spread_scratch(pieces)
        + [
            pltpu.VMEM((4, D // 4, LANES), LOW),
            pltpu.VMEM((VECTORS, 16, LANES), F32),
            pltpu.SemaphoreType.DMA((4,)),
        ],
        input_output_aliases={1 + len(pieces) + 4 + at: at for at in range(4)},
        compiler_params=params(24),
        name="spread_last",
    )(info, *pieces, thirds[2], third_step[2], fourth_step[2], last_step[2], *outs)
    return (
        layer_out,
        grad_tokens,
        sum_qkv,
        vectors[7],
        vectors[6],
        sum_out,
        vectors[5],
        vectors[3],
        vectors[4],
        sum_up,
        vectors[8],
        sum_down.reshape(ff, D),
        vectors[2],
        vectors[0],
        vectors[1],
    )


def solution(mesh):
    whole = P()
    rows = P(("dp", "blk"), None)
    return jax.shard_map(
        per_device,
        mesh=mesh,
        in_specs=(
            (rows,)
            + (whole,) * 13
            + (P("dp", None, "blk"), P("dp", None, None, None), rows)
        ),
        out_specs=(rows, rows) + (whole,) * 13,
        check_vma=False,
    )
```
